32 devices in a mesh: group: 2 (over y), seq: 4 (over z), tp: 2 (over x), role: 2 (over core).
Axes of the slice: x: 2, y: 2, z: 4, core: 2. Of those that a mesh axis runs over, the one named last changes fastest.
Arguments:
- queries: bfloat16 [2, 3072, 4096], P('role', ('group', 'seq'), 'tp'), parts along dimension 1, may hold values from -6 to 6
- new_kv: bfloat16 [2, 3072, 2, 512], P('role', ('group', 'seq'), None, 'tp'), parts along dimension 1, may hold values from -6 to 6
- pool: bfloat16 [2, 2048, 2, 16, 512], P('role', ('group', 'seq'), None, None, 'tp'), parts along dimension 1, may hold values from -6 to 6
- out_weight: bfloat16 [4096, 4096], P('tp', 'seq'), may hold values from -0.5 to 0.5
- tok_conv: int32 [2, 3072], P('role', ('group', 'seq')), parts along dimension 1, may hold values from 0 to 95, as said below
- page_conv: int32 [2, 1024], P('role', ('group', 'seq')), parts along dimension 1, may hold values from 0 to 95, as said below
- page_fill: int32 [2, 1024], P('role', ('group', 'seq')), parts along dimension 1, may hold values from 1 to 16, as said below
- page_owner: int32 [2, 1024], P('role', ('group', 'seq')), parts along dimension 1, may hold values from 0 to 3, as said below
- page_index: int32 [2, 1024], P('role', ('group', 'seq')), parts along dimension 1, may hold values from 0 to 255, as said below
Outputs:
- projected: bfloat16 [2, 3072, 4096], P('role', ('group', 'seq', 'tp')), parts along dimension 1
The draws below stay inside these ranges and needn't reach their ends.
There are 2 independent parts, one for each index of `group`. The reference program is written for one: setup_inputs(seed, part) draws one part's arguments, and reference() takes and returns one part's arrays. A program takes and returns all parts, laid end to end along the dimension named above; an argument that names none is the same for every part. Nothing has to cross between parts.
Inputs may be any that keep to these rules, and one draw needn't show every extreme that they name: `tok_conv`: in each device's block of 384 tokens conversation numbers never fall and each present number holds one or more tokens; in half 0 a block holds 8 conversations, in half 1 it holds 96 conversations of 4 tokens each. `page_conv`: in each device's block of 128 slots conversation numbers never fall, and every conversation of the matching token block has one or more slots. `page_fill`: every slot of a conversation but its last holds 16 live positions. `page_owner`: no owner is named by more than 64 slots of one device's block; in each half one owner is named by exactly 64 slots of every device's block. `page_index`: within a half, no two slots name the same owner and page number.
All inputs are finite; a program needn't handle non-finite values.
Results may differ from the reference program's by a relative error of at most 0.0066.
Values may be sent and summed in bfloat16 or wider, within the bound.
No kernel may reach another device: no remote copies, remote signals or barrier semaphores. Data moves between devices by JAX's collectives and lax.ppermute only.
A program may use at most 128 MiB of HBM per device.

```python
import math
import jax
import jax.numpy as jnp
from jax import lax

HQ = 32
KVH = 4
HD = 128
OUTW = 4096
BLOCK = 16
ITERS = 4
PCONV = 8
HP = 128
ROWS = 384
CAP = 64
PAGES_OWN = 256
TOKENS = 1536
N_SEQ = 4
N_TP = 2


def spread_counts(spread_key, whole_total, pieces):
    base_share = whole_total // pieces + (jnp.arange(pieces) < whole_total % pieces).astype(jnp.int32)
    moved = jax.random.randint(spread_key, (pieces,), 0, base_share // 2 + 1)
    return (base_share - moved + jnp.roll(moved, 1)).astype(jnp.int32)


def labels_from(lengths, length_total):
    bounds = jnp.cumsum(lengths)
    return jnp.sum(jnp.arange(length_total)[:, None] >= bounds[None, :], axis=1).astype(jnp.int32)


def device_layout(device_key, conversations, new_lengths):
    page_counts = spread_counts(jax.random.fold_in(device_key, 1), HP, conversations)
    fills = jax.random.randint(jax.random.fold_in(device_key, 2), (conversations,), 1, BLOCK + 1)
    slot_conv = labels_from(page_counts, HP)
    last_slot = jnp.cumsum(page_counts) - 1
    is_last = jnp.arange(HP) == last_slot[slot_conv]
    slot_fill = jnp.where(is_last, fills[slot_conv], BLOCK).astype(jnp.int32)
    token_conv = labels_from(new_lengths, ROWS)
    return (token_conv, slot_conv, slot_fill)


def prefill_device(device_key):
    lengths = spread_counts(jax.random.fold_in(device_key, 3), ROWS, PCONV)
    return device_layout(device_key, PCONV, lengths)


def decode_device(device_key):
    lengths = jnp.full((ROWS // ITERS,), ITERS, jnp.int32)
    return device_layout(device_key, ROWS // ITERS, lengths)


def conversation_layout(base_key):
    first_half = jax.vmap(prefill_device)(jax.random.split(jax.random.fold_in(base_key, 11), N_SEQ))
    second_half = jax.vmap(decode_device)(jax.random.split(jax.random.fold_in(base_key, 12), N_SEQ))
    return tuple((jnp.stack([lower.reshape(-1), upper.reshape(-1)]) for lower, upper in zip(first_half, second_half)))


def pick_order(order_key):
    return jax.random.permutation(order_key, PAGES_OWN).astype(jnp.int32)


def pick_shuffle(order_key):
    return jax.random.permutation(order_key, HP).astype(jnp.int32)


def page_places(base_key):
    owner_halves = []
    index_halves = []
    for half_index in range(2):
        half_key = jax.random.fold_in(base_key, 20 + half_index)
        busiest = jax.random.randint(jax.random.fold_in(half_key, 1), (), 0, N_SEQ)
        orders = jax.vmap(pick_order)(jax.random.split(jax.random.fold_in(half_key, 2), N_SEQ))
        device_ids = jnp.arange(N_SEQ)[:, None]
        slot_ids = jnp.arange(HP)[None, :]
        shifted = device_ids + slot_ids - CAP
        cycled = shifted % (N_SEQ - 1)
        elsewhere = jnp.where(cycled < busiest, cycled, cycled + 1)
        slot_owner = jnp.where(slot_ids < CAP, busiest, elsewhere)
        occurrence = jnp.where(slot_ids < CAP, slot_ids, jnp.maximum(shifted, 0) // (N_SEQ - 1))
        slot_page = orders[slot_owner, device_ids * CAP + occurrence]
        shuffles = jax.vmap(pick_shuffle)(jax.random.split(jax.random.fold_in(half_key, 3), N_SEQ))
        owner_halves.append(jnp.take_along_axis(slot_owner, shuffles, axis=1).reshape(-1))
        index_halves.append(jnp.take_along_axis(slot_page, shuffles, axis=1).reshape(-1))
    return (jnp.stack(owner_halves).astype(jnp.int32), jnp.stack(index_halves).astype(jnp.int32))


def sign_pattern(base_key):
    return jnp.where(jax.random.bernoulli(jax.random.fold_in(base_key, 77), 0.5, (HD,)), 1.0, -1.0).astype(jnp.float32)


def draw_tok_conv(key, part):
    shared = conversation_layout(key)
    key = jax.random.fold_in(key, 31)
    return shared[0]


def draw_page_conv(key, part):
    shared = conversation_layout(key)
    key = jax.random.fold_in(key, 32)
    return shared[1]


def draw_page_fill(key, part):
    shared = conversation_layout(key)
    key = jax.random.fold_in(key, 33)
    return shared[2]


def draw_page_owner(key, part):
    shared = page_places(key)
    key = jax.random.fold_in(key, 34)
    return shared[0]


def draw_page_index(key, part):
    shared = page_places(key)
    key = jax.random.fold_in(key, 35)
    return shared[1]


def draw_queries(key, part):
    key = jax.random.fold_in(key, 5)
    values = jnp.clip(jax.random.normal(key, (2, TOKENS, HQ, HD), jnp.float32), -6.0, 6.0)
    return values.reshape(2, TOKENS, HQ * HD).astype(jnp.bfloat16)


def draw_new_kv(key, part):
    key = jax.random.fold_in(key, 6)
    values = jnp.clip(jax.random.normal(key, (2, TOKENS, 2, KVH, HD), jnp.float32), -6.0, 6.0)
    return values.reshape(2, TOKENS, 2, KVH * HD).astype(jnp.bfloat16)


def block_scale(key, shape, cuts, smallest, high):
    def one(dim, blocks):
        heights = jax.random.uniform(jax.random.fold_in(jax.random.fold_in(key, 6), dim), (blocks,), jnp.float32, smallest / len(cuts), high / len(cuts))
        return jnp.repeat(jnp.exp(heights), shape[dim] // blocks).reshape((-1,) + (1,) * (len(shape) - dim - 1))

    level = one(*cuts[0])
    for cut in cuts[1:]:
        level = level * one(*cut)
    return level


def centred(own_key, shape, spread, reach, cuts=(), held_as=jnp.bfloat16):
    values = jax.random.normal(own_key, shape, jnp.float32) * spread
    if len(cuts) > 0:
        values = block_scale(own_key, shape, cuts, -0.22, 0.18) * values
    return jnp.clip(values, min=-reach, max=reach).astype(held_as)


def setup_inputs(seed: int = 0, part: int = 0) -> dict:
    keys = jax.random.split(jax.random.key(seed), 10)
    part_keys = jax.random.split(jax.random.fold_in(keys[9], part), 10)
    queries = draw_queries(jax.random.fold_in(jax.random.fold_in(keys[9], part), 71), part)
    new_kv = draw_new_kv(jax.random.fold_in(jax.random.fold_in(keys[9], part), 71), part)
    pool = centred(part_keys[2], (2, N_SEQ * PAGES_OWN, 2, BLOCK, KVH * HD), 1.0, 6.0, ((0, 2), (1, 4), (4, 2)))
    out_weight = centred(keys[3], (HQ * HD, OUTW), HD ** -0.5, 0.5, ((0, 2), (1, 4)))
    tok_conv = draw_tok_conv(jax.random.fold_in(jax.random.fold_in(keys[9], part), 71), part)
    page_conv = draw_page_conv(jax.random.fold_in(jax.random.fold_in(keys[9], part), 71), part)
    page_fill = draw_page_fill(jax.random.fold_in(jax.random.fold_in(keys[9], part), 71), part)
    page_owner = draw_page_owner(jax.random.fold_in(jax.random.fold_in(keys[9], part), 71), part)
    page_index = draw_page_index(jax.random.fold_in(jax.random.fold_in(keys[9], part), 71), part)
    return dict(queries=queries, new_kv=new_kv, pool=pool, out_weight=out_weight, tok_conv=tok_conv, page_conv=page_conv, page_fill=page_fill, page_owner=page_owner, page_index=page_index)


def attend_block(query_rows, fresh_rows, history, token_conv, slot_conv, slot_fill):
    group_size = HQ // KVH
    score_scale = 1.0 / math.sqrt(HD)
    key_rows = jnp.concatenate([history[:, 0].reshape(HP * BLOCK, KVH, HD), fresh_rows[:, 0].reshape(ROWS, KVH, HD)], axis=0)
    value_rows = jnp.concatenate([history[:, 1].reshape(HP * BLOCK, KVH, HD), fresh_rows[:, 1].reshape(ROWS, KVH, HD)], axis=0)
    slot_range = jnp.arange(BLOCK)
    history_ok = (slot_conv[:, None, None] == token_conv[None, None, :]) & (slot_range[None, :, None] < slot_fill[:, None, None])
    history_ok = history_ok.reshape(HP * BLOCK, ROWS).T
    row_range = jnp.arange(ROWS)
    fresh_ok = (token_conv[:, None] == token_conv[None, :]) & (row_range[None, :] <= row_range[:, None])
    allowed = jnp.concatenate([history_ok, fresh_ok], axis=1)
    query_heads = query_rows.reshape(ROWS, KVH, group_size, HD).astype(jnp.float32)
    scores = jnp.einsum('rkgd,nkd->kgrn', query_heads, key_rows.astype(jnp.float32)) * score_scale
    scores = jnp.where(allowed[None, None], scores, -jnp.inf)
    row_max = lax.optimization_barrier(jnp.max(scores, axis=-1, keepdims=True))
    expanded = jnp.exp(scores - row_max)
    weights_bf = (expanded / lax.optimization_barrier(jnp.sum(expanded, axis=-1, keepdims=True))).astype(jnp.bfloat16)
    weights_bf = lax.optimization_barrier(weights_bf)
    attended = jnp.einsum('kgrn,nkd->rkgd', weights_bf.astype(jnp.float32), value_rows.astype(jnp.float32))
    return attended.reshape(ROWS, HQ * HD).astype(jnp.bfloat16)

def reference(queries, new_kv, pool, out_weight, tok_conv, page_conv, page_fill, page_owner, page_index):
    halves = []
    for half_index in range(2):
        places = (page_owner[half_index] * PAGES_OWN + page_index[half_index]).astype(jnp.int32).reshape(N_SEQ, HP)
        half_pool = pool[half_index]

        def one_block(operands):
            query_rows, fresh_rows, block_places, token_conv, slot_conv, slot_fill = operands
            history = jnp.take(half_pool, block_places, axis=0)
            return attend_block(query_rows, fresh_rows, history, token_conv, slot_conv, slot_fill)
        blocks = lax.map(one_block, (queries[half_index].reshape(N_SEQ, ROWS, HQ * HD), new_kv[half_index].reshape(N_SEQ, ROWS, 2, KVH * HD), places, tok_conv[half_index].reshape(N_SEQ, ROWS), page_conv[half_index].reshape(N_SEQ, HP), page_fill[half_index].reshape(N_SEQ, HP)))
        halves.append(blocks.reshape(TOKENS, HQ * HD))
    attended = jnp.stack(halves)
    group_width = HQ * HD // N_TP
    summed = jnp.zeros((2, TOKENS, OUTW), jnp.float32)
    for group_index in range(N_TP):
        columns = attended[:, :, group_index * group_width:(group_index + 1) * group_width].astype(jnp.float32)
        weight_rows = out_weight[group_index * group_width:(group_index + 1) * group_width].astype(jnp.float32)
        partial_bf = jnp.einsum('htc,co->hto', columns, weight_rows).astype(jnp.bfloat16)
        partial_bf = lax.optimization_barrier(partial_bf)
        summed = summed + partial_bf.astype(jnp.float32)
    return summed.astype(jnp.bfloat16)
```

```python
import functools
import math

import jax
import jax.numpy as jnp
from jax import lax
from jax.experimental import pallas as pl
from jax.experimental.pallas import tpu as pltpu
from jax.sharding import PartitionSpec as P

HD = 128
TILE = 32
KEYS = 256
LANES = 128
HIDDEN = -1e30
PARTS = 2
VMEM = 56 * 1024 * 1024


def bucket_ranks(slot_owner, owner_count):
    one_hot = (slot_owner[..., None] == jnp.arange(owner_count)).astype(jnp.int32)
    before = jnp.cumsum(one_hot, axis=-2) - one_hot
    return jnp.sum(before * one_hot, axis=-1)


def attend_kernel(
    spec, position, hist_at, hist_steps, fresh_at, fresh_steps,
    query, pages, fresh, key_conv, key_row, tok_conv, out, keys, values, scores, sums,
):
    kv_local, group_size, slots, page_len, rows, fresh_base, key_total = spec
    channels = kv_local * HD
    hist = slots * page_len
    for head in range(kv_local):
        values[head, :, HD:] = jnp.ones((key_total, HD), jnp.bfloat16)
        for first, last in ((hist, fresh_base), (fresh_base + rows, key_total)):
            keys[head, first:last] = jnp.zeros((last - first, HD), jnp.bfloat16)
            values[head, first:last, :HD] = jnp.zeros((last - first, HD), jnp.bfloat16)
        at = head * HD
        keys[head, fresh_base : fresh_base + rows] = fresh[:, at : at + HD]
        values[head, fresh_base : fresh_base + rows, :HD] = fresh[:, channels + at : channels + at + HD]

    def place(slot, carry):
        page = position[slot]
        row = pl.ds(pl.multiple_of(slot * page_len, page_len), page_len)
        for head in range(kv_local):
            at = head * HD
            keys[head, row] = pages[page, 0, :, at : at + HD]
            values[head, row, :HD] = pages[page, 1, :, at : at + HD]
        return carry

    lax.fori_loop(0, slots, place, 0, unroll=8)
    to_exp2 = math.log2(math.e) / math.sqrt(HD)
    wide = group_size * TILE

    def tile(index, carry):
        first = pl.multiple_of(index * TILE, TILE)
        tokens = pl.ds(first, TILE)
        conv = tok_conv[tokens]
        number = first + lax.broadcasted_iota(jnp.int32, (TILE, 1), 0)
        steps_h, steps_f = hist_steps[index], fresh_steps[index]
        at_h, at_f = hist_at[index], fresh_at[index]
        heads = [
            jnp.concatenate(
                [
                    query[tokens, (head * group_size + g) * HD : (head * group_size + g + 1) * HD]
                    for g in range(group_size)
                ],
                axis=0,
            )
            for head in range(kv_local)
        ]

        def key_range(step):
            start = jnp.where(
                step < steps_h, at_h + step * KEYS, fresh_base + at_f + (step - steps_h) * KEYS
            )
            return pl.ds(pl.multiple_of(start, LANES), KEYS)

        def score(step, tops):
            where = key_range(step)
            ok = (key_conv[:, where] == conv) & (key_row[:, where] <= number)
            held = pl.ds(pl.multiple_of(step * KEYS, KEYS), KEYS)
            new = []
            for head in range(kv_local):
                s = lax.dot_general(
                    heads[head], keys[head, where], (((1,), (1,)), ((), ())),
                    preferred_element_type=jnp.float32,
                ).reshape(group_size, TILE, KEYS)
                s = jnp.where(ok[None], s, HIDDEN).reshape(wide, KEYS)
                scores[head, :, held] = s
                top = tops[head]
                for k in range(0, KEYS, LANES):
                    top = jnp.maximum(top, s[:, k : k + LANES])
                new.append(top)
            return tuple(new)

        low = jnp.full((wide, LANES), HIDDEN, jnp.float32)
        tops = lax.fori_loop(0, steps_h + steps_f, score, (low,) * kv_local)
        tops = [jnp.max(top, axis=1, keepdims=True) * to_exp2 for top in tops]
        sums[...] = jnp.zeros_like(sums)

        def gather(step, carry):
            where = key_range(step)
            held = pl.ds(pl.multiple_of(step * KEYS, KEYS), KEYS)
            for head in range(kv_local):
                w = jnp.exp2(scores[head, :, held] * to_exp2 - tops[head]).astype(jnp.bfloat16)
                sums[head] += jnp.dot(w, values[head, where], preferred_element_type=jnp.float32)
            return carry

        lax.fori_loop(0, steps_h + steps_f, gather, 0)
        for head in range(kv_local):
            done = (sums[head, :, :HD] / sums[head, :, HD:]).astype(jnp.bfloat16)
            for g in range(group_size):
                at = (head * group_size + g) * HD
                out[tokens, at : at + HD] = done[g * TILE : (g + 1) * TILE]
        return carry

    lax.fori_loop(0, rows // TILE, tile, 0)


def attend(queries, pages, new_kv, position, tok_conv, page_conv, page_fill):
    rows, width = queries.shape
    page_len, channels = pages.shape[2], pages.shape[3]
    slots = position.shape[0]
    kv_local = channels // HD
    group_size = width // channels
    hist = slots * page_len
    fresh_base = hist + KEYS
    key_total = fresh_base + pl.cdiv(rows, KEYS) * KEYS + KEYS
    live = jnp.arange(page_len)[None, :] < page_fill[:, None]
    hist_conv = jnp.where(live, page_conv[:, None], -1).reshape(hist)
    tail = key_total - fresh_base - rows
    key_conv = jnp.concatenate(
        [hist_conv, jnp.full((KEYS,), -1, jnp.int32), tok_conv, jnp.full((tail,), -1, jnp.int32)]
    )[None]
    key_row = jnp.maximum(jnp.arange(key_total, dtype=jnp.int32) - fresh_base, -1)[None]
    lowest, highest = tok_conv[::TILE], tok_conv[TILE - 1 :: TILE]
    hist_at = jnp.sum(page_conv[None] < lowest[:, None], axis=1, dtype=jnp.int32) * page_len
    hist_at = hist_at // LANES * LANES
    hist_end = jnp.sum(page_conv[None] <= highest[:, None], axis=1, dtype=jnp.int32) * page_len
    hist_steps = (hist_end - hist_at + KEYS - 1) // KEYS
    fresh_at = jnp.sum(tok_conv[None] < lowest[:, None], axis=1, dtype=jnp.int32) // LANES * LANES
    fresh_end = (jnp.arange(rows // TILE, dtype=jnp.int32) + 1) * TILE
    fresh_steps = (fresh_end - fresh_at + KEYS - 1) // KEYS
    most = (hist // KEYS + 1 + pl.cdiv(rows, KEYS) + 1) * KEYS
    spec = (kv_local, group_size, slots, page_len, rows, fresh_base, key_total)
    smem = pl.BlockSpec(memory_space=pltpu.SMEM)
    vmem = pl.BlockSpec(memory_space=pltpu.VMEM)
    return pl.pallas_call(
        functools.partial(attend_kernel, spec),
        out_shape=jax.ShapeDtypeStruct((rows, width), jnp.bfloat16),
        in_specs=[smem] * 5 + [vmem] * 6,
        out_specs=vmem,
        scratch_shapes=[
            pltpu.VMEM((kv_local, key_total, HD), jnp.bfloat16),
            pltpu.VMEM((kv_local, key_total, 2 * HD), jnp.bfloat16),
            pltpu.VMEM((kv_local, group_size * TILE, most), jnp.float32),
            pltpu.VMEM((kv_local, group_size * TILE, 2 * HD), jnp.float32),
        ],
        compiler_params=pltpu.CompilerParams(vmem_limit_bytes=VMEM),
        cost_estimate=pl.CostEstimate(
            flops=rows * width * 800 * 4, bytes_accessed=8 << 20, transcendentals=rows * width // HD * 800
        ),
        name="attend",
    )(
        position, hist_at, hist_steps, fresh_at, fresh_steps,
        queries, pages, new_kv, key_conv, key_row, tok_conv[:, None],
    )


def project_kernel(places, attended, *refs):
    pieces, (kept, sent) = refs[:-2], refs[-2:]
    depth = pieces[0].shape[1]
    half = kept.shape[1]
    for row, out in ((places[0], kept), (places[1], sent)):
        total = None
        for n, piece in enumerate(pieces):
            at = pl.ds(pl.multiple_of(places[2 + n] * depth, depth), depth)
            term = jnp.dot(
                attended[pl.ds(pl.multiple_of(row * half, 16), half), at],
                piece[0],
                preferred_element_type=jnp.float32,
            )
            total = term if total is None else total + term
        out[0] = total.astype(jnp.bfloat16)


def project(attended, pieces, places):
    rows, width = attended.shape
    owners, depth, columns = pieces[0].shape
    half = rows // 2
    shape = jax.ShapeDtypeStruct((owners, half, columns), jnp.bfloat16)
    block = pl.BlockSpec((1, half, columns), lambda z, places: (z, 0, 0))
    return pl.pallas_call(
        project_kernel,
        out_shape=(shape, shape),
        grid_spec=pltpu.PrefetchScalarGridSpec(
            num_scalar_prefetch=1,
            grid=(owners,),
            in_specs=[pl.BlockSpec((rows, width), lambda z, places: (0, 0))]
            + [pl.BlockSpec((1, depth, columns), lambda z, places: (z, 0, 0))] * len(pieces),
            out_specs=(block, block),
        ),
        compiler_params=pltpu.CompilerParams(vmem_limit_bytes=VMEM),
        cost_estimate=pl.CostEstimate(
            flops=2 * rows * width * owners * columns,
            bytes_accessed=2 * (rows * width + (width + rows) * owners * columns),
            transcendentals=0,
        ),
        name="project",
    )(places, attended, *pieces)


def join_kernel(*refs):
    out = refs[-1]
    count = (len(refs) - 1) // 2
    columns = refs[0].shape[2]
    for n in range(count):
        total = refs[n][0].astype(jnp.float32) + refs[count + n][0].astype(jnp.float32)
        out[0, :, n * columns : (n + 1) * columns] = total.astype(jnp.bfloat16)


def join(kept, came):
    owners, half, columns = kept[0].shape
    count = len(kept)
    return pl.pallas_call(
        join_kernel,
        out_shape=jax.ShapeDtypeStruct((1, half, owners * columns * count), jnp.bfloat16),
        grid=(owners,),
        in_specs=[pl.BlockSpec((1, half, columns), lambda z: (z, 0, 0))] * (2 * count),
        out_specs=pl.BlockSpec((1, half, columns * count), lambda z: (0, 0, z)),
        compiler_params=pltpu.CompilerParams(vmem_limit_bytes=VMEM),
        name="join",
    )(*kept, *came)


SWAP = [(0, 1), (1, 0)]


def shards(
    queries, new_kv, pool, out_weight, tok_conv, page_conv, page_fill, page_owner, page_index
):
    row_count = queries.shape[1]
    slot_count = page_owner.shape[1]
    owner_count = lax.axis_size("seq")
    tp_count = lax.axis_size("tp")
    bucket = 2 * slot_count // owner_count
    group, role, tp = lax.axis_index("group"), lax.axis_index("role"), lax.axis_index("tp")

    depth = out_weight.shape[0] // 4
    columns = out_weight.shape[1]
    parts = PARTS if columns % (PARTS * LANES) == 0 else 1
    part = columns // parts
    quarter = lax.dynamic_slice_in_dim(out_weight, (2 * group + role) * depth, depth, 0)
    gathered = [
        lax.all_gather(quarter[:, n * part : (n + 1) * part], "seq", axis=0) for n in range(parts)
    ]
    weights = []
    for own in gathered:
        across = lax.ppermute(own, "group", SWAP)
        weights.append((own, across, lax.ppermute(own, "role", SWAP), lax.ppermute(across, "role", SWAP)))

    slot_owner = page_owner[0]
    position = slot_owner * bucket + bucket_ranks(slot_owner, owner_count)
    wanted = (
        jnp.zeros((owner_count * bucket,), jnp.int32)
        .at[position]
        .set(page_index[0], mode="promise_in_bounds", unique_indices=True)
        .reshape(owner_count, bucket)
    )
    asked = lax.all_to_all(wanted, "seq", split_axis=0, concat_axis=0, tiled=True)
    found = pool[0].at[asked].get(mode="promise_in_bounds")
    fetched = lax.all_to_all(found, "seq", split_axis=0, concat_axis=0, tiled=True)
    pages = fetched.reshape((owner_count * bucket,) + pool.shape[2:])

    attended = attend(
        queries[0], pages, new_kv[0].reshape(row_count, -1), position,
        tok_conv[0], page_conv[0], page_fill[0],
    )

    if tp_count != 2:
        partial = []
        places = jnp.stack(
            [0, 1, 2 * group + role, 2 * (1 - group) + role, 2 * group + 1 - role,
             2 * (1 - group) + 1 - role]
        ).astype(jnp.int32)
        for pieces in weights:
            partial.append(jnp.concatenate(project(attended, pieces, places), axis=1))
        partial = jnp.stack(partial, axis=2).transpose(1, 0, 2, 3).reshape(row_count, -1)
        return lax.psum_scatter(partial, "tp", scatter_dimension=0, tiled=True)[None]

    places = jnp.stack(
        [tp, 1 - tp, 2 * group + role, 2 * (1 - group) + role, 2 * group + 1 - role,
         2 * (1 - group) + 1 - role]
    ).astype(jnp.int32)
    kept, came = [], []
    for pieces in weights:
        mine, theirs = project(attended, pieces, places)
        kept.append(mine)
        came.append(lax.ppermute(theirs, "tp", SWAP))
    return join(kept, came)


def solution(mesh):
    return jax.shard_map(
        shards,
        mesh=mesh,
        in_specs=(
            P("role", ("group", "seq"), "tp"),
            P("role", ("group", "seq"), None, "tp"),
            P("role", ("group", "seq"), None, None, "tp"),
            P("tp", "seq"),
            P("role", ("group", "seq")),
            P("role", ("group", "seq")),
            P("role", ("group", "seq")),
            P("role", ("group", "seq")),
            P("role", ("group", "seq")),
        ),
        out_specs=P("role", ("group", "seq", "tp"), None),
        check_vma=False,
    )
```

```python
import functools
import math

import jax
import jax.numpy as jnp
from jax import lax
from jax.experimental import pallas as pl
from jax.experimental.pallas import tpu as pltpu
from jax.sharding import PartitionSpec as P

HD = 128
TILE = 64
KEYS = 256
LANES = 128
HIDDEN = -1e30
PARTS = 4
VMEM = 56 * 1024 * 1024


def bucket_ranks(slot_owner, owner_count):
    one_hot = (slot_owner[..., None] == jnp.arange(owner_count)).astype(jnp.int32)
    before = jnp.cumsum(one_hot, axis=-2) - one_hot
    return jnp.sum(before * one_hot, axis=-1)


def attend_kernel(
    spec, position, hist_at, hist_steps, fresh_at, fresh_steps,
    query, pages, fresh, key_conv, key_row, tok_conv, out, keys, values, scores, sums,
):
    kv_local, group_size, slots, page_len, rows, fresh_base, key_total = spec
    channels = kv_local * HD
    hist = slots * page_len
    for head in range(kv_local):
        values[head, :, HD:] = jnp.ones((key_total, HD), jnp.bfloat16)
        for first, last in ((hist, fresh_base), (fresh_base + rows, key_total)):
            keys[head, first:last] = jnp.zeros((last - first, HD), jnp.bfloat16)
            values[head, first:last, :HD] = jnp.zeros((last - first, HD), jnp.bfloat16)
        at = head * HD
        keys[head, fresh_base : fresh_base + rows] = fresh[:, at : at + HD]
        values[head, fresh_base : fresh_base + rows, :HD] = fresh[:, channels + at : channels + at + HD]

    def place(slot, carry):
        page = position[slot]
        row = pl.ds(pl.multiple_of(slot * page_len, page_len), page_len)
        for head in range(kv_local):
            at = head * HD
            keys[head, row] = pages[page, 0, :, at : at + HD]
            values[head, row, :HD] = pages[page, 1, :, at : at + HD]
        return carry

    lax.fori_loop(0, slots, place, 0, unroll=8)
    to_exp2 = math.log2(math.e) / math.sqrt(HD)
    wide = group_size * TILE

    def tile(index, carry):
        first = pl.multiple_of(index * TILE, TILE)
        tokens = pl.ds(first, TILE)
        conv = tok_conv[tokens]
        number = first + lax.broadcasted_iota(jnp.int32, (TILE, 1), 0)
        steps_h, steps_f = hist_steps[index], fresh_steps[index]
        at_h, at_f = hist_at[index], fresh_at[index]
        heads = [
            jnp.concatenate(
                [
                    query[tokens, (head * group_size + g) * HD : (head * group_size + g + 1) * HD]
                    for g in range(group_size)
                ],
                axis=0,
            )
            for head in range(kv_local)
        ]

        def key_range(step):
            start = jnp.where(
                step < steps_h, at_h + step * KEYS, fresh_base + at_f + (step - steps_h) * KEYS
            )
            return pl.ds(pl.multiple_of(start, LANES), KEYS)

        def score(step, tops):
            where = key_range(step)
            ok = (key_conv[:, where] == conv) & (key_row[:, where] <= number)
            held = pl.ds(pl.multiple_of(step * KEYS, KEYS), KEYS)
            new = []
            for head in range(kv_local):
                s = lax.dot_general(
                    heads[head], keys[head, where], (((1,), (1,)), ((), ())),
                    preferred_element_type=jnp.float32,
                ).reshape(group_size, TILE, KEYS)
                s = jnp.where(ok[None], s, HIDDEN).reshape(wide, KEYS)
                scores[head, :, held] = s
                top = tops[head]
                for k in range(0, KEYS, LANES):
                    top = jnp.maximum(top, s[:, k : k + LANES])
                new.append(top)
            return tuple(new)

        low = jnp.full((wide, LANES), HIDDEN, jnp.float32)
        tops = lax.fori_loop(0, steps_h + steps_f, score, (low,) * kv_local)
        tops = [jnp.max(top, axis=1, keepdims=True) * to_exp2 for top in tops]
        sums[...] = jnp.zeros_like(sums)

        def gather(step, carry):
            where = key_range(step)
            held = pl.ds(pl.multiple_of(step * KEYS, KEYS), KEYS)
            for head in range(kv_local):
                w = jnp.exp2(scores[head, :, held] * to_exp2 - tops[head]).astype(jnp.bfloat16)
                sums[head] += jnp.dot(w, values[head, where], preferred_element_type=jnp.float32)
            return carry

        lax.fori_loop(0, steps_h + steps_f, gather, 0)
        for head in range(kv_local):
            done = (sums[head, :, :HD] / sums[head, :, HD:]).astype(jnp.bfloat16)
            for g in range(group_size):
                at = (head * group_size + g) * HD
                out[tokens, at : at + HD] = done[g * TILE : (g + 1) * TILE]
        return carry

    lax.fori_loop(0, rows // TILE, tile, 0)


def attend(queries, pages, new_kv, position, tok_conv, page_conv, page_fill):
    rows, width = queries.shape
    page_len, channels = pages.shape[2], pages.shape[3]
    slots = position.shape[0]
    kv_local = channels // HD
    group_size = width // channels
    hist = slots * page_len
    fresh_base = hist + KEYS
    key_total = fresh_base + pl.cdiv(rows, KEYS) * KEYS + KEYS
    live = jnp.arange(page_len)[None, :] < page_fill[:, None]
    hist_conv = jnp.where(live, page_conv[:, None], -1).reshape(hist)
    tail = key_total - fresh_base - rows
    key_conv = jnp.concatenate(
        [hist_conv, jnp.full((KEYS,), -1, jnp.int32), tok_conv, jnp.full((tail,), -1, jnp.int32)]
    )[None]
    key_row = jnp.maximum(jnp.arange(key_total, dtype=jnp.int32) - fresh_base, -1)[None]
    lowest, highest = tok_conv[::TILE], tok_conv[TILE - 1 :: TILE]
    hist_at = jnp.sum(page_conv[None] < lowest[:, None], axis=1, dtype=jnp.int32) * page_len
    hist_at = hist_at // LANES * LANES
    hist_end = jnp.sum(page_conv[None] <= highest[:, None], axis=1, dtype=jnp.int32) * page_len
    hist_steps = (hist_end - hist_at + KEYS - 1) // KEYS
    fresh_at = jnp.sum(tok_conv[None] < lowest[:, None], axis=1, dtype=jnp.int32) // LANES * LANES
    fresh_end = (jnp.arange(rows // TILE, dtype=jnp.int32) + 1) * TILE
    fresh_steps = (fresh_end - fresh_at + KEYS - 1) // KEYS
    most = (hist // KEYS + 1 + pl.cdiv(rows, KEYS) + 1) * KEYS
    spec = (kv_local, group_size, slots, page_len, rows, fresh_base, key_total)
    smem = pl.BlockSpec(memory_space=pltpu.SMEM)
    vmem = pl.BlockSpec(memory_space=pltpu.VMEM)
    return pl.pallas_call(
        functools.partial(attend_kernel, spec),
        out_shape=jax.ShapeDtypeStruct((rows, width), jnp.bfloat16),
        in_specs=[smem] * 5 + [vmem] * 6,
        out_specs=vmem,
        scratch_shapes=[
            pltpu.VMEM((kv_local, key_total, HD), jnp.bfloat16),
            pltpu.VMEM((kv_local, key_total, 2 * HD), jnp.bfloat16),
            pltpu.VMEM((kv_local, group_size * TILE, most), jnp.float32),
            pltpu.VMEM((kv_local, group_size * TILE, 2 * HD), jnp.float32),
        ],
        compiler_params=pltpu.CompilerParams(vmem_limit_bytes=VMEM),
        cost_estimate=pl.CostEstimate(
            flops=rows * width * 800 * 4, bytes_accessed=8 << 20, transcendentals=rows * width // HD * 800
        ),
        name="attend",
    )(
        position, hist_at, hist_steps, fresh_at, fresh_steps,
        queries, pages, new_kv, key_conv, key_row, tok_conv[:, None],
    )


def project_kernel(kv_local, places, *refs):
    heads, pieces = refs[:kv_local], refs[kv_local:-3]
    kept, sent, left = refs[-3:]
    depth = pieces[0].shape[1]
    half = kept.shape[1]

    @pl.when(pl.program_id(0) == 0)
    def _():
        per_head = len(pieces) // kv_local
        for n in range(len(pieces)):
            at = (n % per_head) * depth
            for side in range(2):
                row = pl.multiple_of(places[side] * half, 16)
                left[places[2 + n], side * half : (side + 1) * half] = heads[n // per_head][
                    pl.ds(row, half), at : at + depth
                ]

    total = None
    for n, piece in enumerate(pieces):
        term = jnp.dot(left[n], piece[0], preferred_element_type=jnp.float32)
        total = term if total is None else total + term
    total = total.astype(jnp.bfloat16)
    kept[0] = total[:half]
    sent[0] = total[half:]


def project(heads, pieces, places):
    rows, width = heads[0].shape
    owners, depth, columns = pieces[0].shape
    half = rows // 2
    shape = jax.ShapeDtypeStruct((owners, half, columns), jnp.bfloat16)
    block = pl.BlockSpec((1, half, columns), lambda z, places: (z, 0, 0))
    total = width * len(heads)
    return pl.pallas_call(
        functools.partial(project_kernel, len(heads)),
        out_shape=(shape, shape),
        grid_spec=pltpu.PrefetchScalarGridSpec(
            num_scalar_prefetch=1,
            grid=(owners,),
            in_specs=[pl.BlockSpec((rows, width), lambda z, places: (0, 0))] * len(heads)
            + [pl.BlockSpec((1, depth, columns), lambda z, places: (z, 0, 0))] * len(pieces),
            out_specs=(block, block),
            scratch_shapes=[pltpu.VMEM((len(pieces), rows, depth), jnp.bfloat16)],
        ),
        compiler_params=pltpu.CompilerParams(vmem_limit_bytes=VMEM),
        cost_estimate=pl.CostEstimate(
            flops=2 * rows * total * owners * columns,
            bytes_accessed=2 * (rows * total + (total + rows) * owners * columns),
            transcendentals=0,
        ),
        name="project",
    )(places, *heads, *pieces)


def join_kernel(*refs):
    out = refs[-1]
    count = (len(refs) - 1) // 2
    columns = refs[0].shape[2]
    for n in range(count):
        total = refs[n][0].astype(jnp.float32) + refs[count + n][0].astype(jnp.float32)
        out[0, :, n * columns : (n + 1) * columns] = total.astype(jnp.bfloat16)


def join(kept, came):
    owners, half, columns = kept[0].shape
    count = len(kept)
    return pl.pallas_call(
        join_kernel,
        out_shape=jax.ShapeDtypeStruct((1, half, owners * columns * count), jnp.bfloat16),
        grid=(owners,),
        in_specs=[pl.BlockSpec((1, half, columns), lambda z: (z, 0, 0))] * (2 * count),
        out_specs=pl.BlockSpec((1, half, columns * count), lambda z: (0, 0, z)),
        compiler_params=pltpu.CompilerParams(vmem_limit_bytes=VMEM),
        name="join",
    )(*kept, *came)


def pick_kernel(asked, pool, *outs):
    kv_local = len(outs)

    def copy(n, carry):
        page = asked[n]
        for head in range(kv_local):
            outs[head][n] = pool[page, :, :, head * HD : (head + 1) * HD]
        return carry

    lax.fori_loop(0, outs[0].shape[0], copy, 0, unroll=8)


def pick(pool, asked):
    count = asked.shape[0]
    kv_local = pool.shape[3] // HD
    vmem = pl.BlockSpec(memory_space=pltpu.VMEM)
    return pl.pallas_call(
        pick_kernel,
        out_shape=tuple(
            jax.ShapeDtypeStruct((count,) + pool.shape[1:3] + (HD,), jnp.bfloat16)
            for _ in range(kv_local)
        ),
        in_specs=[pl.BlockSpec(memory_space=pltpu.SMEM), vmem],
        out_specs=(vmem,) * kv_local,
        compiler_params=pltpu.CompilerParams(vmem_limit_bytes=VMEM),
        name="pick",
    )(asked, pool)


SWAP = [(0, 1), (1, 0)]


def after(value, *others):
    return lax.optimization_barrier((value,) + others)[0]


def shards(
    queries, new_kv, pool, out_weight, tok_conv, page_conv, page_fill, page_owner, page_index
):
    row_count = queries.shape[1]
    slot_count = page_owner.shape[1]
    owner_count = lax.axis_size("seq")
    tp_count = lax.axis_size("tp")
    bucket = 2 * slot_count // owner_count
    group, role, tp = lax.axis_index("group"), lax.axis_index("role"), lax.axis_index("tp")

    kv_local = pool.shape[4] // HD

    own = 2 * group + role
    depth = out_weight.shape[0] // 4
    columns = out_weight.shape[1]
    parts = PARTS if columns % (PARTS * LANES) == 0 else 1
    part = columns // parts
    quarter = lax.dynamic_slice_in_dim(out_weight, own * depth, depth, 0)
    gathered = [
        lax.all_gather(quarter[:, n * part : (n + 1) * part], "seq", axis=0) for n in range(parts)
    ]

    slot_owner = page_owner[0]
    position = slot_owner * bucket + bucket_ranks(slot_owner, owner_count)
    wanted = (
        jnp.zeros((owner_count * bucket,), jnp.int32)
        .at[position]
        .set(page_index[0], mode="promise_in_bounds", unique_indices=True)
        .reshape(owner_count, bucket)
    )
    asked = lax.all_to_all(wanted, "seq", split_axis=0, concat_axis=0, tiled=True)
    found = pick(pool[0], asked.reshape(-1))

    order = [(q ^ own) for q in range(4)]
    order = [(v % 2) * 2 + v // 2 for v in order]
    flip = tp if tp_count == 2 else 0
    places = jnp.stack([jnp.asarray(v, jnp.int32) for v in (flip, 1 - flip, *order)])

    fresh = new_kv[0].reshape(row_count, 2, kv_local, HD)
    width = queries.shape[2] // kv_local
    heads = []
    weights = [None] * parts
    last = found[0]
    for head in range(kv_local):
        leaving = found[head] if head == 0 else after(found[head], last)
        came = lax.all_to_all(
            leaving.reshape((owner_count, bucket) + leaving.shape[1:]),
            "seq", split_axis=0, concat_axis=0, tiled=True,
        )
        if head < parts:
            across = lax.ppermute(after(gathered[head], last), "group", SWAP)
            weights[head] = (gathered[head], across)
        heads.append(
            attend(
                queries[0, :, head * width : (head + 1) * width],
                came.reshape((owner_count * bucket,) + leaving.shape[1:]),
                fresh[:, :, head].reshape(row_count, 2 * HD), position,
                tok_conv[0], page_conv[0], page_fill[0],
            )
        )
        last = came
    done = heads[-1]
    kept, sent, back = [], [], []
    for n in range(parts):
        if weights[n] is None:
            weights[n] = (gathered[n], lax.ppermute(after(gathered[n], done), "group", SWAP))
        one, two = weights[n]
        hold = last if n < kv_local else done
        pieces = (
            one, two, lax.ppermute(after(one, hold), "role", SWAP),
            lax.ppermute(after(two, hold), "role", SWAP),
        )
        mine, theirs = project(heads, pieces, places)
        kept.append(mine)
        sent.append(theirs)
        if n >= 1:
            done = mine
    if tp_count != 2:
        partial = [jnp.concatenate(both, axis=1) for both in zip(kept, sent)]
        partial = jnp.stack(partial, axis=2).transpose(1, 0, 2, 3).reshape(row_count, -1)
        return lax.psum_scatter(partial, "tp", scatter_dimension=0, tiled=True)[None]
    return join(kept, [lax.ppermute(theirs, "tp", SWAP) for theirs in sent])


def solution(mesh):
    return jax.shard_map(
        shards,
        mesh=mesh,
        in_specs=(
            P("role", ("group", "seq"), "tp"),
            P("role", ("group", "seq"), None, "tp"),
            P("role", ("group", "seq"), None, None, "tp"),
            P("tp", "seq"),
            P("role", ("group", "seq")),
            P("role", ("group", "seq")),
            P("role", ("group", "seq")),
            P("role", ("group", "seq")),
            P("role", ("group", "seq")),
        ),
        out_specs=P("role", ("group", "seq", "tp"), None),
        check_vma=False,
    )
```

```python
import functools
import math

import jax
import jax.numpy as jnp
from jax import lax
from jax.experimental import pallas as pl
from jax.experimental.pallas import tpu as pltpu
from jax.sharding import PartitionSpec as P

HD = 128
TILE = 32
KEYS = 256
LANES = 128
HIDDEN = -1e30
COLUMNS = 256
VMEM = 56 * 1024 * 1024


def bucket_ranks(slot_owner, owner_count):
    one_hot = (slot_owner[..., None] == jnp.arange(owner_count)).astype(jnp.int32)
    before = jnp.cumsum(one_hot, axis=-2) - one_hot
    return jnp.sum(before * one_hot, axis=-1)


def attend_kernel(
    spec, control, position, hist_at, hist_steps, fresh_at, fresh_steps,
    query, pages, fresh, key_conv, key_row, tok_conv, out, keys, values, scores, sums,
):
    kv_local, group_size, slots, page_len, rows, fresh_base, key_total = spec
    channels = kv_local * HD
    hist = slots * page_len
    half, depth = out.shape[1], out.shape[2]
    tiles = half // TILE
    for head in range(kv_local):
        values[head, :, HD:] = jnp.ones((key_total, HD), jnp.bfloat16)
        for first, last in ((hist, fresh_base), (fresh_base + rows, key_total)):
            keys[head, first:last] = jnp.zeros((last - first, HD), jnp.bfloat16)
            values[head, first:last, :HD] = jnp.zeros((last - first, HD), jnp.bfloat16)
        at = head * HD
        keys[head, fresh_base : fresh_base + rows] = fresh[:, at : at + HD]
        values[head, fresh_base : fresh_base + rows, :HD] = fresh[:, channels + at : channels + at + HD]

    def place(slot, carry):
        page = position[slot]
        row = pl.ds(pl.multiple_of(slot * page_len, page_len), page_len)
        for head in range(kv_local):
            at = head * HD
            keys[head, row] = pages[page, 0, :, at : at + HD]
            values[head, row, :HD] = pages[page, 1, :, at : at + HD]
        return carry

    lax.fori_loop(0, slots, place, 0, unroll=8)
    to_exp2 = math.log2(math.e) / math.sqrt(HD)
    wide = group_size * TILE

    def tile(number_here, carry):
        index = control[0] * tiles + number_here
        first = pl.multiple_of(index * TILE, TILE)
        leaving = pl.ds(pl.multiple_of(number_here * TILE, TILE), TILE)
        tokens = pl.ds(first, TILE)
        conv = tok_conv[tokens]
        number = first + lax.broadcasted_iota(jnp.int32, (TILE, 1), 0)
        steps_h, steps_f = hist_steps[index], fresh_steps[index]
        at_h, at_f = hist_at[index], fresh_at[index]
        heads = [
            jnp.concatenate(
                [
                    query[tokens, (head * group_size + g) * HD : (head * group_size + g + 1) * HD]
                    for g in range(group_size)
                ],
                axis=0,
            )
            for head in range(kv_local)
        ]

        def key_range(step):
            start = jnp.where(
                step < steps_h, at_h + step * KEYS, fresh_base + at_f + (step - steps_h) * KEYS
            )
            return pl.ds(pl.multiple_of(start, LANES), KEYS)

        def score(step, tops):
            where = key_range(step)
            ok = (key_conv[:, where] == conv) & (key_row[:, where] <= number)
            held = pl.ds(pl.multiple_of(step * KEYS, KEYS), KEYS)
            new = []
            for head in range(kv_local):
                s = lax.dot_general(
                    heads[head], keys[head, where], (((1,), (1,)), ((), ())),
                    preferred_element_type=jnp.float32,
                ).reshape(group_size, TILE, KEYS)
                s = jnp.where(ok[None], s, HIDDEN).reshape(wide, KEYS)
                scores[head, :, held] = s
                top = tops[head]
                for k in range(0, KEYS, LANES):
                    top = jnp.maximum(top, s[:, k : k + LANES])
                new.append(top)
            return tuple(new)

        low = jnp.full((wide, LANES), HIDDEN, jnp.float32)
        tops = lax.fori_loop(0, steps_h + steps_f, score, (low,) * kv_local)
        tops = [jnp.max(top, axis=1, keepdims=True) * to_exp2 for top in tops]
        sums[...] = jnp.zeros_like(sums)

        def gather(step, carry):
            where = key_range(step)
            held = pl.ds(pl.multiple_of(step * KEYS, KEYS), KEYS)
            for head in range(kv_local):
                w = jnp.exp2(scores[head, :, held] * to_exp2 - tops[head]).astype(jnp.bfloat16)
                sums[head] += jnp.dot(w, values[head, where], preferred_element_type=jnp.float32)
            return carry

        lax.fori_loop(0, steps_h + steps_f, gather, 0)
        for head in range(kv_local):
            done = (sums[head, :, :HD] / sums[head, :, HD:]).astype(jnp.bfloat16)
            for g in range(group_size):
                at = (head * group_size + g) * HD
                out[control[1 + at // depth], leaving, at % depth : at % depth + HD] = done[
                    g * TILE : (g + 1) * TILE
                ]
        return carry

    lax.fori_loop(0, tiles, tile, 0)


def attend_tables(rows, slots, page_len, tok_conv, page_conv, page_fill):
    hist = slots * page_len
    fresh_base = hist + KEYS
    key_total = fresh_base + pl.cdiv(rows, KEYS) * KEYS + KEYS
    live = jnp.arange(page_len)[None, :] < page_fill[:, None]
    hist_conv = jnp.where(live, page_conv[:, None], -1).reshape(hist)
    tail = key_total - fresh_base - rows
    key_conv = jnp.concatenate(
        [hist_conv, jnp.full((KEYS,), -1, jnp.int32), tok_conv, jnp.full((tail,), -1, jnp.int32)]
    )[None]
    key_row = jnp.maximum(jnp.arange(key_total, dtype=jnp.int32) - fresh_base, -1)[None]
    lowest, highest = tok_conv[::TILE], tok_conv[TILE - 1 :: TILE]
    hist_at = jnp.sum(page_conv[None] < lowest[:, None], axis=1, dtype=jnp.int32) * page_len
    hist_at = hist_at // LANES * LANES
    hist_end = jnp.sum(page_conv[None] <= highest[:, None], axis=1, dtype=jnp.int32) * page_len
    hist_steps = (hist_end - hist_at + KEYS - 1) // KEYS
    fresh_at = jnp.sum(tok_conv[None] < lowest[:, None], axis=1, dtype=jnp.int32) // LANES * LANES
    fresh_end = (jnp.arange(rows // TILE, dtype=jnp.int32) + 1) * TILE
    fresh_steps = (fresh_end - fresh_at + KEYS - 1) // KEYS
    return key_conv, key_row, tok_conv[:, None], hist_at, hist_steps, fresh_at, fresh_steps


def attend(control, tables, position, queries, pages, new_kv):
    rows, width = queries.shape
    page_len, channels = pages.shape[2], pages.shape[3]
    slots = position.shape[0]
    kv_local = channels // HD
    group_size = width // channels
    hist = slots * page_len
    fresh_base = hist + KEYS
    key_total = fresh_base + pl.cdiv(rows, KEYS) * KEYS + KEYS
    key_conv, key_row, tok_conv, *steps = tables
    depth = width // 4
    most = (hist // KEYS + 1 + pl.cdiv(rows, KEYS) + 1) * KEYS
    spec = (kv_local, group_size, slots, page_len, rows, fresh_base, key_total)
    smem = pl.BlockSpec(memory_space=pltpu.SMEM)
    vmem = pl.BlockSpec(memory_space=pltpu.VMEM)
    return pl.pallas_call(
        functools.partial(attend_kernel, spec),
        out_shape=jax.ShapeDtypeStruct((4, rows // 2, depth), jnp.bfloat16),
        in_specs=[smem] * 6 + [vmem] * 6,
        out_specs=vmem,
        scratch_shapes=[
            pltpu.VMEM((kv_local, key_total, HD), jnp.bfloat16),
            pltpu.VMEM((kv_local, key_total, 2 * HD), jnp.bfloat16),
            pltpu.VMEM((kv_local, group_size * TILE, most), jnp.float32),
            pltpu.VMEM((kv_local, group_size * TILE, 2 * HD), jnp.float32),
        ],
        compiler_params=pltpu.CompilerParams(vmem_limit_bytes=VMEM),
        cost_estimate=pl.CostEstimate(
            flops=rows * width * 800 * 2, bytes_accessed=8 << 20, transcendentals=rows * width // HD * 400
        ),
        name="attend",
    )(
        control, position, *steps, queries, pages, new_kv, key_conv, key_row, tok_conv,
    )


def multiply(left, pieces):
    total = None
    for n, piece in enumerate(pieces):
        term = jnp.dot(left[n], piece[...], preferred_element_type=jnp.float32)
        total = term if total is None else total + term
    return total.astype(jnp.bfloat16)


def project_kernel(rows_at, left, *refs):
    refs[-1][...] = multiply(left, refs[:-1])


def finish_kernel(rows_at, left, came, *refs):
    pieces = refs[:4]
    total = multiply(left, pieces).astype(jnp.float32) + came[...].astype(jnp.float32)
    refs[-1][0] = total.astype(jnp.bfloat16)


def project(left, pieces, rows_at, came=None, base=None, out=None, width=None):
    depth = left.shape[2]
    half = left.shape[1]
    columns = pieces[0].shape[1]
    cut = min(COLUMNS, columns)
    table = rows_at if base is None else jnp.concatenate([rows_at, (base * (columns // cut))[None]])
    in_specs = [pl.BlockSpec(left.shape, lambda j, at: (0, 0, 0))]
    operands = [left]
    aliases = {}
    if came is None:
        kernel = project_kernel
        out_shape = jax.ShapeDtypeStruct((half, columns), jnp.bfloat16)
        out_specs = pl.BlockSpec((half, cut), lambda j, at: (0, j))
    else:
        kernel = finish_kernel
        in_specs.append(pl.BlockSpec((half, cut), lambda j, at: (0, j)))
        operands.append(came)
        out_shape = jax.ShapeDtypeStruct((1, half, width), jnp.bfloat16)
        out_specs = pl.BlockSpec((1, half, cut), lambda j, at: (0, 0, at[4] + j))
    for n in range(4):
        in_specs.append(pl.BlockSpec((depth, cut), functools.partial(lambda n, j, at: (at[n], j), n)))
    operands += pieces
    if out is not None:
        in_specs.append(pl.BlockSpec(memory_space=pl.ANY))
        operands.append(out)
        aliases = {len(operands): 0}
    return pl.pallas_call(
        kernel,
        out_shape=out_shape,
        grid_spec=pltpu.PrefetchScalarGridSpec(
            num_scalar_prefetch=1, grid=(columns // cut,), in_specs=in_specs, out_specs=out_specs
        ),
        input_output_aliases=aliases,
        compiler_params=pltpu.CompilerParams(vmem_limit_bytes=VMEM),
        cost_estimate=pl.CostEstimate(
            flops=8 * half * depth * columns, bytes_accessed=8 * depth * (columns + half), transcendentals=0
        ),
        name="project" if came is None else "finish",
    )(table.astype(jnp.int32), *operands)


def pick_kernel(asked, pool, out):
    def copy(n, carry):
        out[n] = pool[asked[n]]
        return carry

    lax.fori_loop(0, out.shape[0], copy, 0, unroll=8)


def pick(pool, asked):
    vmem = pl.BlockSpec(memory_space=pltpu.VMEM)
    return pl.pallas_call(
        pick_kernel,
        out_shape=jax.ShapeDtypeStruct(asked.shape + pool.shape[1:], jnp.bfloat16),
        in_specs=[pl.BlockSpec(memory_space=pltpu.SMEM), vmem],
        out_specs=vmem,
        compiler_params=pltpu.CompilerParams(vmem_limit_bytes=VMEM),
        name="pick",
    )(asked, pool)


SWAP = [(0, 1), (1, 0)]


def after(value, *others):
    return lax.optimization_barrier((value,) + others)[0]


def shards(
    queries, new_kv, pool, out_weight, tok_conv, page_conv, page_fill, page_owner, page_index
):
    row_count = queries.shape[1]
    slot_count = page_owner.shape[1]
    owner_count = lax.axis_size("seq")
    tp_count = lax.axis_size("tp")
    bucket = 2 * slot_count // owner_count
    group, role, tp = lax.axis_index("group"), lax.axis_index("role"), lax.axis_index("tp")
    seq = lax.axis_index("seq")


    own = 2 * group + role
    depth = out_weight.shape[0] // 4
    columns = out_weight.shape[1]
    quarter = lax.dynamic_slice_in_dim(out_weight, own * depth, depth, 0)
    order = [q ^ own for q in range(4)]
    order = [(v % 2) * 2 + v // 2 for v in order]
    flip = tp if tp_count == 2 else 0

    def control(side):
        return jnp.stack([jnp.asarray(v, jnp.int32) for v in (side, *order)])

    whole = jnp.zeros((4,), jnp.int32)
    swap_group = functools.partial(lax.ppermute, axis_name="group", perm=SWAP)
    swap_role = functools.partial(lax.ppermute, axis_name="role", perm=SWAP)

    if owner_count == 4:
        middle = (seq == 1) | (seq == 2)
        near = lax.ppermute(quarter, "seq", [(0, 1), (1, 0), (2, 3), (3, 2)])
        inner = lax.ppermute(quarter, "seq", [(1, 2), (2, 1)])

    slot_owner = page_owner[0]
    position = slot_owner * bucket + bucket_ranks(slot_owner, owner_count)
    wanted = (
        jnp.zeros((owner_count * bucket,), jnp.int32)
        .at[position]
        .set(page_index[0], mode="promise_in_bounds", unique_indices=True)
        .reshape(owner_count, bucket)
    )
    asked = lax.all_to_all(wanted, "seq", split_axis=0, concat_axis=0, tiled=True)
    found = pick(pool[0], asked.reshape(-1))
    pages = lax.all_to_all(
        found.reshape((owner_count, bucket) + found.shape[1:]),
        "seq", split_axis=0, concat_axis=0, tiled=True,
    ).reshape(found.shape)
    fresh = new_kv[0].reshape(row_count, -1)
    tables = attend_tables(
        row_count, slot_count, pool.shape[3], tok_conv[0], page_conv[0], page_fill[0]
    )

    if owner_count != 4 or tp_count != 2:
        mine = lax.all_gather(quarter, "seq", axis=1, tiled=True)
        across = swap_group(mine)
        pieces = [mine, across, swap_role(mine), swap_role(across)]
        partial = [
            project(attend(control(side), tables, position, queries[0], pages, fresh), pieces, whole)
            for side in (0, 1)
        ]
        return lax.psum_scatter(
            jnp.concatenate(partial, axis=0), "tp", scatter_dimension=0, tiled=True
        )[None]

    swap_tp = functools.partial(lax.ppermute, axis_name="tp", perm=SWAP)
    forward = functools.partial(lax.ppermute, axis_name="seq", perm=[(1, 0), (2, 3)])
    cross = functools.partial(lax.ppermute, axis_name="seq", perm=[(1, 2), (2, 1)])
    cut = columns // 2

    def four(one, two, *hold):
        return [one, two, swap_role(after(one, *hold)), swap_role(after(two, *hold))]

    near, inner = after(near, found), after(inner, found)
    near_across = swap_group(near)
    far_a = cross(near[:, :cut])
    next_shard = jnp.where(middle, inner, forward(inner))
    next_across = swap_group(next_shard)
    far_a = jnp.where(middle, far_a, forward(far_a))
    far_a_across = swap_group(far_a)
    near_all = four(near, near_across)
    next_all = four(next_shard, next_across)

    far_b = cross(after(near[:, cut:], pages))
    pages = after(pages, near_across, next_shard, far_a)
    left = attend(control(1 - flip), tables, position, queries[0], pages, fresh)
    far_b_on = forward(after(far_b, left))
    local = jnp.stack([own, own ^ 2, own ^ 1, own ^ 3]).astype(jnp.int32)
    sent = [project(left, [out_weight] * 4, local)]
    far_a_all = four(far_a, far_a_across)
    for pieces in (near_all, next_all, far_a_all):
        sent.append(project(after(left, sent[-1]), pieces, whole))
    came = [swap_tp(part) for part in sent]
    far_b = jnp.where(middle, far_b, after(far_b_on, sent[2]))
    far_b_across = swap_group(far_b)
    stay = attend(
        control(flip), tables, position, queries[0], after(pages, sent[3], far_b), fresh
    )
    far_b_all = four(far_b, far_b_across, stay)
    total = columns * owner_count
    second = jnp.where(seq < 2, 2, 1)
    third = jnp.where(seq < 2, 3, 0)
    out = project(stay, [out_weight] * 4, local, came[0], seq, None, total)
    out = project(stay, near_all, whole, came[1], seq ^ 1, out, total)
    last = project(after(left, out), far_b_all, whole)
    stay = after(stay, last)
    last = swap_tp(last)
    out = project(stay, next_all, whole, came[2], second, out, total)
    out = project(stay, far_a_all, whole, came[3], 2 * third, out, total)
    return project(stay, far_b_all, whole, last, 2 * third + 1, out, total)


def solution(mesh):
    return jax.shard_map(
        shards,
        mesh=mesh,
        in_specs=(
            P("role", ("group", "seq"), "tp"),
            P("role", ("group", "seq"), None, "tp"),
            P("role", ("group", "seq"), None, None, "tp"),
            P("tp", "seq"),
            P("role", ("group", "seq")),
            P("role", ("group", "seq")),
            P("role", ("group", "seq")),
            P("role", ("group", "seq")),
            P("role", ("group", "seq")),
        ),
        out_specs=P("role", ("group", "seq", "tp"), None),
        check_vma=False,
    )
```

```python
import functools
import math

import jax
import jax.numpy as jnp
from jax import lax
from jax.experimental import pallas as pl
from jax.experimental.pallas import tpu as pltpu
from jax.sharding import PartitionSpec as P

HD = 128
TILE = 64
KEYS = 256
LANES = 128
HIDDEN = -1e30
COLUMNS = 256
MIB = 1024 * 1024


def cost(flops=3 * 10**9):
    return pl.CostEstimate(flops=flops, bytes_accessed=1000, transcendentals=0)


def rank_kernel(owner, page, position, wanted, count):
    owners, bucket = wanted.shape
    for n in range(owners):
        count[n] = 0

    def clear(k, carry):
        for n in range(owners):
            wanted[n, k] = 0
        return carry

    lax.fori_loop(0, bucket, clear, 0)

    def put(slot, carry):
        to = owner[0, slot]
        rank = count[to]
        count[to] = rank + 1
        wanted[to, rank] = page[0, slot]
        position[slot] = to * bucket + rank
        return carry

    lax.fori_loop(0, owner.shape[1], put, 0, unroll=4)


def rank(page_owner, page_index, owners, bucket):
    smem = pl.BlockSpec(memory_space=pltpu.SMEM)
    return pl.pallas_call(
        rank_kernel,
        out_shape=(
            jax.ShapeDtypeStruct((page_owner.shape[1],), jnp.int32),
            jax.ShapeDtypeStruct((owners, bucket), jnp.int32),
        ),
        in_specs=[smem, smem],
        out_specs=(smem, smem),
        scratch_shapes=[pltpu.SMEM((owners,), jnp.int32)],
        cost_estimate=cost(),
        name="rank",
    )(page_owner, page_index)


def place_kernel(position, pages, fresh, keys, values):
    kv_local, key_total = keys.shape[:2]
    slots, page_len, rows = position.shape[0], pages.shape[2], fresh.shape[0]
    channels = kv_local * HD
    hist = slots * page_len
    fresh_base = hist + KEYS
    for head in range(kv_local):
        values[head, :, HD:] = jnp.ones((key_total, HD), jnp.bfloat16)
        for first, last in ((hist, fresh_base), (fresh_base + rows, key_total)):
            keys[head, first:last] = jnp.zeros((last - first, HD), jnp.bfloat16)
            values[head, first:last, :HD] = jnp.zeros((last - first, HD), jnp.bfloat16)
        at = head * HD
        keys[head, fresh_base : fresh_base + rows] = fresh[:, at : at + HD]
        values[head, fresh_base : fresh_base + rows, :HD] = fresh[:, channels + at : channels + at + HD]

    def place(slot, carry):
        page = position[slot]
        row = pl.ds(pl.multiple_of(slot * page_len, page_len), page_len)
        for head in range(kv_local):
            at = head * HD
            keys[head, row] = pages[page, 0, :, at : at + HD]
            values[head, row, :HD] = pages[page, 1, :, at : at + HD]
        return carry

    lax.fori_loop(0, slots, place, 0, unroll=8)


def place(position, pages, fresh):
    kv_local = pages.shape[3] // HD
    rows = fresh.shape[0]
    key_total = position.shape[0] * pages.shape[2] + KEYS + pl.cdiv(rows, KEYS) * KEYS + KEYS
    vmem = pl.BlockSpec(memory_space=pltpu.VMEM)
    return pl.pallas_call(
        place_kernel,
        out_shape=(
            jax.ShapeDtypeStruct((kv_local, key_total, HD), jnp.bfloat16),
            jax.ShapeDtypeStruct((kv_local, key_total, 2 * HD), jnp.bfloat16),
        ),
        in_specs=[pl.BlockSpec(memory_space=pltpu.SMEM), vmem, vmem],
        out_specs=(vmem, vmem),
        compiler_params=pltpu.CompilerParams(vmem_limit_bytes=20 * MIB),
        cost_estimate=cost(),
        name="place",
    )(position, pages, fresh)


def attend_kernel(
    fresh_base, side, control, hist_at, hist_steps, fresh_at, fresh_steps,
    query, keys, values, key_conv, key_row, tok_conv, out, scores, sums,
):
    kv_local = keys.shape[0]
    group_size = query.shape[1] // (kv_local * HD)
    half, depth = out.shape[1], out.shape[2]
    tiles = half // TILE
    to_exp2 = math.log2(math.e) / math.sqrt(HD)
    wide = group_size * TILE

    def tile(number_here, carry):
        index = control[side] * tiles + number_here
        first = pl.multiple_of(index * TILE, TILE)
        leaving = pl.ds(pl.multiple_of(number_here * TILE, TILE), TILE)
        tokens = pl.ds(first, TILE)
        conv = tok_conv[tokens]
        number = first + lax.broadcasted_iota(jnp.int32, (TILE, 1), 0)
        steps_h, steps_f = hist_steps[index], fresh_steps[index]
        at_h, at_f = hist_at[index], fresh_at[index]
        heads = [
            jnp.concatenate(
                [
                    query[tokens, (head * group_size + g) * HD : (head * group_size + g + 1) * HD]
                    for g in range(group_size)
                ],
                axis=0,
            )
            for head in range(kv_local)
        ]

        def key_range(step):
            start = jnp.where(
                step < steps_h, at_h + step * KEYS, fresh_base + at_f + (step - steps_h) * KEYS
            )
            return pl.ds(pl.multiple_of(start, LANES), KEYS)

        def score(step, tops):
            where = key_range(step)
            ok = (key_conv[:, where] == conv) & (key_row[:, where] <= number)
            held = pl.ds(pl.multiple_of(step * KEYS, KEYS), KEYS)
            new = []
            for head in range(kv_local):
                s = lax.dot_general(
                    heads[head], keys[head, where], (((1,), (1,)), ((), ())),
                    preferred_element_type=jnp.float32,
                ).reshape(group_size, TILE, KEYS)
                s = jnp.where(ok[None], s, HIDDEN).reshape(wide, KEYS)
                scores[head, :, held] = s
                top = tops[head]
                for k in range(0, KEYS, LANES):
                    top = jnp.maximum(top, s[:, k : k + LANES])
                new.append(top)
            return tuple(new)

        low = jnp.full((wide, LANES), HIDDEN, jnp.float32)
        tops = lax.fori_loop(0, steps_h + steps_f, score, (low,) * kv_local)
        tops = [jnp.max(top, axis=1, keepdims=True) * to_exp2 for top in tops]
        sums[...] = jnp.zeros_like(sums)

        def gather(step, carry):
            where = key_range(step)
            held = pl.ds(pl.multiple_of(step * KEYS, KEYS), KEYS)
            for head in range(kv_local):
                w = jnp.exp2(scores[head, :, held] * to_exp2 - tops[head]).astype(jnp.bfloat16)
                sums[head] += jnp.dot(w, values[head, where], preferred_element_type=jnp.float32)
            return carry

        lax.fori_loop(0, steps_h + steps_f, gather, 0)
        for head in range(kv_local):
            done = (sums[head, :, :HD] / sums[head, :, HD:]).astype(jnp.bfloat16)
            for g in range(group_size):
                at = (head * group_size + g) * HD
                out[control[2 + at // depth], leaving, at % depth : at % depth + HD] = done[
                    g * TILE : (g + 1) * TILE
                ]
        return carry

    lax.fori_loop(0, tiles, tile, 0)


def attend_tables(rows, slots, page_len, tok_conv, page_conv, page_fill):
    hist = slots * page_len
    fresh_base = hist + KEYS
    key_total = fresh_base + pl.cdiv(rows, KEYS) * KEYS + KEYS
    live = jnp.arange(page_len)[None, :] < page_fill[:, None]
    hist_conv = jnp.where(live, page_conv[:, None], -1).reshape(hist)
    tail = key_total - fresh_base - rows
    key_conv = jnp.concatenate(
        [hist_conv, jnp.full((KEYS,), -1, jnp.int32), tok_conv, jnp.full((tail,), -1, jnp.int32)]
    )[None]
    key_row = jnp.maximum(jnp.arange(key_total, dtype=jnp.int32) - fresh_base, -1)[None]
    lowest, highest = tok_conv[::TILE], tok_conv[TILE - 1 :: TILE]
    hist_at = jnp.sum(page_conv[None] < lowest[:, None], axis=1, dtype=jnp.int32) * page_len
    hist_at = hist_at // LANES * LANES
    hist_end = jnp.sum(page_conv[None] <= highest[:, None], axis=1, dtype=jnp.int32) * page_len
    hist_steps = (hist_end - hist_at + KEYS - 1) // KEYS
    fresh_at = jnp.sum(tok_conv[None] < lowest[:, None], axis=1, dtype=jnp.int32) // LANES * LANES
    fresh_end = (jnp.arange(rows // TILE, dtype=jnp.int32) + 1) * TILE
    fresh_steps = (fresh_end - fresh_at + KEYS - 1) // KEYS
    return key_conv, key_row, tok_conv[:, None], hist_at, hist_steps, fresh_at, fresh_steps


def attend(side, control, tables, queries, keys, values, slots):
    rows, width = queries.shape
    kv_local, key_total = keys.shape[:2]
    group_size = width // (kv_local * HD)
    key_conv, key_row, tok_conv, *steps = tables
    fresh_base = slots + KEYS
    most = slots // KEYS + pl.cdiv(rows, KEYS) + 2
    smem = pl.BlockSpec(memory_space=pltpu.SMEM)
    vmem = pl.BlockSpec(memory_space=pltpu.VMEM)
    return pl.pallas_call(
        functools.partial(attend_kernel, fresh_base, side),
        out_shape=jax.ShapeDtypeStruct((4, rows // 2, width // 4), jnp.bfloat16),
        in_specs=[smem] * 5 + [vmem] * 6,
        out_specs=vmem,
        scratch_shapes=[
            pltpu.VMEM((kv_local, group_size * TILE, most * KEYS), jnp.float32),
            pltpu.VMEM((kv_local, group_size * TILE, 2 * HD), jnp.float32),
        ],
        compiler_params=pltpu.CompilerParams(vmem_limit_bytes=28 * MIB),
        cost_estimate=cost(16 * 10**9),
        name="attend",
    )(control, *steps, queries, keys, values, key_conv, key_row, tok_conv)


def multiply(left, pieces, at):
    total = None
    for n, piece in enumerate(pieces):
        term = jnp.dot(left[n], piece[:, at], preferred_element_type=jnp.float32)
        total = term if total is None else total + term
    return total.astype(jnp.bfloat16)


def blocks(columns):
    cut = min(COLUMNS, columns)
    return [slice(k, k + cut) for k in range(0, columns, cut)]


def quarters(control, refs):
    if len(refs) == 4:
        return refs
    depth = refs[0].shape[0] // 4
    return [refs[0].at[pl.ds(pl.multiple_of(control[6 + n] * depth, depth), depth)] for n in range(4)]


def project_kernel(control, left, *refs):
    pieces = quarters(control, refs[:-1])
    for at in blocks(pieces[0].shape[1]):
        refs[-1][:, at] = multiply(left, pieces, at)


def finish_kernel(has_out, control, left, came, *refs):
    pieces = quarters(control, refs[: len(refs) - 1 - has_out])
    for at in blocks(pieces[0].shape[1]):
        total = multiply(left, pieces, at).astype(jnp.float32) + came[:, at].astype(jnp.float32)
        refs[-1][0, :, at] = total.astype(jnp.bfloat16)


def project(control, left, pieces, came=None, base=None, out=None, width=None):
    half = left.shape[1]
    columns = pieces[0].shape[1]
    vmem = pl.BlockSpec(memory_space=pltpu.VMEM)
    in_specs = [vmem]
    operands = [left]
    aliases = {}
    if came is None:
        kernel = project_kernel
        out_shape = jax.ShapeDtypeStruct((half, columns), jnp.bfloat16)
        out_specs = vmem
    else:
        kernel = functools.partial(finish_kernel, int(out is not None))
        in_specs.append(vmem)
        operands.append(came)
        out_shape = jax.ShapeDtypeStruct((1, half, width), jnp.bfloat16)
        out_specs = pl.BlockSpec((1, half, columns), lambda j, control: (0, 0, control[base]))
    in_specs += [vmem] * len(pieces)
    operands += pieces
    if out is not None:
        in_specs.append(pl.BlockSpec(memory_space=pl.ANY))
        operands.append(out)
        aliases = {len(operands): 0}
    return pl.pallas_call(
        kernel,
        out_shape=out_shape,
        grid_spec=pltpu.PrefetchScalarGridSpec(
            num_scalar_prefetch=1, grid=(1,), in_specs=in_specs, out_specs=out_specs
        ),
        input_output_aliases=aliases,
        compiler_params=pltpu.CompilerParams(vmem_limit_bytes=16 * MIB),
        cost_estimate=cost(),
        name="project" if came is None else "finish",
    )(control, *operands)


def pick_kernel(asked, pool, out):
    for owner in range(asked.shape[0]):

        def copy(n, carry):
            out[owner, n] = pool[asked[owner, n]]
            return carry

        lax.fori_loop(0, asked.shape[1], copy, 0, unroll=8)


def pick(pool, asked):
    vmem = pl.BlockSpec(memory_space=pltpu.VMEM)
    return pl.pallas_call(
        pick_kernel,
        out_shape=jax.ShapeDtypeStruct(asked.shape + pool.shape[1:], jnp.bfloat16),
        in_specs=[pl.BlockSpec(memory_space=pltpu.SMEM), vmem],
        out_specs=vmem,
        compiler_params=pltpu.CompilerParams(vmem_limit_bytes=16 * MIB),
        cost_estimate=cost(),
        name="pick",
    )(asked, pool)


SWAP = [(0, 1), (1, 0)]


def after(value, *others):
    return lax.optimization_barrier((value,) + others)[0]


def shards(
    queries, new_kv, pool, out_weight, tok_conv, page_conv, page_fill, page_owner, page_index
):
    row_count = queries.shape[1]
    slot_count = page_owner.shape[1]
    owner_count = lax.axis_size("seq")
    tp_count = lax.axis_size("tp")
    bucket = 2 * slot_count // owner_count
    group, role, tp = lax.axis_index("group"), lax.axis_index("role"), lax.axis_index("tp")
    seq = lax.axis_index("seq")


    own = 2 * group + role
    depth = out_weight.shape[0] // 4
    columns = out_weight.shape[1]
    quarter = lax.dynamic_slice_in_dim(out_weight, own * depth, depth, 0)
    order = [q ^ own for q in range(4)]
    order = [(v % 2) * 2 + v // 2 for v in order]
    flip = tp if tp_count == 2 else 0
    second = jnp.where(seq < 2, 2, 1)
    third = 2 * jnp.where(seq < 2, 3, 0)
    local = [own, own ^ 2, own ^ 1, own ^ 3]
    control = jnp.stack(
        [
            jnp.asarray(v, jnp.int32)
            for v in (flip, 1 - flip, *order, *local, seq, seq ^ 1, second, third, third + 1)
        ]
    )
    swap_group = functools.partial(lax.ppermute, axis_name="group", perm=SWAP)
    swap_role = functools.partial(lax.ppermute, axis_name="role", perm=SWAP)

    if owner_count == 4:
        middle = (seq == 1) | (seq == 2)
        near = lax.ppermute(quarter, "seq", [(0, 1), (1, 0), (2, 3), (3, 2)])
        inner = lax.ppermute(quarter, "seq", [(1, 2), (2, 1)])

    position, wanted = rank(page_owner, page_index, owner_count, bucket)
    asked = lax.all_to_all(wanted, "seq", split_axis=0, concat_axis=0, tiled=True)
    if owner_count == 4:
        near, inner = after(near, asked), after(inner, asked)
        asked = after(asked, near, inner)
    found = pick(pool[0], asked)
    pages = lax.all_to_all(found, "seq", split_axis=0, concat_axis=0, tiled=True)
    pages = pages.reshape((owner_count * bucket,) + found.shape[2:])
    slots = slot_count * pool.shape[3]
    fresh = new_kv[0].reshape(row_count, -1)
    tables = attend_tables(
        row_count, slot_count, pool.shape[3], tok_conv[0], page_conv[0], page_fill[0]
    )

    if owner_count != 4 or tp_count != 2:
        mine = lax.all_gather(quarter, "seq", axis=1, tiled=True)
        across = swap_group(mine)
        pieces = [mine, across, swap_role(mine), swap_role(across)]
        keys, values = place(position, pages, fresh)
        partial = [
            project(control, attend(side, control, tables, queries[0], keys, values, slots), pieces)
            for side in (0, 1)
        ]
        return lax.psum_scatter(
            jnp.concatenate(partial, axis=0), "tp", scatter_dimension=0, tiled=True
        )[None]

    swap_tp = functools.partial(lax.ppermute, axis_name="tp", perm=SWAP)
    forward = functools.partial(lax.ppermute, axis_name="seq", perm=[(1, 0), (2, 3)])
    cross = functools.partial(lax.ppermute, axis_name="seq", perm=[(1, 2), (2, 1)])
    cut = columns // 2

    def four(one, two, *hold):
        return [one, two, swap_role(after(one, *hold)), swap_role(after(two, *hold))]

    near_across = swap_group(near)
    far_a = cross(near[:, :cut])
    next_shard = jnp.where(middle, inner, forward(inner))
    next_across = swap_group(next_shard)
    far_a = jnp.where(middle, far_a, forward(far_a))
    far_a_across = swap_group(far_a)
    near_all = four(near, near_across)
    next_all = four(next_shard, next_across)
    far_a_all = four(far_a, far_a_across)

    far_b = cross(after(near[:, cut:], pages))
    keys, values = place(position, after(pages, near_across, next_shard, far_a), fresh)
    left = attend(1, control, tables, queries[0], keys, values, slots)
    far_b_on = forward(after(far_b, left))
    sent = [project(control, left, [out_weight])]
    for pieces in (near_all, next_all, far_a_all):
        sent.append(project(control, after(left, sent[-1]), pieces))
    came = [swap_tp(part) for part in sent]
    far_b = jnp.where(middle, far_b, after(far_b_on, sent[2]))
    far_b_across = swap_group(far_b)
    stay = attend(0, control, tables, after(queries[0], sent[3], far_b), keys, values, slots)
    far_b_all = four(far_b, far_b_across, stay)
    total = columns * owner_count
    out = project(control, stay, [out_weight], came[0], 10, None, total)
    out = project(control, stay, near_all, came[1], 11, out, total)
    last = project(control, after(left, out), far_b_all)
    stay = after(stay, last)
    last = swap_tp(last)
    out = project(control, stay, next_all, came[2], 12, out, total)
    out = project(control, stay, far_a_all, came[3], 13, out, total)
    return project(control, stay, far_b_all, last, 14, out, total)


def solution(mesh):
    return jax.shard_map(
        shards,
        mesh=mesh,
        in_specs=(
            P("role", ("group", "seq"), "tp"),
            P("role", ("group", "seq"), None, "tp"),
            P("role", ("group", "seq"), None, None, "tp"),
            P("tp", "seq"),
            P("role", ("group", "seq")),
            P("role", ("group", "seq")),
            P("role", ("group", "seq")),
            P("role", ("group", "seq")),
            P("role", ("group", "seq")),
        ),
        out_specs=P("role", ("group", "seq", "tp"), None),
        check_vma=False,
    )
```

```python
import functools
import math

import jax
import jax.numpy as jnp
from jax import lax
from jax.experimental import pallas as pl
from jax.experimental.pallas import tpu as pltpu
from jax.sharding import PartitionSpec as P

HD = 128
TILE = 64
KEYS = 256
LANES = 128
HIDDEN = -1e30
COLUMNS = 256
MIB = 1024 * 1024


def cost(flops=3 * 10**9):
    return pl.CostEstimate(flops=flops, bytes_accessed=1000, transcendentals=0)


def rank_kernel(owner, page, position, wanted, count):
    owners, bucket = wanted.shape
    for n in range(owners):
        count[n] = 0

    def clear(k, carry):
        for n in range(owners):
            wanted[n, k] = 0
        return carry

    lax.fori_loop(0, bucket, clear, 0)

    def put(slot, carry):
        to = owner[0, slot]
        rank = count[to]
        count[to] = rank + 1
        wanted[to, rank] = page[0, slot]
        position[slot] = to * bucket + rank
        return carry

    lax.fori_loop(0, owner.shape[1], put, 0, unroll=4)


def rank(page_owner, page_index, owners, bucket):
    smem = pl.BlockSpec(memory_space=pltpu.SMEM)
    return pl.pallas_call(
        rank_kernel,
        out_shape=(
            jax.ShapeDtypeStruct((page_owner.shape[1],), jnp.int32),
            jax.ShapeDtypeStruct((owners, bucket), jnp.int32),
        ),
        in_specs=[smem, smem],
        out_specs=(smem, smem),
        scratch_shapes=[pltpu.SMEM((owners,), jnp.int32)],
        cost_estimate=cost(),
        name="rank",
    )(page_owner, page_index)


def place_kernel(position, pages, fresh, keys, values):
    kv_local, key_total = keys.shape[:2]
    slots, page_len, rows = position.shape[0], pages.shape[2], fresh.shape[0]
    channels = kv_local * HD
    hist = slots * page_len
    fresh_base = hist + KEYS
    for head in range(kv_local):
        values[head, :, HD:] = jnp.ones((key_total, HD), jnp.bfloat16)
        for first, last in ((hist, fresh_base), (fresh_base + rows, key_total)):
            keys[head, first:last] = jnp.zeros((last - first, HD), jnp.bfloat16)
            values[head, first:last, :HD] = jnp.zeros((last - first, HD), jnp.bfloat16)
        at = head * HD
        keys[head, fresh_base : fresh_base + rows] = fresh[:, at : at + HD]
        values[head, fresh_base : fresh_base + rows, :HD] = fresh[:, channels + at : channels + at + HD]

    def place(slot, carry):
        page = position[slot]
        row = pl.ds(pl.multiple_of(slot * page_len, page_len), page_len)
        for head in range(kv_local):
            at = head * HD
            keys[head, row] = pages[page, 0, :, at : at + HD]
            values[head, row, :HD] = pages[page, 1, :, at : at + HD]
        return carry

    lax.fori_loop(0, slots, place, 0, unroll=8)


def place(position, pages, fresh):
    kv_local = pages.shape[3] // HD
    rows = fresh.shape[0]
    key_total = position.shape[0] * pages.shape[2] + KEYS + pl.cdiv(rows, KEYS) * KEYS + KEYS
    vmem = pl.BlockSpec(memory_space=pltpu.VMEM)
    return pl.pallas_call(
        place_kernel,
        out_shape=(
            jax.ShapeDtypeStruct((kv_local, key_total, HD), jnp.bfloat16),
            jax.ShapeDtypeStruct((kv_local, key_total, 2 * HD), jnp.bfloat16),
        ),
        in_specs=[pl.BlockSpec(memory_space=pltpu.SMEM), vmem, vmem],
        out_specs=(vmem, vmem),
        compiler_params=pltpu.CompilerParams(vmem_limit_bytes=20 * MIB),
        cost_estimate=cost(),
        name="place",
    )(position, pages, fresh)


def attend_kernel(
    fresh_base, side, control, hist_at, hist_steps, fresh_at, fresh_steps,
    query, keys, values, key_conv, key_row, tok_conv, out, scores, sums,
):
    kv_local = keys.shape[0]
    group_size = query.shape[1] // (kv_local * HD)
    half, depth = out.shape[1], out.shape[2]
    tiles = half // TILE
    to_exp2 = math.log2(math.e) / math.sqrt(HD)
    wide = group_size * TILE

    def tile(number_here, carry):
        index = control[side] * tiles + number_here
        first = pl.multiple_of(index * TILE, TILE)
        leaving = pl.ds(pl.multiple_of(number_here * TILE, TILE), TILE)
        tokens = pl.ds(first, TILE)
        conv = tok_conv[tokens]
        number = first + lax.broadcasted_iota(jnp.int32, (TILE, 1), 0)
        steps_h, steps_f = hist_steps[index], fresh_steps[index]
        at_h, at_f = hist_at[index], fresh_at[index]
        heads = [
            jnp.concatenate(
                [
                    query[tokens, (head * group_size + g) * HD : (head * group_size + g + 1) * HD]
                    for g in range(group_size)
                ],
                axis=0,
            )
            for head in range(kv_local)
        ]

        def key_range(step):
            start = jnp.where(
                step < steps_h, at_h + step * KEYS, fresh_base + at_f + (step - steps_h) * KEYS
            )
            return pl.ds(pl.multiple_of(start, LANES), KEYS)

        def score(step, tops):
            where = key_range(step)
            ok = (key_conv[:, where] == conv) & (key_row[:, where] <= number)
            held = pl.ds(pl.multiple_of(step * KEYS, KEYS), KEYS)
            new = []
            for head in range(kv_local):
                s = lax.dot_general(
                    heads[head], keys[head, where], (((1,), (1,)), ((), ())),
                    preferred_element_type=jnp.float32,
                ).reshape(group_size, TILE, KEYS)
                s = jnp.where(ok[None], s, HIDDEN).reshape(wide, KEYS)
                scores[head, :, held] = s
                top = tops[head]
                for k in range(0, KEYS, LANES):
                    top = jnp.maximum(top, s[:, k : k + LANES])
                new.append(top)
            return tuple(new)

        low = jnp.full((wide, LANES), HIDDEN, jnp.float32)
        tops = lax.fori_loop(0, steps_h + steps_f, score, (low,) * kv_local)
        tops = [jnp.max(top, axis=1, keepdims=True) * to_exp2 for top in tops]
        sums[...] = jnp.zeros_like(sums)

        def gather(step, carry):
            where = key_range(step)
            held = pl.ds(pl.multiple_of(step * KEYS, KEYS), KEYS)
            for head in range(kv_local):
                w = jnp.exp2(scores[head, :, held] * to_exp2 - tops[head]).astype(jnp.bfloat16)
                sums[head] += jnp.dot(w, values[head, where], preferred_element_type=jnp.float32)
            return carry

        lax.fori_loop(0, steps_h + steps_f, gather, 0)
        for head in range(kv_local):
            done = (sums[head, :, :HD] / sums[head, :, HD:]).astype(jnp.bfloat16)
            for g in range(group_size):
                at = (head * group_size + g) * HD
                out[control[2 + at // depth], leaving, at % depth : at % depth + HD] = done[
                    g * TILE : (g + 1) * TILE
                ]
        return carry

    lax.fori_loop(0, tiles, tile, 0)


def attend_tables(rows, slots, page_len, tok_conv, page_conv, page_fill):
    hist = slots * page_len
    fresh_base = hist + KEYS
    key_total = fresh_base + pl.cdiv(rows, KEYS) * KEYS + KEYS
    live = jnp.arange(page_len)[None, :] < page_fill[:, None]
    hist_conv = jnp.where(live, page_conv[:, None], -1).reshape(hist)
    tail = key_total - fresh_base - rows
    key_conv = jnp.concatenate(
        [hist_conv, jnp.full((KEYS,), -1, jnp.int32), tok_conv, jnp.full((tail,), -1, jnp.int32)]
    )[None]
    key_row = jnp.maximum(jnp.arange(key_total, dtype=jnp.int32) - fresh_base, -1)[None]
    lowest, highest = tok_conv[::TILE], tok_conv[TILE - 1 :: TILE]
    hist_at = jnp.sum(page_conv[None] < lowest[:, None], axis=1, dtype=jnp.int32) * page_len
    hist_at = hist_at // LANES * LANES
    hist_end = jnp.sum(page_conv[None] <= highest[:, None], axis=1, dtype=jnp.int32) * page_len
    hist_steps = (hist_end - hist_at + KEYS - 1) // KEYS
    fresh_at = jnp.sum(tok_conv[None] < lowest[:, None], axis=1, dtype=jnp.int32) // LANES * LANES
    fresh_end = (jnp.arange(rows // TILE, dtype=jnp.int32) + 1) * TILE
    fresh_steps = (fresh_end - fresh_at + KEYS - 1) // KEYS
    return key_conv, key_row, tok_conv[:, None], hist_at, hist_steps, fresh_at, fresh_steps


def attend(side, control, tables, queries, keys, values, slots):
    rows, width = queries.shape
    kv_local, key_total = keys.shape[:2]
    group_size = width // (kv_local * HD)
    key_conv, key_row, tok_conv, *steps = tables
    fresh_base = slots + KEYS
    most = slots // KEYS + pl.cdiv(rows, KEYS) + 2
    smem = pl.BlockSpec(memory_space=pltpu.SMEM)
    vmem = pl.BlockSpec(memory_space=pltpu.VMEM)
    return pl.pallas_call(
        functools.partial(attend_kernel, fresh_base, side),
        out_shape=jax.ShapeDtypeStruct((4, rows // 2, width // 4), jnp.bfloat16),
        in_specs=[smem] * 5 + [vmem] * 6,
        out_specs=vmem,
        scratch_shapes=[
            pltpu.VMEM((kv_local, group_size * TILE, most * KEYS), jnp.float32),
            pltpu.VMEM((kv_local, group_size * TILE, 2 * HD), jnp.float32),
        ],
        compiler_params=pltpu.CompilerParams(vmem_limit_bytes=28 * MIB),
        cost_estimate=cost(16 * 10**9),
        name="attend",
    )(control, *steps, queries, keys, values, key_conv, key_row, tok_conv)


def multiply(left, pieces, at):
    total = None
    for n, piece in enumerate(pieces):
        term = jnp.dot(left[n], piece[:, at], preferred_element_type=jnp.float32)
        total = term if total is None else total + term
    return total.astype(jnp.bfloat16)


def blocks(columns):
    cut = min(COLUMNS, columns)
    return [slice(k, k + cut) for k in range(0, columns, cut)]


def quarters(control, refs):
    if len(refs) == 4:
        return refs
    depth = refs[0].shape[0] // 4
    return [refs[0].at[pl.ds(pl.multiple_of(control[6 + n] * depth, depth), depth)] for n in range(4)]


def project_kernel(control, left, *refs):
    pieces = quarters(control, refs[:-1])
    for at in blocks(pieces[0].shape[1]):
        refs[-1][:, at] = multiply(left, pieces, at)


def finish_kernel(has_out, control, left, came, *refs):
    pieces = quarters(control, refs[: len(refs) - 1 - has_out])
    for at in blocks(pieces[0].shape[1]):
        total = multiply(left, pieces, at).astype(jnp.float32) + came[:, at].astype(jnp.float32)
        refs[-1][0, :, at] = total.astype(jnp.bfloat16)


def project(control, left, pieces, came=None, base=None, out=None, width=None):
    half = left.shape[1]
    columns = pieces[0].shape[1]
    vmem = pl.BlockSpec(memory_space=pltpu.VMEM)
    in_specs = [vmem]
    operands = [left]
    aliases = {}
    if came is None:
        kernel = project_kernel
        out_shape = jax.ShapeDtypeStruct((half, columns), jnp.bfloat16)
        out_specs = vmem
    else:
        kernel = functools.partial(finish_kernel, int(out is not None))
        in_specs.append(vmem)
        operands.append(came)
        out_shape = jax.ShapeDtypeStruct((1, half, width), jnp.bfloat16)
        out_specs = pl.BlockSpec((1, half, columns), lambda j, control: (0, 0, control[base]))
    in_specs += [vmem] * len(pieces)
    operands += pieces
    if out is not None:
        in_specs.append(pl.BlockSpec(memory_space=pl.ANY))
        operands.append(out)
        aliases = {len(operands): 0}
    return pl.pallas_call(
        kernel,
        out_shape=out_shape,
        grid_spec=pltpu.PrefetchScalarGridSpec(
            num_scalar_prefetch=1, grid=(1,), in_specs=in_specs, out_specs=out_specs
        ),
        input_output_aliases=aliases,
        compiler_params=pltpu.CompilerParams(vmem_limit_bytes=16 * MIB),
        cost_estimate=cost(),
        name="project" if came is None else "finish",
    )(control, *operands)


def pick_kernel(asked, pool, out):
    for owner in range(asked.shape[0]):

        def copy(n, carry):
            out[owner, n] = pool[asked[owner, n]]
            return carry

        lax.fori_loop(0, asked.shape[1], copy, 0, unroll=8)


def pick(pool, asked):
    vmem = pl.BlockSpec(memory_space=pltpu.VMEM)
    return pl.pallas_call(
        pick_kernel,
        out_shape=jax.ShapeDtypeStruct(asked.shape + pool.shape[1:], jnp.bfloat16),
        in_specs=[pl.BlockSpec(memory_space=pltpu.SMEM), vmem],
        out_specs=vmem,
        compiler_params=pltpu.CompilerParams(vmem_limit_bytes=16 * MIB),
        cost_estimate=cost(),
        name="pick",
    )(asked, pool)


SWAP = [(0, 1), (1, 0)]


def after(value, *others):
    return lax.optimization_barrier((value,) + others)[0]


def shards(
    queries, new_kv, pool, out_weight, tok_conv, page_conv, page_fill, page_owner, page_index
):
    row_count = queries.shape[1]
    slot_count = page_owner.shape[1]
    owner_count = lax.axis_size("seq")
    tp_count = lax.axis_size("tp")
    bucket = 2 * slot_count // owner_count
    group, role, tp = lax.axis_index("group"), lax.axis_index("role"), lax.axis_index("tp")
    seq = lax.axis_index("seq")


    own = 2 * group + role
    depth = out_weight.shape[0] // 4
    columns = out_weight.shape[1]
    quarter = lax.dynamic_slice_in_dim(out_weight, own * depth, depth, 0)
    order = [q ^ own for q in range(4)]
    order = [(v % 2) * 2 + v // 2 for v in order]
    flip = tp if tp_count == 2 else 0
    second = jnp.where(seq < 2, 2, 1)
    third = jnp.where(seq < 2, 3, 0)
    local = [own, own ^ 2, own ^ 1, own ^ 3]
    halves = [2 * shard + h for shard in (seq ^ 1, second, third) for h in (0, 1)]
    control = jnp.stack(
        [jnp.asarray(v, jnp.int32) for v in (flip, 1 - flip, *order, *local, seq, *halves)]
    )
    swap_group = functools.partial(lax.ppermute, axis_name="group", perm=SWAP)
    swap_role = functools.partial(lax.ppermute, axis_name="role", perm=SWAP)

    if owner_count == 4:
        middle = (seq == 1) | (seq == 2)
        cut = columns // 2
        parts = [quarter[:, :cut], quarter[:, cut:]]
        pair = functools.partial(lax.ppermute, axis_name="seq", perm=[(0, 1), (1, 0), (2, 3), (3, 2)])
        cross = functools.partial(lax.ppermute, axis_name="seq", perm=[(1, 2), (2, 1)])
        forward = functools.partial(lax.ppermute, axis_name="seq", perm=[(1, 0), (2, 3)])
        near, inner = [pair(parts[0])], [cross(parts[0])]

    position, wanted = rank(page_owner, page_index, owner_count, bucket)
    asked = lax.all_to_all(wanted, "seq", split_axis=0, concat_axis=0, tiled=True)
    if owner_count == 4:
        near, inner = [after(near[0], asked)], [after(inner[0], asked)]
        asked = after(asked, near[0], inner[0])
    found = pick(pool[0], asked)
    pages = lax.all_to_all(found, "seq", split_axis=0, concat_axis=0, tiled=True)
    pages = pages.reshape((owner_count * bucket,) + found.shape[2:])
    slots = slot_count * pool.shape[3]
    fresh = new_kv[0].reshape(row_count, -1)
    tables = attend_tables(
        row_count, slot_count, pool.shape[3], tok_conv[0], page_conv[0], page_fill[0]
    )

    if owner_count != 4 or tp_count != 2:
        mine = lax.all_gather(quarter, "seq", axis=1, tiled=True)
        across = swap_group(mine)
        pieces = [mine, across, swap_role(mine), swap_role(across)]
        keys, values = place(position, pages, fresh)
        partial = [
            project(control, attend(side, control, tables, queries[0], keys, values, slots), pieces)
            for side in (0, 1)
        ]
        return lax.psum_scatter(
            jnp.concatenate(partial, axis=0), "tp", scatter_dimension=0, tiled=True
        )[None]

    swap_tp = functools.partial(lax.ppermute, axis_name="tp", perm=SWAP)

    def four(one, two, *hold):
        return [one, two, swap_role(after(one, *hold)), swap_role(after(two, *hold))]

    part = after(parts[1], found)
    near.append(pair(part))
    inner.append(cross(part))
    near_across = [swap_group(near[0])]
    far = [cross(near[0])]
    next_shard = [jnp.where(middle, inner[0], forward(inner[0]))]
    next_across = [swap_group(next_shard[0])]
    far_on = forward(far[0])
    near_across.append(swap_group(near[1]))
    next_shard.append(jnp.where(middle, inner[1], forward(inner[1])))
    next_across.append(swap_group(next_shard[1]))
    far.append(cross(near[1]))

    keys, values = place(position, after(pages, next_shard[0], next_shard[1], far[0]), fresh)
    left = attend(1, control, tables, queries[0], keys, values, slots)
    far[0] = jnp.where(middle, far[0], far_on)
    far_across = [swap_group(far[0])]
    sent = [project(control, left, [out_weight])]
    far_on = forward(after(far[1], left))
    weights = []
    for n in range(4):
        one, two = ((near, near_across), (next_shard, next_across))[n // 2]
        weights.append(four(one[n % 2], two[n % 2], *[keys] * (n % 2)))
        sent.append(project(control, after(left, sent[-1]), weights[-1]))
    weights.append(four(far[0], far_across[0], sent[2]))
    sent.append(project(control, after(left, sent[-1]), weights[-1]))
    came = [swap_tp(each) for each in sent]
    far[1] = jnp.where(middle, far[1], after(far_on, sent[4]))
    far_across.append(swap_group(far[1]))
    stay = attend(0, control, tables, after(queries[0], sent[5], far[1]), keys, values, slots)
    weights.append(four(far[1], far_across[1], stay))
    total = columns * owner_count
    out = project(control, stay, [out_weight], came[0], 10, None, total)
    for n in range(2):
        out = project(control, stay, weights[n], came[n + 1], 11 + n, out, total)
    last = project(control, after(left, out), weights[5])
    stay = after(stay, last)
    came.append(swap_tp(last))
    for n in range(2, 6):
        out = project(control, stay, weights[n], came[n + 1], 11 + n, out, total)
    return out


def solution(mesh):
    return jax.shard_map(
        shards,
        mesh=mesh,
        in_specs=(
            P("role", ("group", "seq"), "tp"),
            P("role", ("group", "seq"), None, "tp"),
            P("role", ("group", "seq"), None, None, "tp"),
            P("tp", "seq"),
            P("role", ("group", "seq")),
            P("role", ("group", "seq")),
            P("role", ("group", "seq")),
            P("role", ("group", "seq")),
            P("role", ("group", "seq")),
        ),
        out_specs=P("role", ("group", "seq", "tp"), None),
        check_vma=False,
    )
```

```python
import functools
import math

import jax
import jax.numpy as jnp
from jax import lax
from jax.experimental import pallas as pl
from jax.experimental.pallas import tpu as pltpu
from jax.sharding import PartitionSpec as P

HD = 128
TILE = 64
KEYS = 256
LANES = 128
HIDDEN = -1e30
COLUMNS = 256
MIB = 1024 * 1024


def cost(flops=3 * 10**9):
    return pl.CostEstimate(flops=flops, bytes_accessed=1000, transcendentals=0)


def rank_kernel(owner, page, position, wanted, count):
    owners, bucket = wanted.shape
    for n in range(owners):
        count[n] = 0

    def clear(k, carry):
        for n in range(owners):
            wanted[n, k] = 0
        return carry

    lax.fori_loop(0, bucket, clear, 0)

    def put(slot, carry):
        to = owner[0, slot]
        rank = count[to]
        count[to] = rank + 1
        wanted[to, rank] = page[0, slot]
        position[slot] = to * bucket + rank
        return carry

    lax.fori_loop(0, owner.shape[1], put, 0, unroll=4)


def rank(page_owner, page_index, owners, bucket):
    smem = pl.BlockSpec(memory_space=pltpu.SMEM)
    return pl.pallas_call(
        rank_kernel,
        out_shape=(
            jax.ShapeDtypeStruct((page_owner.shape[1],), jnp.int32),
            jax.ShapeDtypeStruct((owners, bucket), jnp.int32),
        ),
        in_specs=[smem, smem],
        out_specs=(smem, smem),
        scratch_shapes=[pltpu.SMEM((owners,), jnp.int32)],
        cost_estimate=cost(),
        name="rank",
    )(page_owner, page_index)


def place_kernel(position, pages, fresh, keys, values):
    kv_local, key_total = keys.shape[:2]
    slots, page_len, rows = position.shape[0], pages.shape[2], fresh.shape[0]
    channels = kv_local * HD
    hist = slots * page_len
    fresh_base = hist + KEYS
    for head in range(kv_local):
        values[head, :, HD:] = jnp.ones((key_total, HD), jnp.bfloat16)
        for first, last in ((hist, fresh_base), (fresh_base + rows, key_total)):
            keys[head, first:last] = jnp.zeros((last - first, HD), jnp.bfloat16)
            values[head, first:last, :HD] = jnp.zeros((last - first, HD), jnp.bfloat16)
        at = head * HD
        keys[head, fresh_base : fresh_base + rows] = fresh[:, at : at + HD]
        values[head, fresh_base : fresh_base + rows, :HD] = fresh[:, channels + at : channels + at + HD]

    def place(slot, carry):
        page = position[slot]
        row = pl.ds(pl.multiple_of(slot * page_len, page_len), page_len)
        for head in range(kv_local):
            at = head * HD
            keys[head, row] = pages[page, 0, :, at : at + HD]
            values[head, row, :HD] = pages[page, 1, :, at : at + HD]
        return carry

    lax.fori_loop(0, slots, place, 0, unroll=8)


def place(position, pages, fresh):
    kv_local = pages.shape[3] // HD
    rows = fresh.shape[0]
    key_total = position.shape[0] * pages.shape[2] + KEYS + pl.cdiv(rows, KEYS) * KEYS + KEYS
    vmem = pl.BlockSpec(memory_space=pltpu.VMEM)
    return pl.pallas_call(
        place_kernel,
        out_shape=(
            jax.ShapeDtypeStruct((kv_local, key_total, HD), jnp.bfloat16),
            jax.ShapeDtypeStruct((kv_local, key_total, 2 * HD), jnp.bfloat16),
        ),
        in_specs=[pl.BlockSpec(memory_space=pltpu.SMEM), vmem, vmem],
        out_specs=(vmem, vmem),
        compiler_params=pltpu.CompilerParams(vmem_limit_bytes=20 * MIB),
        cost_estimate=cost(),
        name="place",
    )(position, pages, fresh)


def attend_kernel(
    fresh_base, side, control, hist_at, hist_steps, fresh_at, fresh_steps,
    query, keys, values, key_conv, key_row, tok_conv, out, scores, sums,
):
    kv_local = keys.shape[0]
    group_size = query.shape[1] // (kv_local * HD)
    half, depth = out.shape[1], out.shape[2]
    tiles = half // TILE
    to_exp2 = math.log2(math.e) / math.sqrt(HD)
    wide = group_size * TILE

    def tile(number_here, carry):
        index = control[side] * tiles + number_here
        first = pl.multiple_of(index * TILE, TILE)
        leaving = pl.ds(pl.multiple_of(number_here * TILE, TILE), TILE)
        tokens = pl.ds(first, TILE)
        conv = tok_conv[tokens]
        number = first + lax.broadcasted_iota(jnp.int32, (TILE, 1), 0)
        steps_h, steps_f = hist_steps[index], fresh_steps[index]
        at_h, at_f = hist_at[index], fresh_at[index]
        heads = [
            jnp.concatenate(
                [
                    query[tokens, (head * group_size + g) * HD : (head * group_size + g + 1) * HD]
                    for g in range(group_size)
                ],
                axis=0,
            )
            for head in range(kv_local)
        ]

        def key_range(step):
            start = jnp.where(
                step < steps_h, at_h + step * KEYS, fresh_base + at_f + (step - steps_h) * KEYS
            )
            return pl.ds(pl.multiple_of(start, LANES), KEYS)

        def score(step, tops):
            where = key_range(step)
            ok = (key_conv[:, where] == conv) & (key_row[:, where] <= number)
            held = pl.ds(pl.multiple_of(step * KEYS, KEYS), KEYS)
            new = []
            for head in range(kv_local):
                s = lax.dot_general(
                    heads[head], keys[head, where], (((1,), (1,)), ((), ())),
                    preferred_element_type=jnp.float32,
                ).reshape(group_size, TILE, KEYS)
                s = jnp.where(ok[None], s, HIDDEN).reshape(wide, KEYS)
                scores[head, :, held] = s
                top = tops[head]
                for k in range(0, KEYS, LANES):
                    top = jnp.maximum(top, s[:, k : k + LANES])
                new.append(top)
            return tuple(new)

        low = jnp.full((wide, LANES), HIDDEN, jnp.float32)
        tops = lax.fori_loop(0, steps_h + steps_f, score, (low,) * kv_local)
        tops = [jnp.max(top, axis=1, keepdims=True) * to_exp2 for top in tops]
        sums[...] = jnp.zeros_like(sums)

        def gather(step, carry):
            where = key_range(step)
            held = pl.ds(pl.multiple_of(step * KEYS, KEYS), KEYS)
            for head in range(kv_local):
                w = jnp.exp2(scores[head, :, held] * to_exp2 - tops[head]).astype(jnp.bfloat16)
                sums[head] += jnp.dot(w, values[head, where], preferred_element_type=jnp.float32)
            return carry

        lax.fori_loop(0, steps_h + steps_f, gather, 0)
        for head in range(kv_local):
            done = (sums[head, :, :HD] / sums[head, :, HD:]).astype(jnp.bfloat16)
            for g in range(group_size):
                at = (head * group_size + g) * HD
                out[control[2 + at // depth], leaving, at % depth : at % depth + HD] = done[
                    g * TILE : (g + 1) * TILE
                ]
        return carry

    lax.fori_loop(0, tiles, tile, 0)


def attend_tables(rows, slots, page_len, tok_conv, page_conv, page_fill):
    hist = slots * page_len
    fresh_base = hist + KEYS
    key_total = fresh_base + pl.cdiv(rows, KEYS) * KEYS + KEYS
    live = jnp.arange(page_len)[None, :] < page_fill[:, None]
    hist_conv = jnp.where(live, page_conv[:, None], -1).reshape(hist)
    tail = key_total - fresh_base - rows
    key_conv = jnp.concatenate(
        [hist_conv, jnp.full((KEYS,), -1, jnp.int32), tok_conv, jnp.full((tail,), -1, jnp.int32)]
    )[None]
    key_row = jnp.maximum(jnp.arange(key_total, dtype=jnp.int32) - fresh_base, -1)[None]
    lowest, highest = tok_conv[::TILE], tok_conv[TILE - 1 :: TILE]
    hist_at = jnp.sum(page_conv[None] < lowest[:, None], axis=1, dtype=jnp.int32) * page_len
    hist_at = hist_at // LANES * LANES
    hist_end = jnp.sum(page_conv[None] <= highest[:, None], axis=1, dtype=jnp.int32) * page_len
    hist_steps = (hist_end - hist_at + KEYS - 1) // KEYS
    fresh_at = jnp.sum(tok_conv[None] < lowest[:, None], axis=1, dtype=jnp.int32) // LANES * LANES
    fresh_end = (jnp.arange(rows // TILE, dtype=jnp.int32) + 1) * TILE
    fresh_steps = (fresh_end - fresh_at + KEYS - 1) // KEYS
    return key_conv, key_row, tok_conv[:, None], hist_at, hist_steps, fresh_at, fresh_steps


def attend(side, control, tables, queries, keys, values, slots):
    rows, width = queries.shape
    kv_local, key_total = keys.shape[:2]
    group_size = width // (kv_local * HD)
    key_conv, key_row, tok_conv, *steps = tables
    fresh_base = slots + KEYS
    most = slots // KEYS + pl.cdiv(rows, KEYS) + 2
    smem = pl.BlockSpec(memory_space=pltpu.SMEM)
    vmem = pl.BlockSpec(memory_space=pltpu.VMEM)
    return pl.pallas_call(
        functools.partial(attend_kernel, fresh_base, side),
        out_shape=jax.ShapeDtypeStruct((4, rows // 2, width // 4), jnp.bfloat16),
        in_specs=[smem] * 5 + [vmem] * 6,
        out_specs=vmem,
        scratch_shapes=[
            pltpu.VMEM((kv_local, group_size * TILE, most * KEYS), jnp.float32),
            pltpu.VMEM((kv_local, group_size * TILE, 2 * HD), jnp.float32),
        ],
        compiler_params=pltpu.CompilerParams(vmem_limit_bytes=28 * MIB),
        cost_estimate=cost(16 * 10**9),
        name="attend",
    )(control, *steps, queries, keys, values, key_conv, key_row, tok_conv)


def multiply(left, pieces, at):
    total = None
    for n, piece in enumerate(pieces):
        term = jnp.dot(left[n], piece[:, at], preferred_element_type=jnp.float32)
        total = term if total is None else total + term
    return total.astype(jnp.bfloat16)


def blocks(columns):
    cut = min(COLUMNS, columns)
    return [slice(k, k + cut) for k in range(0, columns, cut)]


def parts_of(control, refs):
    if len(refs) == 1:
        depth = refs[0].shape[0] // 4
        return [
            (0, [refs[0].at[pl.ds(pl.multiple_of(control[6 + n] * depth, depth), depth)] for n in range(4)])
        ]
    columns = refs[0].shape[1]
    return [(k // 4 * columns, refs[k : k + 4]) for k in range(0, len(refs), 4)]


def project_kernel(control, left, *refs):
    for first, pieces in parts_of(control, refs[:-1]):
        for at in blocks(pieces[0].shape[1]):
            refs[-1][:, first + at.start : first + at.stop] = multiply(left, pieces, at)


def finish_kernel(has_out, control, left, came, *refs):
    for first, pieces in parts_of(control, refs[: len(refs) - 1 - has_out]):
        for at in blocks(pieces[0].shape[1]):
            to = slice(first + at.start, first + at.stop)
            total = multiply(left, pieces, at).astype(jnp.float32) + came[:, to].astype(jnp.float32)
            refs[-1][0, :, to] = total.astype(jnp.bfloat16)


def project(control, left, pieces, came=None, base=None, out=None, width=None):
    half = left.shape[1]
    columns = pieces[0].shape[1] * max(1, len(pieces) // 4)
    vmem = pl.BlockSpec(memory_space=pltpu.VMEM)
    in_specs = [vmem]
    operands = [left]
    aliases = {}
    if came is None:
        kernel = project_kernel
        out_shape = jax.ShapeDtypeStruct((half, columns), jnp.bfloat16)
        out_specs = vmem
    else:
        kernel = functools.partial(finish_kernel, int(out is not None))
        in_specs.append(vmem)
        operands.append(came)
        out_shape = jax.ShapeDtypeStruct((1, half, width), jnp.bfloat16)
        out_specs = pl.BlockSpec((1, half, columns), lambda j, control: (0, 0, control[base]))
    in_specs += [vmem] * len(pieces)
    operands += pieces
    if out is not None:
        in_specs.append(pl.BlockSpec(memory_space=pl.ANY))
        operands.append(out)
        aliases = {len(operands): 0}
    return pl.pallas_call(
        kernel,
        out_shape=out_shape,
        grid_spec=pltpu.PrefetchScalarGridSpec(
            num_scalar_prefetch=1, grid=(1,), in_specs=in_specs, out_specs=out_specs
        ),
        input_output_aliases=aliases,
        compiler_params=pltpu.CompilerParams(vmem_limit_bytes=16 * MIB),
        cost_estimate=cost(),
        name="project" if came is None else "finish",
    )(control, *operands)


def pick_kernel(asked, pool, out):
    for owner in range(asked.shape[0]):

        def copy(n, carry):
            out[owner, n] = pool[asked[owner, n]]
            return carry

        lax.fori_loop(0, asked.shape[1], copy, 0, unroll=8)


def pick(pool, asked):
    vmem = pl.BlockSpec(memory_space=pltpu.VMEM)
    return pl.pallas_call(
        pick_kernel,
        out_shape=jax.ShapeDtypeStruct(asked.shape + pool.shape[1:], jnp.bfloat16),
        in_specs=[pl.BlockSpec(memory_space=pltpu.SMEM), vmem],
        out_specs=vmem,
        compiler_params=pltpu.CompilerParams(vmem_limit_bytes=16 * MIB),
        cost_estimate=cost(),
        name="pick",
    )(asked, pool)


SWAP = [(0, 1), (1, 0)]


def after(value, *others):
    return lax.optimization_barrier((value,) + others)[0]


def shards(
    queries, new_kv, pool, out_weight, tok_conv, page_conv, page_fill, page_owner, page_index
):
    row_count = queries.shape[1]
    slot_count = page_owner.shape[1]
    owner_count = lax.axis_size("seq")
    tp_count = lax.axis_size("tp")
    bucket = 2 * slot_count // owner_count
    group, role, tp = lax.axis_index("group"), lax.axis_index("role"), lax.axis_index("tp")
    seq = lax.axis_index("seq")


    own = 2 * group + role
    depth = out_weight.shape[0] // 4
    columns = out_weight.shape[1]
    quarter = lax.dynamic_slice_in_dim(out_weight, own * depth, depth, 0)
    order = [q ^ own for q in range(4)]
    order = [(v % 2) * 2 + v // 2 for v in order]
    flip = tp if tp_count == 2 else 0
    second = jnp.where(seq < 2, 2, 1)
    third = jnp.where(seq < 2, 3, 0)
    local = [own, own ^ 2, own ^ 1, own ^ 3]
    control = jnp.stack(
        [jnp.asarray(v, jnp.int32) for v in (flip, 1 - flip, *order, *local, seq, seq ^ 1, second, 2 * third, 2 * third + 1)]
    )
    swap_group = functools.partial(lax.ppermute, axis_name="group", perm=SWAP)
    swap_role = functools.partial(lax.ppermute, axis_name="role", perm=SWAP)

    if owner_count == 4:
        middle = (seq == 1) | (seq == 2)
        cut = columns // 2
        parts = [quarter[:, :cut], quarter[:, cut:]]
        pair = functools.partial(lax.ppermute, axis_name="seq", perm=[(0, 1), (1, 0), (2, 3), (3, 2)])
        cross = functools.partial(lax.ppermute, axis_name="seq", perm=[(1, 2), (2, 1)])
        forward = functools.partial(lax.ppermute, axis_name="seq", perm=[(1, 0), (2, 3)])
        near, inner = [pair(parts[0])], [cross(parts[0])]

    position, wanted = rank(page_owner, page_index, owner_count, bucket)
    asked = lax.all_to_all(wanted, "seq", split_axis=0, concat_axis=0, tiled=True)
    if owner_count == 4:
        near, inner = [after(near[0], asked)], [after(inner[0], asked)]
        later = after(parts[1], near[0], inner[0])
        near.append(pair(later))
        inner.append(cross(later))
        asked = after(asked, near[0], inner[0])
    found = pick(pool[0], asked)
    if owner_count == 4:
        near[1], inner[1] = after(near[1], found), after(inner[1], found)
        found = after(found, near[1], inner[1])
    pages = lax.all_to_all(found, "seq", split_axis=0, concat_axis=0, tiled=True)
    pages = pages.reshape((owner_count * bucket,) + found.shape[2:])
    slots = slot_count * pool.shape[3]
    fresh = new_kv[0].reshape(row_count, -1)
    tables = attend_tables(
        row_count, slot_count, pool.shape[3], tok_conv[0], page_conv[0], page_fill[0]
    )

    if owner_count != 4 or tp_count != 2:
        mine = lax.all_gather(quarter, "seq", axis=1, tiled=True)
        across = swap_group(mine)
        pieces = [mine, across, swap_role(mine), swap_role(across)]
        keys, values = place(position, pages, fresh)
        partial = [
            project(control, attend(side, control, tables, queries[0], keys, values, slots), pieces)
            for side in (0, 1)
        ]
        return lax.psum_scatter(
            jnp.concatenate(partial, axis=0), "tp", scatter_dimension=0, tiled=True
        )[None]

    swap_tp = functools.partial(lax.ppermute, axis_name="tp", perm=SWAP)

    def four(one, two, *hold):
        return [one, two, swap_role(after(one, *hold)), swap_role(after(two, *hold))]

    near_across = [swap_group(part) for part in near]
    next_shard = [jnp.where(middle, part, forward(part)) for part in inner]
    next_across = [swap_group(part) for part in next_shard]
    near_all = four(near[0], near_across[0]) + four(near[1], near_across[1])
    next_all = four(next_shard[0], next_across[0]) + four(next_shard[1], next_across[1])
    far = [cross(after(near[0], *next_shard)), cross(after(near[1], pages))]

    keys, values = place(position, after(pages, far[0], *near_all, *next_all), fresh)
    left = attend(1, control, tables, queries[0], keys, values, slots)
    far_on = [forward(far[0]), forward(after(far[1], left))]
    sent = [project(control, left, [out_weight])]
    sent.append(project(control, after(left, sent[-1]), near_all))
    sent.append(project(control, after(left, sent[-1]), next_all))
    came = [swap_tp(each) for each in sent]
    far[0] = jnp.where(middle, far[0], after(far_on[0], sent[0]))
    far[1] = jnp.where(middle, far[1], after(far_on[1], sent[2]))
    far_across = [swap_group(part) for part in far]
    stay = attend(0, control, tables, after(queries[0], sent[2], far[1]), keys, values, slots)
    far_all = [four(far[n], far_across[n], stay) for n in (0, 1)]
    total = columns * owner_count
    out = project(control, stay, [out_weight], came[0], 10, None, total)
    for n in range(2):
        sent.append(project(control, after(left, out), far_all[n]))
        came.append(swap_tp(sent[-1]))
        out = project(
            control, after(stay, sent[-1]), (near_all, next_all)[n], came[n + 1], 11 + n, out, total
        )
    for n in range(2):
        out = project(control, stay, far_all[n], came[n + 3], 13 + n, out, total)
    return out


def solution(mesh):
    return jax.shard_map(
        shards,
        mesh=mesh,
        in_specs=(
            P("role", ("group", "seq"), "tp"),
            P("role", ("group", "seq"), None, "tp"),
            P("role", ("group", "seq"), None, None, "tp"),
            P("tp", "seq"),
            P("role", ("group", "seq")),
            P("role", ("group", "seq")),
            P("role", ("group", "seq")),
            P("role", ("group", "seq")),
            P("role", ("group", "seq")),
        ),
        out_specs=P("role", ("group", "seq", "tp"), None),
        check_vma=False,
    )
```

```python
import functools
import math

import jax
import jax.numpy as jnp
from jax import lax
from jax.experimental import pallas as pl
from jax.experimental.pallas import tpu as pltpu
from jax.sharding import PartitionSpec as P

HD = 128
TILE = 64
KEYS = 256
LANES = 128
HIDDEN = -1e30
COLUMNS = 256
MIB = 1024 * 1024


def cost(flops=3 * 10**9):
    return pl.CostEstimate(flops=flops, bytes_accessed=1000, transcendentals=0)


def rank_kernel(owner, page, position, wanted, count):
    owners, bucket = wanted.shape
    for n in range(owners):
        count[n] = 0

    def clear(k, carry):
        for n in range(owners):
            wanted[n, k] = 0
        return carry

    lax.fori_loop(0, bucket, clear, 0)

    def put(slot, carry):
        to = owner[0, slot]
        rank = count[to]
        count[to] = rank + 1
        wanted[to, rank] = page[0, slot]
        position[slot] = to * bucket + rank
        return carry

    lax.fori_loop(0, owner.shape[1], put, 0, unroll=4)


def rank(page_owner, page_index, owners, bucket):
    smem = pl.BlockSpec(memory_space=pltpu.SMEM)
    return pl.pallas_call(
        rank_kernel,
        out_shape=(
            jax.ShapeDtypeStruct((page_owner.shape[1],), jnp.int32),
            jax.ShapeDtypeStruct((owners, bucket), jnp.int32),
        ),
        in_specs=[smem, smem],
        out_specs=(smem, smem),
        scratch_shapes=[pltpu.SMEM((owners,), jnp.int32)],
        cost_estimate=cost(),
        name="rank",
    )(page_owner, page_index)


def place_kernel(position, pages, fresh, keys, values):
    kv_local, key_total = keys.shape[:2]
    slots, page_len, rows = position.shape[0], pages.shape[2], fresh.shape[0]
    channels = kv_local * HD
    hist = slots * page_len
    fresh_base = hist + KEYS
    for head in range(kv_local):
        values[head, :, HD:] = jnp.ones((key_total, HD), jnp.bfloat16)
        for first, last in ((hist, fresh_base), (fresh_base + rows, key_total)):
            keys[head, first:last] = jnp.zeros((last - first, HD), jnp.bfloat16)
            values[head, first:last, :HD] = jnp.zeros((last - first, HD), jnp.bfloat16)
        at = head * HD
        keys[head, fresh_base : fresh_base + rows] = fresh[:, at : at + HD]
        values[head, fresh_base : fresh_base + rows, :HD] = fresh[:, channels + at : channels + at + HD]

    def place(slot, carry):
        page = position[slot]
        row = pl.ds(pl.multiple_of(slot * page_len, page_len), page_len)
        for head in range(kv_local):
            at = head * HD
            keys[head, row] = pages[page, 0, :, at : at + HD]
            values[head, row, :HD] = pages[page, 1, :, at : at + HD]
        return carry

    lax.fori_loop(0, slots, place, 0, unroll=8)


def place(position, pages, fresh):
    kv_local = pages.shape[3] // HD
    rows = fresh.shape[0]
    key_total = position.shape[0] * pages.shape[2] + KEYS + pl.cdiv(rows, KEYS) * KEYS + KEYS
    vmem = pl.BlockSpec(memory_space=pltpu.VMEM)
    return pl.pallas_call(
        place_kernel,
        out_shape=(
            jax.ShapeDtypeStruct((kv_local, key_total, HD), jnp.bfloat16),
            jax.ShapeDtypeStruct((kv_local, key_total, 2 * HD), jnp.bfloat16),
        ),
        in_specs=[pl.BlockSpec(memory_space=pltpu.SMEM), vmem, vmem],
        out_specs=(vmem, vmem),
        compiler_params=pltpu.CompilerParams(vmem_limit_bytes=12 * MIB),
        cost_estimate=cost(),
        name="place",
    )(position, pages, fresh)


def attend_kernel(
    fresh_base, side, control, hist_at, hist_steps, fresh_at, fresh_steps,
    query, keys, values, key_conv, key_row, tok_conv, out, scores, sums,
):
    kv_local = keys.shape[0]
    group_size = query.shape[1] // (kv_local * HD)
    half, depth = out.shape[1], out.shape[2]
    tiles = half // TILE
    to_exp2 = math.log2(math.e) / math.sqrt(HD)
    wide = group_size * TILE

    def tile(number_here, carry):
        index = control[side] * tiles + number_here
        first = pl.multiple_of(index * TILE, TILE)
        leaving = pl.ds(pl.multiple_of(number_here * TILE, TILE), TILE)
        tokens = pl.ds(first, TILE)
        conv = tok_conv[tokens]
        number = first + lax.broadcasted_iota(jnp.int32, (TILE, 1), 0)
        steps_h, steps_f = hist_steps[index], fresh_steps[index]
        at_h, at_f = hist_at[index], fresh_at[index]
        heads = [
            jnp.concatenate(
                [
                    query[tokens, (head * group_size + g) * HD : (head * group_size + g + 1) * HD]
                    for g in range(group_size)
                ],
                axis=0,
            )
            for head in range(kv_local)
        ]

        def key_range(step):
            start = jnp.where(
                step < steps_h, at_h + step * KEYS, fresh_base + at_f + (step - steps_h) * KEYS
            )
            return pl.ds(pl.multiple_of(start, LANES), KEYS)

        def score(step, tops):
            where = key_range(step)
            ok = (key_conv[:, where] == conv) & (key_row[:, where] <= number)
            held = pl.ds(pl.multiple_of(step * KEYS, KEYS), KEYS)
            new = []
            for head in range(kv_local):
                s = lax.dot_general(
                    heads[head], keys[head, where], (((1,), (1,)), ((), ())),
                    preferred_element_type=jnp.float32,
                ).reshape(group_size, TILE, KEYS)
                s = jnp.where(ok[None], s, HIDDEN).reshape(wide, KEYS)
                scores[head, :, held] = s
                top = tops[head]
                for k in range(0, KEYS, LANES):
                    top = jnp.maximum(top, s[:, k : k + LANES])
                new.append(top)
            return tuple(new)

        low = jnp.full((wide, LANES), HIDDEN, jnp.float32)
        tops = lax.fori_loop(0, steps_h + steps_f, score, (low,) * kv_local)
        tops = [jnp.max(top, axis=1, keepdims=True) * to_exp2 for top in tops]
        sums[...] = jnp.zeros_like(sums)

        def gather(step, carry):
            where = key_range(step)
            held = pl.ds(pl.multiple_of(step * KEYS, KEYS), KEYS)
            for head in range(kv_local):
                w = jnp.exp2(scores[head, :, held] * to_exp2 - tops[head]).astype(jnp.bfloat16)
                sums[head] += jnp.dot(w, values[head, where], preferred_element_type=jnp.float32)
            return carry

        lax.fori_loop(0, steps_h + steps_f, gather, 0)
        for head in range(kv_local):
            done = (sums[head, :, :HD] / sums[head, :, HD:]).astype(jnp.bfloat16)
            for g in range(group_size):
                at = (head * group_size + g) * HD
                out[control[2 + at // depth], leaving, at % depth : at % depth + HD] = done[
                    g * TILE : (g + 1) * TILE
                ]
        return carry

    lax.fori_loop(0, tiles, tile, 0)


def attend_tables(rows, slots, page_len, tok_conv, page_conv, page_fill):
    hist = slots * page_len
    fresh_base = hist + KEYS
    key_total = fresh_base + pl.cdiv(rows, KEYS) * KEYS + KEYS
    live = jnp.arange(page_len)[None, :] < page_fill[:, None]
    hist_conv = jnp.where(live, page_conv[:, None], -1).reshape(hist)
    tail = key_total - fresh_base - rows
    key_conv = jnp.concatenate(
        [hist_conv, jnp.full((KEYS,), -1, jnp.int32), tok_conv, jnp.full((tail,), -1, jnp.int32)]
    )[None]
    key_row = jnp.maximum(jnp.arange(key_total, dtype=jnp.int32) - fresh_base, -1)[None]
    lowest, highest = tok_conv[::TILE], tok_conv[TILE - 1 :: TILE]
    hist_at = jnp.sum(page_conv[None] < lowest[:, None], axis=1, dtype=jnp.int32) * page_len
    hist_at = hist_at // LANES * LANES
    hist_end = jnp.sum(page_conv[None] <= highest[:, None], axis=1, dtype=jnp.int32) * page_len
    hist_steps = (hist_end - hist_at + KEYS - 1) // KEYS
    fresh_at = jnp.sum(tok_conv[None] < lowest[:, None], axis=1, dtype=jnp.int32) // LANES * LANES
    fresh_end = (jnp.arange(rows // TILE, dtype=jnp.int32) + 1) * TILE
    fresh_steps = (fresh_end - fresh_at + KEYS - 1) // KEYS
    return key_conv, key_row, tok_conv[:, None], hist_at, hist_steps, fresh_at, fresh_steps


def attend(side, control, tables, queries, keys, values, slots):
    rows, width = queries.shape
    kv_local, key_total = keys.shape[:2]
    group_size = width // (kv_local * HD)
    key_conv, key_row, tok_conv, *steps = tables
    fresh_base = slots + KEYS
    most = slots // KEYS + pl.cdiv(rows, KEYS)
    smem = pl.BlockSpec(memory_space=pltpu.SMEM)
    vmem = pl.BlockSpec(memory_space=pltpu.VMEM)
    return pl.pallas_call(
        functools.partial(attend_kernel, fresh_base, side),
        out_shape=jax.ShapeDtypeStruct((4, rows // 2, width // 4), jnp.bfloat16),
        in_specs=[smem] * 5 + [vmem] * 6,
        out_specs=vmem,
        scratch_shapes=[
            pltpu.VMEM((kv_local, group_size * TILE, most * KEYS), jnp.float32),
            pltpu.VMEM((kv_local, group_size * TILE, 2 * HD), jnp.float32),
        ],
        compiler_params=pltpu.CompilerParams(vmem_limit_bytes=20 * MIB),
        cost_estimate=cost(16 * 10**9),
        name="attend",
    )(control, *steps, queries, keys, values, key_conv, key_row, tok_conv)


def multiply(left, pieces, at):
    total = None
    for n, piece in enumerate(pieces):
        term = jnp.dot(left[n], piece[:, at], preferred_element_type=jnp.float32)
        total = term if total is None else total + term
    return total.astype(jnp.bfloat16)


def blocks(columns):
    cut = min(COLUMNS, columns)
    return [slice(k, k + cut) for k in range(0, columns, cut)]


def parts_of(control, refs):
    if len(refs) == 1:
        depth = refs[0].shape[0] // 4
        return [
            (0, [refs[0].at[pl.ds(pl.multiple_of(control[6 + n] * depth, depth), depth)] for n in range(4)])
        ]
    columns = refs[0].shape[1]
    return [(k // 4 * columns, refs[k : k + 4]) for k in range(0, len(refs), 4)]


def project_kernel(control, left, *refs):
    for first, pieces in parts_of(control, refs[:-1]):
        for at in blocks(pieces[0].shape[1]):
            refs[-1][:, first + at.start : first + at.stop] = multiply(left, pieces, at)


def finish_kernel(has_out, control, left, came, *refs):
    for first, pieces in parts_of(control, refs[: len(refs) - 1 - has_out]):
        for at in blocks(pieces[0].shape[1]):
            to = slice(first + at.start, first + at.stop)
            total = multiply(left, pieces, at).astype(jnp.float32) + came[:, to].astype(jnp.float32)
            refs[-1][0, :, to] = total.astype(jnp.bfloat16)


def project(control, left, pieces, came=None, base=None, out=None, width=None):
    half = left.shape[1]
    columns = pieces[0].shape[1] * max(1, len(pieces) // 4)
    vmem = pl.BlockSpec(memory_space=pltpu.VMEM)
    in_specs = [vmem]
    operands = [left]
    aliases = {}
    if came is None:
        kernel = project_kernel
        out_shape = jax.ShapeDtypeStruct((half, columns), jnp.bfloat16)
        out_specs = vmem
    else:
        kernel = functools.partial(finish_kernel, int(out is not None))
        in_specs.append(vmem)
        operands.append(came)
        out_shape = jax.ShapeDtypeStruct((1, half, width), jnp.bfloat16)
        out_specs = pl.BlockSpec((1, half, columns), lambda j, control: (0, 0, control[base]))
    in_specs += [vmem] * len(pieces)
    operands += pieces
    if out is not None:
        in_specs.append(pl.BlockSpec(memory_space=pl.ANY))
        operands.append(out)
        aliases = {len(operands): 0}
    return pl.pallas_call(
        kernel,
        out_shape=out_shape,
        grid_spec=pltpu.PrefetchScalarGridSpec(
            num_scalar_prefetch=1, grid=(1,), in_specs=in_specs, out_specs=out_specs
        ),
        input_output_aliases=aliases,
        compiler_params=pltpu.CompilerParams(vmem_limit_bytes=10 * MIB),
        cost_estimate=cost(),
        name="project" if came is None else "finish",
    )(control, *operands)


def pick_kernel(asked, pool, out):
    owner = pl.program_id(0)

    def copy(n, carry):
        out[0, n] = pool[asked[owner, n]]
        return carry

    lax.fori_loop(0, asked.shape[1], copy, 0, unroll=8)


def pick(pool, asked):
    block = (1, asked.shape[1]) + pool.shape[1:]
    return pl.pallas_call(
        pick_kernel,
        out_shape=jax.ShapeDtypeStruct(asked.shape + pool.shape[1:], jnp.bfloat16),
        grid=(asked.shape[0],),
        in_specs=[
            pl.BlockSpec(memory_space=pltpu.SMEM),
            pl.BlockSpec(memory_space=pltpu.VMEM),
        ],
        out_specs=pl.BlockSpec(block, lambda owner: (owner, 0, 0, 0, 0)),
        compiler_params=pltpu.CompilerParams(vmem_limit_bytes=12 * MIB),
        cost_estimate=cost(),
        name="pick",
    )(asked, pool)


SWAP = [(0, 1), (1, 0)]


def after(value, *others):
    return lax.optimization_barrier((value,) + others)[0]


def shards(
    queries, new_kv, pool, out_weight, tok_conv, page_conv, page_fill, page_owner, page_index
):
    row_count = queries.shape[1]
    slot_count = page_owner.shape[1]
    owner_count = lax.axis_size("seq")
    tp_count = lax.axis_size("tp")
    bucket = 2 * slot_count // owner_count
    group, role, tp = lax.axis_index("group"), lax.axis_index("role"), lax.axis_index("tp")
    seq = lax.axis_index("seq")


    own = 2 * group + role
    depth = out_weight.shape[0] // 4
    columns = out_weight.shape[1]
    quarter = lax.dynamic_slice_in_dim(out_weight, own * depth, depth, 0)
    order = [q ^ own for q in range(4)]
    order = [(v % 2) * 2 + v // 2 for v in order]
    flip = tp if tp_count == 2 else 0
    second = jnp.where(seq < 2, 2, 1)
    third = jnp.where(seq < 2, 3, 0)
    local = [own, own ^ 2, own ^ 1, own ^ 3]
    control = jnp.stack(
        [jnp.asarray(v, jnp.int32) for v in (flip, 1 - flip, *order, *local, seq, seq ^ 1, second, 2 * third, 2 * third + 1)]
    )
    swap_group = functools.partial(lax.ppermute, axis_name="group", perm=SWAP)
    swap_role = functools.partial(lax.ppermute, axis_name="role", perm=SWAP)

    if owner_count == 4:
        middle = (seq == 1) | (seq == 2)
        cut = columns // 2
        parts = [quarter[:, :cut], quarter[:, cut:]]
        pair = functools.partial(lax.ppermute, axis_name="seq", perm=[(0, 1), (1, 0), (2, 3), (3, 2)])
        cross = functools.partial(lax.ppermute, axis_name="seq", perm=[(1, 2), (2, 1)])
        forward = functools.partial(lax.ppermute, axis_name="seq", perm=[(1, 0), (2, 3)])
        near, inner = [pair(parts[0])], [cross(parts[0])]

    position, wanted = rank(page_owner, page_index, owner_count, bucket)
    asked = lax.all_to_all(wanted, "seq", split_axis=0, concat_axis=0, tiled=True)
    if owner_count == 4:
        near, inner = [after(near[0], asked)], [after(inner[0], asked)]
        later = after(parts[1], near[0], inner[0])
        near.append(pair(later))
        inner.append(cross(later))
        asked = after(asked, near[0], inner[0])
    found = pick(pool[0], asked)
    if owner_count == 4:
        near[1], inner[1] = after(near[1], found), after(inner[1], found)
        found = after(found, near[1], inner[1])
    pages = lax.all_to_all(found, "seq", split_axis=0, concat_axis=0, tiled=True)
    pages = pages.reshape((owner_count * bucket,) + found.shape[2:])
    slots = slot_count * pool.shape[3]
    fresh = new_kv[0].reshape(row_count, -1)
    tables = attend_tables(
        row_count, slot_count, pool.shape[3], tok_conv[0], page_conv[0], page_fill[0]
    )

    if owner_count != 4 or tp_count != 2:
        mine = lax.all_gather(quarter, "seq", axis=1, tiled=True)
        across = swap_group(mine)
        pieces = [mine, across, swap_role(mine), swap_role(across)]
        keys, values = place(position, pages, fresh)
        partial = [
            project(control, attend(side, control, tables, queries[0], keys, values, slots), pieces)
            for side in (0, 1)
        ]
        return lax.psum_scatter(
            jnp.concatenate(partial, axis=0), "tp", scatter_dimension=0, tiled=True
        )[None]

    swap_tp = functools.partial(lax.ppermute, axis_name="tp", perm=SWAP)

    def four(one, two, *hold):
        return [one, two, swap_role(after(one, *hold)), swap_role(after(two, *hold))]

    near_across = [swap_group(part) for part in near]
    next_shard = [jnp.where(middle, part, forward(part)) for part in inner]
    next_across = [swap_group(part) for part in next_shard]
    near_all = four(near[0], near_across[0]) + four(near[1], near_across[1])
    far = [cross(after(near[0], *next_shard))]
    far.append(cross(after(near[1], far[0])))
    next_all = four(next_shard[0], next_across[0], far[0]) + four(next_shard[1], next_across[1], far[0])
    far_on = [forward(far[0])]

    keys, values = place(position, after(pages, *near_all, *next_all), fresh)
    left = attend(1, control, tables, queries[0], keys, values, slots)
    far[0] = jnp.where(middle, far[0], after(far_on[0], left))
    far_across = [swap_group(far[0])]
    sent = [project(control, left, [out_weight])]
    far_on.append(forward(after(far[1], sent[0])))
    sent.append(project(control, after(left, sent[-1]), near_all))
    sent.append(project(control, after(left, sent[-1]), next_all))
    came = [swap_tp(each) for each in sent]
    far_all = [four(far[0], far_across[0], sent[2])]
    far[1] = jnp.where(middle, far[1], after(far_on[1], sent[2]))
    far_across.append(swap_group(far[1]))
    stay = attend(0, control, tables, after(queries[0], sent[2], far[1]), keys, values, slots)
    sent.append(project(control, after(left, stay, *came), far_all[0]))
    far_all.append(four(far[1], far_across[1], sent[3]))
    came.append(swap_tp(sent[3]))
    total = columns * owner_count
    out = project(control, after(stay, sent[3]), [out_weight], came[0], 10, None, total)
    out = project(control, stay, near_all, came[1], 11, out, total)
    sent.append(project(control, after(left, out), far_all[1]))
    came.append(swap_tp(sent[4]))
    out = project(control, after(stay, sent[4]), next_all, came[2], 12, out, total)
    for n in range(2):
        out = project(control, stay, far_all[n], came[n + 3], 13 + n, out, total)
    return out


def solution(mesh):
    return jax.shard_map(
        shards,
        mesh=mesh,
        in_specs=(
            P("role", ("group", "seq"), "tp"),
            P("role", ("group", "seq"), None, "tp"),
            P("role", ("group", "seq"), None, None, "tp"),
            P("tp", "seq"),
            P("role", ("group", "seq")),
            P("role", ("group", "seq")),
            P("role", ("group", "seq")),
            P("role", ("group", "seq")),
            P("role", ("group", "seq")),
        ),
        out_specs=P("role", ("group", "seq", "tp"), None),
        check_vma=False,
    )
```

```python
import functools
import math

import jax
import jax.numpy as jnp
from jax import lax
from jax.experimental import pallas as pl
from jax.experimental.pallas import tpu as pltpu
from jax.sharding import PartitionSpec as P

HD = 128
TILE = 64
KEYS = 256
LANES = 128
HIDDEN = -1e30
COLUMNS = 256
MIB = 1024 * 1024


def cost(flops=3 * 10**9):
    return pl.CostEstimate(flops=flops, bytes_accessed=1000, transcendentals=0)


def rank_kernel(owner, page, position, wanted, count):
    owners, bucket = wanted.shape
    for n in range(owners):
        count[n] = 0

    def clear(k, carry):
        for n in range(owners):
            wanted[n, k] = 0
        return carry

    lax.fori_loop(0, bucket, clear, 0)

    def put(slot, carry):
        to = owner[0, slot]
        rank = count[to]
        count[to] = rank + 1
        wanted[to, rank] = page[0, slot]
        position[slot] = to * bucket + rank
        return carry

    lax.fori_loop(0, owner.shape[1], put, 0, unroll=4)


def rank(page_owner, page_index, owners, bucket):
    smem = pl.BlockSpec(memory_space=pltpu.SMEM)
    return pl.pallas_call(
        rank_kernel,
        out_shape=(
            jax.ShapeDtypeStruct((page_owner.shape[1],), jnp.int32),
            jax.ShapeDtypeStruct((owners, bucket), jnp.int32),
        ),
        in_specs=[smem, smem],
        out_specs=(smem, smem),
        scratch_shapes=[pltpu.SMEM((owners,), jnp.int32)],
        cost_estimate=cost(),
        name="rank",
    )(page_owner, page_index)


def place_kernel(position, pages, fresh, keys, values):
    kv_local, key_total = keys.shape[:2]
    slots, page_len, rows = position.shape[0], pages.shape[2], fresh.shape[0]
    channels = kv_local * HD
    hist = slots * page_len
    fresh_base = hist + KEYS
    for head in range(kv_local):
        values[head, :, HD:] = jnp.ones((key_total, HD), jnp.bfloat16)
        for first, last in ((hist, fresh_base), (fresh_base + rows, key_total)):
            keys[head, first:last] = jnp.zeros((last - first, HD), jnp.bfloat16)
            values[head, first:last, :HD] = jnp.zeros((last - first, HD), jnp.bfloat16)
        at = head * HD
        keys[head, fresh_base : fresh_base + rows] = fresh[:, at : at + HD]
        values[head, fresh_base : fresh_base + rows, :HD] = fresh[:, channels + at : channels + at + HD]

    def place(slot, carry):
        page = position[slot]
        row = pl.ds(pl.multiple_of(slot * page_len, page_len), page_len)
        for head in range(kv_local):
            at = head * HD
            keys[head, row] = pages[page, 0, :, at : at + HD]
            values[head, row, :HD] = pages[page, 1, :, at : at + HD]
        return carry

    lax.fori_loop(0, slots, place, 0, unroll=8)


def place(position, pages, fresh):
    kv_local = pages.shape[3] // HD
    rows = fresh.shape[0]
    key_total = position.shape[0] * pages.shape[2] + KEYS + pl.cdiv(rows, KEYS) * KEYS + KEYS
    vmem = pl.BlockSpec(memory_space=pltpu.VMEM)
    return pl.pallas_call(
        place_kernel,
        out_shape=(
            jax.ShapeDtypeStruct((kv_local, key_total, HD), jnp.bfloat16),
            jax.ShapeDtypeStruct((kv_local, key_total, 2 * HD), jnp.bfloat16),
        ),
        in_specs=[pl.BlockSpec(memory_space=pltpu.SMEM), vmem, vmem],
        out_specs=(vmem, vmem),
        compiler_params=pltpu.CompilerParams(vmem_limit_bytes=20 * MIB),
        cost_estimate=cost(10**9),
        name="place",
    )(position, pages, fresh)


def attend_kernel(
    fresh_base, side, control, hist_at, hist_steps, fresh_at, fresh_steps,
    query, keys, values, key_conv, key_row, tok_conv, out, scores, sums,
):
    kv_local = keys.shape[0]
    group_size = query.shape[1] // (kv_local * HD)
    half, depth = out.shape[1], out.shape[2]
    tiles = half // TILE
    to_exp2 = math.log2(math.e) / math.sqrt(HD)
    wide = group_size * TILE

    def tile(number_here, carry):
        index = control[side] * tiles + number_here
        first = pl.multiple_of(index * TILE, TILE)
        leaving = pl.ds(pl.multiple_of(number_here * TILE, TILE), TILE)
        tokens = pl.ds(first, TILE)
        conv = tok_conv[tokens]
        number = first + lax.broadcasted_iota(jnp.int32, (TILE, 1), 0)
        steps_h, steps_f = hist_steps[index], fresh_steps[index]
        at_h, at_f = hist_at[index], fresh_at[index]
        heads = [
            jnp.concatenate(
                [
                    query[tokens, (head * group_size + g) * HD : (head * group_size + g + 1) * HD]
                    for g in range(group_size)
                ],
                axis=0,
            )
            for head in range(kv_local)
        ]

        def key_range(step):
            start = jnp.where(
                step < steps_h, at_h + step * KEYS, fresh_base + at_f + (step - steps_h) * KEYS
            )
            return pl.ds(pl.multiple_of(start, LANES), KEYS)

        def score(step, tops):
            where = key_range(step)
            ok = (key_conv[:, where] == conv) & (key_row[:, where] <= number)
            held = pl.ds(pl.multiple_of(step * KEYS, KEYS), KEYS)
            new = []
            for head in range(kv_local):
                s = lax.dot_general(
                    heads[head], keys[head, where], (((1,), (1,)), ((), ())),
                    preferred_element_type=jnp.float32,
                ).reshape(group_size, TILE, KEYS)
                s = jnp.where(ok[None], s, HIDDEN).reshape(wide, KEYS)
                scores[head, :, held] = s
                top = tops[head]
                for k in range(0, KEYS, LANES):
                    top = jnp.maximum(top, s[:, k : k + LANES])
                new.append(top)
            return tuple(new)

        low = jnp.full((wide, LANES), HIDDEN, jnp.float32)
        tops = lax.fori_loop(0, steps_h + steps_f, score, (low,) * kv_local)
        tops = [jnp.max(top, axis=1, keepdims=True) * to_exp2 for top in tops]
        sums[...] = jnp.zeros_like(sums)

        def gather(step, carry):
            where = key_range(step)
            held = pl.ds(pl.multiple_of(step * KEYS, KEYS), KEYS)
            for head in range(kv_local):
                w = jnp.exp2(scores[head, :, held] * to_exp2 - tops[head]).astype(jnp.bfloat16)
                sums[head] += jnp.dot(w, values[head, where], preferred_element_type=jnp.float32)
            return carry

        lax.fori_loop(0, steps_h + steps_f, gather, 0)
        for head in range(kv_local):
            done = (sums[head, :, :HD] / sums[head, :, HD:]).astype(jnp.bfloat16)
            for g in range(group_size):
                at = (head * group_size + g) * HD
                out[control[2 + at // depth], leaving, at % depth : at % depth + HD] = done[
                    g * TILE : (g + 1) * TILE
                ]
        return carry

    lax.fori_loop(0, tiles, tile, 0)


def attend_tables(rows, slots, page_len, tok_conv, page_conv, page_fill):
    hist = slots * page_len
    fresh_base = hist + KEYS
    key_total = fresh_base + pl.cdiv(rows, KEYS) * KEYS + KEYS
    live = jnp.arange(page_len)[None, :] < page_fill[:, None]
    hist_conv = jnp.where(live, page_conv[:, None], -1).reshape(hist)
    tail = key_total - fresh_base - rows
    key_conv = jnp.concatenate(
        [hist_conv, jnp.full((KEYS,), -1, jnp.int32), tok_conv, jnp.full((tail,), -1, jnp.int32)]
    )[None]
    key_row = jnp.maximum(jnp.arange(key_total, dtype=jnp.int32) - fresh_base, -1)[None]
    lowest, highest = tok_conv[::TILE], tok_conv[TILE - 1 :: TILE]
    hist_at = jnp.sum(page_conv[None] < lowest[:, None], axis=1, dtype=jnp.int32) * page_len
    hist_at = hist_at // LANES * LANES
    hist_end = jnp.sum(page_conv[None] <= highest[:, None], axis=1, dtype=jnp.int32) * page_len
    hist_steps = (hist_end - hist_at + KEYS - 1) // KEYS
    fresh_at = jnp.sum(tok_conv[None] < lowest[:, None], axis=1, dtype=jnp.int32) // LANES * LANES
    fresh_end = (jnp.arange(rows // TILE, dtype=jnp.int32) + 1) * TILE
    fresh_steps = (fresh_end - fresh_at + KEYS - 1) // KEYS
    return key_conv, key_row, tok_conv[:, None], hist_at, hist_steps, fresh_at, fresh_steps


def attend(side, control, tables, queries, keys, values, slots):
    rows, width = queries.shape
    kv_local, key_total = keys.shape[:2]
    group_size = width // (kv_local * HD)
    key_conv, key_row, tok_conv, *steps = tables
    fresh_base = slots + KEYS
    most = slots // KEYS + pl.cdiv(rows, KEYS)
    smem = pl.BlockSpec(memory_space=pltpu.SMEM)
    vmem = pl.BlockSpec(memory_space=pltpu.VMEM)
    return pl.pallas_call(
        functools.partial(attend_kernel, fresh_base, side),
        out_shape=jax.ShapeDtypeStruct((4, rows // 2, width // 4), jnp.bfloat16),
        in_specs=[smem] * 5 + [vmem] * 6,
        out_specs=vmem,
        scratch_shapes=[
            pltpu.VMEM((kv_local, group_size * TILE, most * KEYS), jnp.float32),
            pltpu.VMEM((kv_local, group_size * TILE, 2 * HD), jnp.float32),
        ],
        compiler_params=pltpu.CompilerParams(vmem_limit_bytes=28 * MIB),
        cost_estimate=cost((16 - 15 * side) * 10**9),
        name="attend",
    )(control, *steps, queries, keys, values, key_conv, key_row, tok_conv)


def multiply(left, pieces, at):
    total = None
    for n, piece in enumerate(pieces):
        term = jnp.dot(left[n], piece[:, at], preferred_element_type=jnp.float32)
        total = term if total is None else total + term
    return total.astype(jnp.bfloat16)


def blocks(columns):
    cut = min(COLUMNS, columns)
    return [slice(k, k + cut) for k in range(0, columns, cut)]


def parts_of(control, refs):
    if len(refs) == 1:
        depth = refs[0].shape[0] // 4
        return [
            (0, [refs[0].at[pl.ds(pl.multiple_of(control[6 + n] * depth, depth), depth)] for n in range(4)])
        ]
    columns = refs[0].shape[1]
    return [(k // 4 * columns, refs[k : k + 4]) for k in range(0, len(refs), 4)]


def project_kernel(control, left, *refs):
    for first, pieces in parts_of(control, refs[:-1]):
        for at in blocks(pieces[0].shape[1]):
            refs[-1][:, first + at.start : first + at.stop] = multiply(left, pieces, at)


def finish_kernel(has_out, control, left, came, *refs):
    for first, pieces in parts_of(control, refs[: len(refs) - 1 - has_out]):
        for at in blocks(pieces[0].shape[1]):
            to = slice(first + at.start, first + at.stop)
            total = multiply(left, pieces, at).astype(jnp.float32) + came[:, to].astype(jnp.float32)
            refs[-1][0, :, to] = total.astype(jnp.bfloat16)


def project(control, left, pieces, came=None, base=None, out=None, width=None):
    half = left.shape[1]
    columns = pieces[0].shape[1] * max(1, len(pieces) // 4)
    vmem = pl.BlockSpec(memory_space=pltpu.VMEM)
    in_specs = [vmem]
    operands = [left]
    aliases = {}
    if came is None:
        kernel = project_kernel
        out_shape = jax.ShapeDtypeStruct((half, columns), jnp.bfloat16)
        out_specs = vmem
    else:
        kernel = functools.partial(finish_kernel, int(out is not None))
        in_specs.append(vmem)
        operands.append(came)
        out_shape = jax.ShapeDtypeStruct((1, half, width), jnp.bfloat16)
        out_specs = pl.BlockSpec((1, half, columns), lambda j, control: (0, 0, control[base]))
    in_specs += [vmem] * len(pieces)
    operands += pieces
    if out is not None:
        in_specs.append(pl.BlockSpec(memory_space=pl.ANY))
        operands.append(out)
        aliases = {len(operands): 0}
    return pl.pallas_call(
        kernel,
        out_shape=out_shape,
        grid_spec=pltpu.PrefetchScalarGridSpec(
            num_scalar_prefetch=1, grid=(1,), in_specs=in_specs, out_specs=out_specs
        ),
        input_output_aliases=aliases,
        compiler_params=pltpu.CompilerParams(vmem_limit_bytes=16 * MIB),
        cost_estimate=cost(),
        name="project" if came is None else "finish",
    )(control, *operands)


def pick_kernel(asked, pool, out):
    owner = pl.program_id(0)

    def copy(n, carry):
        out[0, n] = pool[asked[owner, n]]
        return carry

    lax.fori_loop(0, asked.shape[1], copy, 0, unroll=8)


def pick(pool, asked):
    block = (1, asked.shape[1]) + pool.shape[1:]
    return pl.pallas_call(
        pick_kernel,
        out_shape=jax.ShapeDtypeStruct(asked.shape + pool.shape[1:], jnp.bfloat16),
        grid=(asked.shape[0],),
        in_specs=[
            pl.BlockSpec(memory_space=pltpu.SMEM),
            pl.BlockSpec(memory_space=pltpu.VMEM),
        ],
        out_specs=pl.BlockSpec(block, lambda owner: (owner, 0, 0, 0, 0)),
        compiler_params=pltpu.CompilerParams(vmem_limit_bytes=12 * MIB),
        cost_estimate=cost(),
        name="pick",
    )(asked, pool)


SWAP = [(0, 1), (1, 0)]


def after(value, *others):
    return lax.optimization_barrier((value,) + others)[0]


def shards(
    queries, new_kv, pool, out_weight, tok_conv, page_conv, page_fill, page_owner, page_index
):
    row_count = queries.shape[1]
    slot_count = page_owner.shape[1]
    owner_count = lax.axis_size("seq")
    tp_count = lax.axis_size("tp")
    bucket = 2 * slot_count // owner_count
    group, role, tp = lax.axis_index("group"), lax.axis_index("role"), lax.axis_index("tp")
    seq = lax.axis_index("seq")


    own = 2 * group + role
    depth = out_weight.shape[0] // 4
    columns = out_weight.shape[1]
    quarter = lax.dynamic_slice_in_dim(out_weight, own * depth, depth, 0)
    order = [q ^ own for q in range(4)]
    order = [(v % 2) * 2 + v // 2 for v in order]
    flip = tp if tp_count == 2 else 0
    second = jnp.where(seq < 2, 2, 1)
    third = jnp.where(seq < 2, 3, 0)
    local = [own, own ^ 2, own ^ 1, own ^ 3]
    control = jnp.stack(
        [jnp.asarray(v, jnp.int32) for v in (flip, 1 - flip, *order, *local, seq, seq ^ 1, second, 2 * third, 2 * third + 1)]
    )
    swap_group = functools.partial(lax.ppermute, axis_name="group", perm=SWAP)
    swap_role = functools.partial(lax.ppermute, axis_name="role", perm=SWAP)

    if owner_count == 4:
        middle = (seq == 1) | (seq == 2)
        cut = columns // 2
        parts = [quarter[:, :cut], quarter[:, cut:]]
        pair = functools.partial(lax.ppermute, axis_name="seq", perm=[(0, 1), (1, 0), (2, 3), (3, 2)])
        cross = functools.partial(lax.ppermute, axis_name="seq", perm=[(1, 2), (2, 1)])
        forward = functools.partial(lax.ppermute, axis_name="seq", perm=[(1, 0), (2, 3)])
        near, inner = [pair(parts[0])], [cross(parts[0])]

    position, wanted = rank(page_owner, page_index, owner_count, bucket)
    asked = lax.all_to_all(wanted, "seq", split_axis=0, concat_axis=0, tiled=True)
    if owner_count == 4:
        near, inner = [after(near[0], asked)], [after(inner[0], asked)]
        later = after(parts[1], near[0], inner[0])
        near.append(pair(later))
        inner.append(cross(later))
        asked = after(asked, near[0], inner[0])
    found = pick(pool[0], asked)
    if owner_count == 4:
        near[1], inner[1] = after(near[1], found), after(inner[1], found)
        found = after(found, near[1], inner[1])
    pages = lax.all_to_all(found, "seq", split_axis=0, concat_axis=0, tiled=True)
    pages = pages.reshape((owner_count * bucket,) + found.shape[2:])
    slots = slot_count * pool.shape[3]
    fresh = new_kv[0].reshape(row_count, -1)
    tables = attend_tables(
        row_count, slot_count, pool.shape[3], tok_conv[0], page_conv[0], page_fill[0]
    )

    if owner_count != 4 or tp_count != 2:
        mine = lax.all_gather(quarter, "seq", axis=1, tiled=True)
        across = swap_group(mine)
        pieces = [mine, across, swap_role(mine), swap_role(across)]
        keys, values = place(position, pages, fresh)
        partial = [
            project(control, attend(side, control, tables, queries[0], keys, values, slots), pieces)
            for side in (0, 1)
        ]
        return lax.psum_scatter(
            jnp.concatenate(partial, axis=0), "tp", scatter_dimension=0, tiled=True
        )[None]

    swap_tp = functools.partial(lax.ppermute, axis_name="tp", perm=SWAP)

    def four(one, two, *hold):
        return [one, two, swap_role(after(one, *hold)), swap_role(after(two, *hold))]

    near_across = [swap_group(part) for part in near]
    next_shard = [jnp.where(middle, part, forward(part)) for part in inner]
    next_across = [swap_group(part) for part in next_shard]
    near_all = four(near[0], near_across[0]) + four(near[1], near_across[1])
    next_all = four(next_shard[0], next_across[0]) + four(next_shard[1], next_across[1])
    far = [cross(after(part, *next_across)) for part in near]

    keys, values = place(position, after(pages, *near_all, *next_all), fresh)
    left = attend(1, control, tables, queries[0], keys, values, slots)
    far_on = [forward(after(far[0], left))]
    sent = [project(control, left, [out_weight])]
    far_on.append(forward(after(far[1], sent[0])))
    sent.append(project(control, after(left, sent[-1]), near_all))
    far[0] = jnp.where(middle, far[0], after(far_on[0], sent[1]))
    far_across = [swap_group(far[0])]
    sent.append(project(control, after(left, sent[-1]), next_all))
    came = [swap_tp(each) for each in sent]
    stay = attend(0, control, tables, after(queries[0], sent[2], far[0]), keys, values, slots)
    far[1] = jnp.where(middle, far[1], after(far_on[1], stay))
    far_across.append(swap_group(far[1]))
    far_all = [four(far[n], far_across[n], stay) for n in (0, 1)]
    total = columns * owner_count
    out = project(control, after(stay, *came[:2]), [out_weight], came[0], 10, None, total)
    out = project(control, stay, near_all, came[1], 11, out, total)
    sent.append(project(control, after(left, out), far_all[0]))
    came.append(swap_tp(sent[3]))
    out = project(control, after(stay, sent[3]), next_all, came[2], 12, out, total)
    sent.append(project(control, after(left, out), far_all[1]))
    came.append(swap_tp(sent[4]))
    for n in range(2):
        out = project(control, after(stay, sent[4]), far_all[n], came[n + 3], 13 + n, out, total)
    return out


def solution(mesh):
    return jax.shard_map(
        shards,
        mesh=mesh,
        in_specs=(
            P("role", ("group", "seq"), "tp"),
            P("role", ("group", "seq"), None, "tp"),
            P("role", ("group", "seq"), None, None, "tp"),
            P("tp", "seq"),
            P("role", ("group", "seq")),
            P("role", ("group", "seq")),
            P("role", ("group", "seq")),
            P("role", ("group", "seq")),
            P("role", ("group", "seq")),
        ),
        out_specs=P("role", ("group", "seq", "tp"), None),
        check_vma=False,
    )
```

```python
import functools
import math

import jax
import jax.numpy as jnp
from jax import lax
from jax.experimental import pallas as pl
from jax.experimental.pallas import tpu as pltpu
from jax.sharding import PartitionSpec as P

HD = 128
TILE = 64
KEYS = 256
LANES = 128
HIDDEN = -1e30
COLUMNS = 256
MIB = 1024 * 1024


def cost(flops=3 * 10**9):
    return pl.CostEstimate(flops=flops, bytes_accessed=1000, transcendentals=0)


def rank_kernel(owner, page, position, wanted, count):
    owners, bucket = wanted.shape
    for n in range(owners):
        count[n] = 0

    def clear(k, carry):
        for n in range(owners):
            wanted[n, k] = 0
        return carry

    lax.fori_loop(0, bucket, clear, 0)

    def put(slot, carry):
        to = owner[0, slot]
        rank = count[to]
        count[to] = rank + 1
        wanted[to, rank] = page[0, slot]
        position[slot] = to * bucket + rank
        return carry

    lax.fori_loop(0, owner.shape[1], put, 0, unroll=4)


def rank(page_owner, page_index, owners, bucket):
    smem = pl.BlockSpec(memory_space=pltpu.SMEM)
    return pl.pallas_call(
        rank_kernel,
        out_shape=(
            jax.ShapeDtypeStruct((page_owner.shape[1],), jnp.int32),
            jax.ShapeDtypeStruct((owners, bucket), jnp.int32),
        ),
        in_specs=[smem, smem],
        out_specs=(smem, smem),
        scratch_shapes=[pltpu.SMEM((owners,), jnp.int32)],
        cost_estimate=cost(),
        name="rank",
    )(page_owner, page_index)


def place_kernel(position, pages, fresh, keys, values):
    kv_local, key_total = keys.shape[:2]
    slots, page_len, rows = position.shape[0], pages.shape[2], fresh.shape[0]
    channels = kv_local * HD
    hist = slots * page_len
    fresh_base = hist + KEYS
    for head in range(kv_local):
        values[head, :, HD:] = jnp.ones((key_total, HD), jnp.bfloat16)
        for first, last in ((hist, fresh_base), (fresh_base + rows, key_total)):
            keys[head, first:last] = jnp.zeros((last - first, HD), jnp.bfloat16)
            values[head, first:last, :HD] = jnp.zeros((last - first, HD), jnp.bfloat16)
        at = head * HD
        keys[head, fresh_base : fresh_base + rows] = fresh[:, at : at + HD]
        values[head, fresh_base : fresh_base + rows, :HD] = fresh[:, channels + at : channels + at + HD]

    def place(slot, carry):
        page = position[slot]
        row = pl.ds(pl.multiple_of(slot * page_len, page_len), page_len)
        for head in range(kv_local):
            at = head * HD
            keys[head, row] = pages[page, 0, :, at : at + HD]
            values[head, row, :HD] = pages[page, 1, :, at : at + HD]
        return carry

    lax.fori_loop(0, slots, place, 0, unroll=8)


def place(position, pages, fresh):
    kv_local = pages.shape[3] // HD
    rows = fresh.shape[0]
    key_total = position.shape[0] * pages.shape[2] + KEYS + pl.cdiv(rows, KEYS) * KEYS + KEYS
    vmem = pl.BlockSpec(memory_space=pltpu.VMEM)
    return pl.pallas_call(
        place_kernel,
        out_shape=(
            jax.ShapeDtypeStruct((kv_local, key_total, HD), jnp.bfloat16),
            jax.ShapeDtypeStruct((kv_local, key_total, 2 * HD), jnp.bfloat16),
        ),
        in_specs=[pl.BlockSpec(memory_space=pltpu.SMEM), vmem, vmem],
        out_specs=(vmem, vmem),
        compiler_params=pltpu.CompilerParams(vmem_limit_bytes=20 * MIB),
        cost_estimate=cost(10**9),
        name="place",
    )(position, pages, fresh)


def attend_kernel(
    fresh_base, side, control, hist_at, hist_steps, fresh_at, fresh_steps,
    query, keys, values, key_conv, key_row, tok_conv, out, scores, sums,
):
    kv_local = keys.shape[0]
    group_size = query.shape[1] // (kv_local * HD)
    half, depth = out.shape[1], out.shape[2]
    tiles = half // TILE
    to_exp2 = math.log2(math.e) / math.sqrt(HD)
    wide = group_size * TILE

    def tile(number_here, carry):
        index = control[side] * tiles + number_here
        first = pl.multiple_of(index * TILE, TILE)
        leaving = pl.ds(pl.multiple_of(number_here * TILE, TILE), TILE)
        tokens = pl.ds(first, TILE)
        conv = tok_conv[tokens]
        number = first + lax.broadcasted_iota(jnp.int32, (TILE, 1), 0)
        steps_h, steps_f = hist_steps[index], fresh_steps[index]
        at_h, at_f = hist_at[index], fresh_at[index]
        heads = [
            jnp.concatenate(
                [
                    query[tokens, (head * group_size + g) * HD : (head * group_size + g + 1) * HD]
                    for g in range(group_size)
                ],
                axis=0,
            )
            for head in range(kv_local)
        ]

        def key_range(step):
            start = jnp.where(
                step < steps_h, at_h + step * KEYS, fresh_base + at_f + (step - steps_h) * KEYS
            )
            return pl.ds(pl.multiple_of(start, LANES), KEYS)

        def score(step, tops):
            where = key_range(step)
            ok = (key_conv[:, where] == conv) & (key_row[:, where] <= number)
            held = pl.ds(pl.multiple_of(step * KEYS, KEYS), KEYS)
            new = []
            for head in range(kv_local):
                s = lax.dot_general(
                    heads[head], keys[head, where], (((1,), (1,)), ((), ())),
                    preferred_element_type=jnp.float32,
                ).reshape(group_size, TILE, KEYS)
                s = jnp.where(ok[None], s, HIDDEN).reshape(wide, KEYS)
                scores[head, :, held] = s
                top = tops[head]
                for k in range(0, KEYS, LANES):
                    top = jnp.maximum(top, s[:, k : k + LANES])
                new.append(top)
            return tuple(new)

        low = jnp.full((wide, LANES), HIDDEN, jnp.float32)
        tops = lax.fori_loop(0, steps_h + steps_f, score, (low,) * kv_local)
        tops = [jnp.max(top, axis=1, keepdims=True) * to_exp2 for top in tops]
        sums[...] = jnp.zeros_like(sums)

        def gather(step, carry):
            where = key_range(step)
            held = pl.ds(pl.multiple_of(step * KEYS, KEYS), KEYS)
            for head in range(kv_local):
                w = jnp.exp2(scores[head, :, held] * to_exp2 - tops[head]).astype(jnp.bfloat16)
                sums[head] += jnp.dot(w, values[head, where], preferred_element_type=jnp.float32)
            return carry

        lax.fori_loop(0, steps_h + steps_f, gather, 0)
        for head in range(kv_local):
            done = (sums[head, :, :HD] / sums[head, :, HD:]).astype(jnp.bfloat16)
            for g in range(group_size):
                at = (head * group_size + g) * HD
                out[control[2 + at // depth], leaving, at % depth : at % depth + HD] = done[
                    g * TILE : (g + 1) * TILE
                ]
        return carry

    lax.fori_loop(0, tiles, tile, 0)


def attend_tables(rows, slots, page_len, tok_conv, page_conv, page_fill):
    hist = slots * page_len
    fresh_base = hist + KEYS
    key_total = fresh_base + pl.cdiv(rows, KEYS) * KEYS + KEYS
    live = jnp.arange(page_len)[None, :] < page_fill[:, None]
    hist_conv = jnp.where(live, page_conv[:, None], -1).reshape(hist)
    tail = key_total - fresh_base - rows
    key_conv = jnp.concatenate(
        [hist_conv, jnp.full((KEYS,), -1, jnp.int32), tok_conv, jnp.full((tail,), -1, jnp.int32)]
    )[None]
    key_row = jnp.maximum(jnp.arange(key_total, dtype=jnp.int32) - fresh_base, -1)[None]
    lowest, highest = tok_conv[::TILE], tok_conv[TILE - 1 :: TILE]
    hist_at = jnp.sum(page_conv[None] < lowest[:, None], axis=1, dtype=jnp.int32) * page_len
    hist_at = hist_at // LANES * LANES
    hist_end = jnp.sum(page_conv[None] <= highest[:, None], axis=1, dtype=jnp.int32) * page_len
    hist_steps = (hist_end - hist_at + KEYS - 1) // KEYS
    fresh_at = jnp.sum(tok_conv[None] < lowest[:, None], axis=1, dtype=jnp.int32) // LANES * LANES
    fresh_end = (jnp.arange(rows // TILE, dtype=jnp.int32) + 1) * TILE
    fresh_steps = (fresh_end - fresh_at + KEYS - 1) // KEYS
    return key_conv, key_row, tok_conv[:, None], hist_at, hist_steps, fresh_at, fresh_steps


def attend(side, control, tables, queries, keys, values, slots):
    rows, width = queries.shape
    kv_local, key_total = keys.shape[:2]
    group_size = width // (kv_local * HD)
    key_conv, key_row, tok_conv, *steps = tables
    fresh_base = slots + KEYS
    most = slots // KEYS + pl.cdiv(rows, KEYS)
    smem = pl.BlockSpec(memory_space=pltpu.SMEM)
    vmem = pl.BlockSpec(memory_space=pltpu.VMEM)
    return pl.pallas_call(
        functools.partial(attend_kernel, fresh_base, side),
        out_shape=jax.ShapeDtypeStruct((4, rows // 2, width // 4), jnp.bfloat16),
        in_specs=[smem] * 5 + [vmem] * 6,
        out_specs=vmem,
        scratch_shapes=[
            pltpu.VMEM((kv_local, group_size * TILE, most * KEYS), jnp.float32),
            pltpu.VMEM((kv_local, group_size * TILE, 2 * HD), jnp.float32),
        ],
        compiler_params=pltpu.CompilerParams(vmem_limit_bytes=28 * MIB),
        cost_estimate=cost((16 - 15 * side) * 10**9),
        name="attend",
    )(control, *steps, queries, keys, values, key_conv, key_row, tok_conv)


def multiply(left, pieces, at):
    total = None
    for n, piece in enumerate(pieces):
        term = jnp.dot(left[n], piece[:, at], preferred_element_type=jnp.float32)
        total = term if total is None else total + term
    return total.astype(jnp.bfloat16)


def blocks(columns):
    cut = min(COLUMNS, columns)
    return [slice(k, min(k + cut, columns)) for k in range(0, columns, cut)]


def parts_of(control, refs):
    if len(refs) == 1:
        depth = refs[0].shape[0] // 4
        return [
            (0, [refs[0].at[pl.ds(pl.multiple_of(control[6 + n] * depth, depth), depth)] for n in range(4)])
        ]
    parts, first = [], 0
    for k in range(0, len(refs), 4):
        parts.append((first, refs[k : k + 4]))
        first += refs[k].shape[1]
    return parts


def project_kernel(control, left, *refs):
    for first, pieces in parts_of(control, refs[:-1]):
        for at in blocks(pieces[0].shape[1]):
            refs[-1][:, first + at.start : first + at.stop] = multiply(left, pieces, at)


def finish_kernel(has_out, control, left, came, *refs):
    for first, pieces in parts_of(control, refs[: len(refs) - 1 - has_out]):
        for at in blocks(pieces[0].shape[1]):
            to = slice(first + at.start, first + at.stop)
            total = multiply(left, pieces, at).astype(jnp.float32) + came[:, to].astype(jnp.float32)
            refs[-1][0, :, to] = total.astype(jnp.bfloat16)


def project(control, left, pieces, came=None, base=None, out=None, width=None):
    half = left.shape[1]
    columns = sum(piece.shape[1] for piece in pieces[::4])
    vmem = pl.BlockSpec(memory_space=pltpu.VMEM)
    in_specs = [vmem]
    operands = [left]
    aliases = {}
    if came is None:
        kernel = project_kernel
        out_shape = jax.ShapeDtypeStruct((half, columns), jnp.bfloat16)
        out_specs = vmem
    else:
        kernel = functools.partial(finish_kernel, int(out is not None))
        in_specs.append(vmem)
        operands.append(came)
        out_shape = jax.ShapeDtypeStruct((1, half, width), jnp.bfloat16)
        out_specs = pl.BlockSpec((1, half, columns), lambda j, control: (0, 0, control[base]))
    in_specs += [vmem] * len(pieces)
    operands += pieces
    if out is not None:
        in_specs.append(pl.BlockSpec(memory_space=pl.ANY))
        operands.append(out)
        aliases = {len(operands): 0}
    return pl.pallas_call(
        kernel,
        out_shape=out_shape,
        grid_spec=pltpu.PrefetchScalarGridSpec(
            num_scalar_prefetch=1, grid=(1,), in_specs=in_specs, out_specs=out_specs
        ),
        input_output_aliases=aliases,
        compiler_params=pltpu.CompilerParams(vmem_limit_bytes=16 * MIB),
        cost_estimate=cost(),
        name="project" if came is None else "finish",
    )(control, *operands)


def pick_kernel(asked, pool, out, sem):
    owners, bucket = asked.shape
    for owner in range(owners):

        def start(n, carry):
            pltpu.make_async_copy(pool.at[asked[owner, n]], out.at[owner, n], sem).start()
            return carry

        lax.fori_loop(0, bucket, start, 0, unroll=8)
    pltpu.make_async_copy(out, out, sem).wait()


def pick(pool, asked):
    hbm = pl.BlockSpec(memory_space=pltpu.HBM)
    return pl.pallas_call(
        pick_kernel,
        out_shape=jax.ShapeDtypeStruct(asked.shape + pool.shape[1:], jnp.bfloat16),
        in_specs=[pl.BlockSpec(memory_space=pltpu.SMEM), hbm],
        out_specs=hbm,
        scratch_shapes=[pltpu.SemaphoreType.DMA],
        cost_estimate=cost(),
        name="pick",
    )(asked, pool)


SWAP = [(0, 1), (1, 0)]


def after(value, *others):
    return lax.optimization_barrier((value,) + others)[0]


def shards(
    queries, new_kv, pool, out_weight, tok_conv, page_conv, page_fill, page_owner, page_index
):
    row_count = queries.shape[1]
    slot_count = page_owner.shape[1]
    owner_count = lax.axis_size("seq")
    tp_count = lax.axis_size("tp")
    bucket = 2 * slot_count // owner_count
    group, role, tp = lax.axis_index("group"), lax.axis_index("role"), lax.axis_index("tp")
    seq = lax.axis_index("seq")


    own = 2 * group + role
    depth = out_weight.shape[0] // 4
    columns = out_weight.shape[1]
    quarter = lax.dynamic_slice_in_dim(out_weight, own * depth, depth, 0)
    order = [q ^ own for q in range(4)]
    order = [(v % 2) * 2 + v // 2 for v in order]
    flip = tp if tp_count == 2 else 0
    second = jnp.where(seq < 2, 2, 1)
    third = jnp.where(seq < 2, 3, 0)
    local = [own, own ^ 2, own ^ 1, own ^ 3]
    control = jnp.stack(
        [jnp.asarray(v, jnp.int32) for v in (flip, 1 - flip, *order, *local, seq, seq ^ 1, second, 2 * third, 2 * third + 1)]
    )
    swap_group = functools.partial(lax.ppermute, axis_name="group", perm=SWAP)
    swap_role = functools.partial(lax.ppermute, axis_name="role", perm=SWAP)

    if owner_count == 4:
        middle = (seq == 1) | (seq == 2)
        cut, early = columns // 2, columns // LANES * 5 // 8 * LANES
        parts = [quarter[:, :early], quarter[:, early:]]
        pair = functools.partial(lax.ppermute, axis_name="seq", perm=[(0, 1), (1, 0), (2, 3), (3, 2)])
        cross = functools.partial(lax.ppermute, axis_name="seq", perm=[(1, 2), (2, 1)])
        forward = functools.partial(lax.ppermute, axis_name="seq", perm=[(1, 0), (2, 3)])
        near, inner = [pair(parts[0])], [cross(parts[0])]

    position, wanted = rank(page_owner, page_index, owner_count, bucket)
    asked = lax.all_to_all(wanted, "seq", split_axis=0, concat_axis=0, tiled=True)
    if owner_count == 4:
        near, inner = [after(near[0], asked)], [after(inner[0], asked)]
        later = after(parts[1], near[0], inner[0])
        near.append(pair(later))
        inner.append(cross(later))
        asked = after(asked, near[0], inner[0])
    found = pick(pool[0], asked)
    if owner_count == 4:
        near[1], inner[1] = after(near[1], found), after(inner[1], found)
        found = after(found, near[1], inner[1])
    pages = lax.all_to_all(found, "seq", split_axis=0, concat_axis=0, tiled=True)
    pages = pages.reshape((owner_count * bucket,) + found.shape[2:])
    slots = slot_count * pool.shape[3]
    fresh = new_kv[0].reshape(row_count, -1)
    tables = attend_tables(
        row_count, slot_count, pool.shape[3], tok_conv[0], page_conv[0], page_fill[0]
    )

    if owner_count != 4 or tp_count != 2:
        mine = lax.all_gather(quarter, "seq", axis=1, tiled=True)
        across = swap_group(mine)
        pieces = [mine, across, swap_role(mine), swap_role(across)]
        keys, values = place(position, pages, fresh)
        partial = [
            project(control, attend(side, control, tables, queries[0], keys, values, slots), pieces)
            for side in (0, 1)
        ]
        return lax.psum_scatter(
            jnp.concatenate(partial, axis=0), "tp", scatter_dimension=0, tiled=True
        )[None]

    swap_tp = functools.partial(lax.ppermute, axis_name="tp", perm=SWAP)

    def four(one, two, *hold):
        return [one, two, swap_role(after(one, *hold)), swap_role(after(two, *hold))]

    near_across = [swap_group(part) for part in near]
    next_shard = [jnp.where(middle, part, forward(part)) for part in inner]
    next_across = [swap_group(part) for part in next_shard]
    near_all = four(near[0], near_across[0]) + four(near[1], near_across[1])
    next_all = four(next_shard[0], next_across[0]) + four(next_shard[1], next_across[1])
    far = [near[0][:, :cut], jnp.concatenate([near[0][:, cut:], near[1]], axis=1)]
    far = [cross(after(part, *next_across)) for part in far]

    keys, values = place(position, after(pages, *near_all, *next_all), fresh)
    left = attend(1, control, tables, queries[0], keys, values, slots)
    far_on = [forward(after(far[0], left))]
    sent = [project(control, left, [out_weight])]
    far_on.append(forward(after(far[1], sent[0])))
    sent.append(project(control, after(left, sent[-1]), near_all))
    far[0] = jnp.where(middle, far[0], after(far_on[0], sent[1]))
    far_across = [swap_group(far[0])]
    sent.append(project(control, after(left, sent[-1]), next_all))
    came = [swap_tp(each) for each in sent]
    stay = attend(0, control, tables, after(queries[0], sent[2], far[0]), keys, values, slots)
    far[1] = jnp.where(middle, far[1], after(far_on[1], stay))
    far_across.append(swap_group(far[1]))
    far_all = [four(far[0], far_across[0], stay)]
    total = columns * owner_count
    out = project(control, after(stay, *came[:2]), [out_weight], came[0], 10, None, total)
    out = project(control, stay, near_all, came[1], 11, out, total)
    out = project(control, stay, next_all, came[2], 12, out, total)
    sent.append(project(control, after(left, out), far_all[0]))
    came.append(swap_tp(sent[3]))
    far_all.append(four(far[1], far_across[1], sent[3]))
    sent.append(project(control, left, far_all[1]))
    came.append(swap_tp(sent[4]))
    out = project(control, after(stay, sent[4]), far_all[0], came[3], 13, out, total)
    return project(control, stay, far_all[1], came[4], 14, out, total)


def solution(mesh):
    return jax.shard_map(
        shards,
        mesh=mesh,
        in_specs=(
            P("role", ("group", "seq"), "tp"),
            P("role", ("group", "seq"), None, "tp"),
            P("role", ("group", "seq"), None, None, "tp"),
            P("tp", "seq"),
            P("role", ("group", "seq")),
            P("role", ("group", "seq")),
            P("role", ("group", "seq")),
            P("role", ("group", "seq")),
            P("role", ("group", "seq")),
        ),
        out_specs=P("role", ("group", "seq", "tp"), None),
        check_vma=False,
    )
```

```python
import functools
import math

import jax
import jax.numpy as jnp
from jax import lax
from jax.experimental import pallas as pl
from jax.experimental.pallas import tpu as pltpu
from jax.sharding import PartitionSpec as P

HD = 128
TILE = 64
KEYS = 256
LANES = 128
HIDDEN = -1e30
COLUMNS = 256
MIB = 1024 * 1024


def cost(flops=3 * 10**9):
    return pl.CostEstimate(flops=flops, bytes_accessed=1000, transcendentals=0)


def rank_kernel(owner, page, position, wanted, count):
    owners, bucket = wanted.shape
    for n in range(owners):
        count[n] = 0

    def clear(k, carry):
        for n in range(owners):
            wanted[n, k] = 0
        return carry

    lax.fori_loop(0, bucket, clear, 0)

    def put(slot, carry):
        to = owner[0, slot]
        rank = count[to]
        count[to] = rank + 1
        wanted[to, rank] = page[0, slot]
        position[slot] = to * bucket + rank
        return carry

    lax.fori_loop(0, owner.shape[1], put, 0, unroll=4)


def rank(page_owner, page_index, owners, bucket):
    smem = pl.BlockSpec(memory_space=pltpu.SMEM)
    return pl.pallas_call(
        rank_kernel,
        out_shape=(
            jax.ShapeDtypeStruct((page_owner.shape[1],), jnp.int32),
            jax.ShapeDtypeStruct((owners, bucket), jnp.int32),
        ),
        in_specs=[smem, smem],
        out_specs=(smem, smem),
        scratch_shapes=[pltpu.SMEM((owners,), jnp.int32)],
        cost_estimate=cost(),
        name="rank",
    )(page_owner, page_index)


def place_kernel(position, pages, fresh, keys, values):
    kv_local, key_total = keys.shape[:2]
    slots, page_len, rows = position.shape[0], pages.shape[2], fresh.shape[0]
    channels = kv_local * HD
    hist = slots * page_len
    fresh_base = hist + KEYS
    for head in range(kv_local):
        values[head, :, HD:] = jnp.ones((key_total, HD), jnp.bfloat16)
        for first, last in ((hist, fresh_base), (fresh_base + rows, key_total)):
            keys[head, first:last] = jnp.zeros((last - first, HD), jnp.bfloat16)
            values[head, first:last, :HD] = jnp.zeros((last - first, HD), jnp.bfloat16)
        at = head * HD
        keys[head, fresh_base : fresh_base + rows] = fresh[:, at : at + HD]
        values[head, fresh_base : fresh_base + rows, :HD] = fresh[:, channels + at : channels + at + HD]

    def place(slot, carry):
        page = position[slot]
        row = pl.ds(pl.multiple_of(slot * page_len, page_len), page_len)
        for head in range(kv_local):
            at = head * HD
            keys[head, row] = pages[page, 0, :, at : at + HD]
            values[head, row, :HD] = pages[page, 1, :, at : at + HD]
        return carry

    lax.fori_loop(0, slots, place, 0, unroll=8)


def place(position, pages, fresh):
    kv_local = pages.shape[3] // HD
    rows = fresh.shape[0]
    key_total = position.shape[0] * pages.shape[2] + KEYS + pl.cdiv(rows, KEYS) * KEYS + KEYS
    vmem = pl.BlockSpec(memory_space=pltpu.VMEM)
    return pl.pallas_call(
        place_kernel,
        out_shape=(
            jax.ShapeDtypeStruct((kv_local, key_total, HD), jnp.bfloat16),
            jax.ShapeDtypeStruct((kv_local, key_total, 2 * HD), jnp.bfloat16),
        ),
        in_specs=[pl.BlockSpec(memory_space=pltpu.SMEM), vmem, vmem],
        out_specs=(vmem, vmem),
        compiler_params=pltpu.CompilerParams(vmem_limit_bytes=20 * MIB),
        cost_estimate=cost(10**9),
        name="place",
    )(position, pages, fresh)


def attend_kernel(
    fresh_base, side, control, hist_at, hist_steps, fresh_at, fresh_steps,
    query, keys, values, key_conv, key_row, tok_conv, out, scores, sums,
):
    kv_local = keys.shape[0]
    group_size = query.shape[1] // (kv_local * HD)
    half, depth = out.shape[1], out.shape[2]
    tiles = half // TILE
    to_exp2 = math.log2(math.e) / math.sqrt(HD)
    wide = group_size * TILE

    def tile(number_here, carry):
        index = control[side] * tiles + number_here
        first = pl.multiple_of(index * TILE, TILE)
        leaving = pl.ds(pl.multiple_of(number_here * TILE, TILE), TILE)
        tokens = pl.ds(first, TILE)
        conv = tok_conv[tokens]
        number = first + lax.broadcasted_iota(jnp.int32, (TILE, 1), 0)
        steps_h, steps_f = hist_steps[index], fresh_steps[index]
        at_h, at_f = hist_at[index], fresh_at[index]
        heads = [
            jnp.concatenate(
                [
                    query[tokens, (head * group_size + g) * HD : (head * group_size + g + 1) * HD]
                    for g in range(group_size)
                ],
                axis=0,
            )
            for head in range(kv_local)
        ]

        def key_range(step):
            start = jnp.where(
                step < steps_h, at_h + step * KEYS, fresh_base + at_f + (step - steps_h) * KEYS
            )
            return pl.ds(pl.multiple_of(start, LANES), KEYS)

        def score(step, tops):
            where = key_range(step)
            ok = (key_conv[:, where] == conv) & (key_row[:, where] <= number)
            held = pl.ds(pl.multiple_of(step * KEYS, KEYS), KEYS)
            new = []
            for head in range(kv_local):
                s = lax.dot_general(
                    heads[head], keys[head, where], (((1,), (1,)), ((), ())),
                    preferred_element_type=jnp.float32,
                ).reshape(group_size, TILE, KEYS)
                s = jnp.where(ok[None], s, HIDDEN).reshape(wide, KEYS)
                scores[head, :, held] = s
                top = tops[head]
                for k in range(0, KEYS, LANES):
                    top = jnp.maximum(top, s[:, k : k + LANES])
                new.append(top)
            return tuple(new)

        low = jnp.full((wide, LANES), HIDDEN, jnp.float32)
        tops = lax.fori_loop(0, steps_h + steps_f, score, (low,) * kv_local)
        tops = [jnp.max(top, axis=1, keepdims=True) * to_exp2 for top in tops]
        sums[...] = jnp.zeros_like(sums)

        def gather(step, carry):
            where = key_range(step)
            held = pl.ds(pl.multiple_of(step * KEYS, KEYS), KEYS)
            for head in range(kv_local):
                w = jnp.exp2(scores[head, :, held] * to_exp2 - tops[head]).astype(jnp.bfloat16)
                sums[head] += jnp.dot(w, values[head, where], preferred_element_type=jnp.float32)
            return carry

        lax.fori_loop(0, steps_h + steps_f, gather, 0)
        for head in range(kv_local):
            done = (sums[head, :, :HD] / sums[head, :, HD:]).astype(jnp.bfloat16)
            for g in range(group_size):
                at = (head * group_size + g) * HD
                out[control[2 + at // depth], leaving, at % depth : at % depth + HD] = done[
                    g * TILE : (g + 1) * TILE
                ]
        return carry

    lax.fori_loop(0, tiles, tile, 0)


def attend_tables(rows, slots, page_len, tok_conv, page_conv, page_fill):
    hist = slots * page_len
    fresh_base = hist + KEYS
    key_total = fresh_base + pl.cdiv(rows, KEYS) * KEYS + KEYS
    live = jnp.arange(page_len)[None, :] < page_fill[:, None]
    hist_conv = jnp.where(live, page_conv[:, None], -1).reshape(hist)
    tail = key_total - fresh_base - rows
    key_conv = jnp.concatenate(
        [hist_conv, jnp.full((KEYS,), -1, jnp.int32), tok_conv, jnp.full((tail,), -1, jnp.int32)]
    )[None]
    key_row = jnp.maximum(jnp.arange(key_total, dtype=jnp.int32) - fresh_base, -1)[None]
    lowest, highest = tok_conv[::TILE], tok_conv[TILE - 1 :: TILE]
    hist_at = jnp.sum(page_conv[None] < lowest[:, None], axis=1, dtype=jnp.int32) * page_len
    hist_at = hist_at // LANES * LANES
    hist_end = jnp.sum(page_conv[None] <= highest[:, None], axis=1, dtype=jnp.int32) * page_len
    hist_steps = (hist_end - hist_at + KEYS - 1) // KEYS
    fresh_at = jnp.sum(tok_conv[None] < lowest[:, None], axis=1, dtype=jnp.int32) // LANES * LANES
    fresh_end = (jnp.arange(rows // TILE, dtype=jnp.int32) + 1) * TILE
    fresh_steps = (fresh_end - fresh_at + KEYS - 1) // KEYS
    return key_conv, key_row, tok_conv[:, None], hist_at, hist_steps, fresh_at, fresh_steps


def attend(side, control, tables, queries, keys, values, slots):
    rows, width = queries.shape
    kv_local, key_total = keys.shape[:2]
    group_size = width // (kv_local * HD)
    key_conv, key_row, tok_conv, *steps = tables
    fresh_base = slots + KEYS
    most = slots // KEYS + pl.cdiv(rows, KEYS)
    smem = pl.BlockSpec(memory_space=pltpu.SMEM)
    vmem = pl.BlockSpec(memory_space=pltpu.VMEM)
    return pl.pallas_call(
        functools.partial(attend_kernel, fresh_base, side),
        out_shape=jax.ShapeDtypeStruct((4, rows // 2, width // 4), jnp.bfloat16),
        in_specs=[smem] * 5 + [vmem] * 6,
        out_specs=vmem,
        scratch_shapes=[
            pltpu.VMEM((kv_local, group_size * TILE, most * KEYS), jnp.float32),
            pltpu.VMEM((kv_local, group_size * TILE, 2 * HD), jnp.float32),
        ],
        compiler_params=pltpu.CompilerParams(vmem_limit_bytes=28 * MIB),
        cost_estimate=cost((16 - 15 * side) * 10**9),
        name="attend",
    )(control, *steps, queries, keys, values, key_conv, key_row, tok_conv)


def multiply(left, pieces, at):
    total = None
    for n, piece in enumerate(pieces):
        term = jnp.dot(left[n], piece[:, at], preferred_element_type=jnp.float32)
        total = term if total is None else total + term
    return total.astype(jnp.bfloat16)


def blocks(columns):
    cut = min(COLUMNS, columns)
    return [slice(k, k + cut) for k in range(0, columns, cut)]


def parts_of(control, refs):
    if len(refs) == 1:
        depth = refs[0].shape[0] // 4
        return [
            (0, [refs[0].at[pl.ds(pl.multiple_of(control[6 + n] * depth, depth), depth)] for n in range(4)])
        ]
    columns = refs[0].shape[1]
    return [(k // 4 * columns, refs[k : k + 4]) for k in range(0, len(refs), 4)]


def project_kernel(control, left, *refs):
    for first, pieces in parts_of(control, refs[:-1]):
        for at in blocks(pieces[0].shape[1]):
            refs[-1][:, first + at.start : first + at.stop] = multiply(left, pieces, at)


def project_both_kernel(control, left, stay, *refs):
    sent, kept = refs[-2:]
    half = left.shape[1]
    for first, pieces in parts_of(control, refs[:-2]):
        for at in blocks(pieces[0].shape[1]):
            total = multiply([jnp.concatenate([left[n], stay[n]], axis=0) for n in range(4)], pieces, at)
            to = slice(first + at.start, first + at.stop)
            sent[:, to] = total[:half]
            kept[:, to] = total[half:]


def project(control, left, pieces, stay=None):
    half = left.shape[1]
    columns = pieces[0].shape[1] * max(1, len(pieces) // 4)
    smem = pl.BlockSpec(memory_space=pltpu.SMEM)
    vmem = pl.BlockSpec(memory_space=pltpu.VMEM)
    shape = jax.ShapeDtypeStruct((half, columns), jnp.bfloat16)
    rows = [left] if stay is None else [left, stay]
    return pl.pallas_call(
        project_kernel if stay is None else project_both_kernel,
        out_shape=shape if stay is None else (shape, shape),
        in_specs=[smem] + [vmem] * (len(rows) + len(pieces)),
        out_specs=vmem if stay is None else (vmem, vmem),
        compiler_params=pltpu.CompilerParams(vmem_limit_bytes=16 * MIB),
        cost_estimate=cost((3 if stay is None else 6) * 10**9),
        name="project",
    )(control, *rows, *pieces)


def join_kernel(count, control, *refs):
    out = refs[-1]
    for n in range(count):
        kept, came = refs[n], refs[count + n]
        columns = kept.shape[1]
        to = pl.ds(pl.multiple_of(control[10 + n] * LANES, LANES), columns)
        total = kept[...].astype(jnp.float32) + came[...].astype(jnp.float32)
        out[0, :, to] = total.astype(jnp.bfloat16)


def join(control, kept, came):
    smem = pl.BlockSpec(memory_space=pltpu.SMEM)
    vmem = pl.BlockSpec(memory_space=pltpu.VMEM)
    total = sum(part.shape[1] for part in kept)
    return pl.pallas_call(
        functools.partial(join_kernel, len(kept)),
        out_shape=jax.ShapeDtypeStruct((1, kept[0].shape[0], total), jnp.bfloat16),
        in_specs=[smem] + [vmem] * (2 * len(kept)),
        out_specs=vmem,
        compiler_params=pltpu.CompilerParams(vmem_limit_bytes=16 * MIB),
        cost_estimate=cost(3 * 10**8),
        name="join",
    )(control, *kept, *came)


def pick_kernel(asked, pool, out, held, rows, sem):
    owners, bucket = asked.shape
    whole = pltpu.make_async_copy(pool, held, sem.at[owners])
    whole.start()
    whole.wait()
    for owner in range(owners):

        def copy(n, carry):
            rows[owner, n] = held[asked[owner, n]]
            return carry

        lax.fori_loop(0, bucket, copy, 0, unroll=8)
        pltpu.make_async_copy(rows.at[owner], out.at[owner], sem.at[owner]).start()
    for owner in range(owners):
        pltpu.make_async_copy(rows.at[owner], out.at[owner], sem.at[owner]).wait()


def pick(pool, asked):
    hbm = pl.BlockSpec(memory_space=pltpu.HBM)
    out = asked.shape + pool.shape[1:]
    return pl.pallas_call(
        pick_kernel,
        out_shape=jax.ShapeDtypeStruct(out, jnp.bfloat16),
        in_specs=[pl.BlockSpec(memory_space=pltpu.SMEM), hbm],
        out_specs=hbm,
        scratch_shapes=[
            pltpu.VMEM(pool.shape, jnp.bfloat16),
            pltpu.VMEM(out, jnp.bfloat16),
            pltpu.SemaphoreType.DMA((asked.shape[0] + 1,)),
        ],
        compiler_params=pltpu.CompilerParams(vmem_limit_bytes=12 * MIB),
        cost_estimate=cost(),
        name="pick",
    )(asked, pool)


SWAP = [(0, 1), (1, 0)]


def after(value, *others):
    return lax.optimization_barrier((value,) + others)[0]


def shards(
    queries, new_kv, pool, out_weight, tok_conv, page_conv, page_fill, page_owner, page_index
):
    row_count = queries.shape[1]
    slot_count = page_owner.shape[1]
    owner_count = lax.axis_size("seq")
    tp_count = lax.axis_size("tp")
    bucket = 2 * slot_count // owner_count
    group, role, tp = lax.axis_index("group"), lax.axis_index("role"), lax.axis_index("tp")
    seq = lax.axis_index("seq")


    own = 2 * group + role
    depth = out_weight.shape[0] // 4
    columns = out_weight.shape[1]
    quarter = lax.dynamic_slice_in_dim(out_weight, own * depth, depth, 0)
    order = [q ^ own for q in range(4)]
    order = [(v % 2) * 2 + v // 2 for v in order]
    flip = tp if tp_count == 2 else 0
    second = jnp.where(seq < 2, 2, 1)
    third = jnp.where(seq < 2, 3, 0)
    local = [own, own ^ 2, own ^ 1, own ^ 3]
    begins = [v * columns // LANES for v in (seq, seq ^ 1, second, third)]
    begins.append(begins[-1] + columns // 2 // LANES)
    control = jnp.stack(
        [jnp.asarray(v, jnp.int32) for v in (flip, 1 - flip, *order, *local, *begins)]
    )
    swap_group = functools.partial(lax.ppermute, axis_name="group", perm=SWAP)
    swap_role = functools.partial(lax.ppermute, axis_name="role", perm=SWAP)

    if owner_count == 4:
        middle = (seq == 1) | (seq == 2)
        cut = columns // 2
        parts = [quarter[:, :cut], quarter[:, cut:]]
        pair = functools.partial(lax.ppermute, axis_name="seq", perm=[(0, 1), (1, 0), (2, 3), (3, 2)])
        cross = functools.partial(lax.ppermute, axis_name="seq", perm=[(1, 2), (2, 1)])
        forward = functools.partial(lax.ppermute, axis_name="seq", perm=[(1, 0), (2, 3)])
        near, inner = [pair(parts[0])], [cross(parts[0])]

    position, wanted = rank(page_owner, page_index, owner_count, bucket)
    asked = lax.all_to_all(wanted, "seq", split_axis=0, concat_axis=0, tiled=True)
    if owner_count == 4:
        near, inner = [after(near[0], asked)], [after(inner[0], asked)]
        later = after(parts[1], near[0], inner[0])
        near.append(pair(later))
        inner.append(cross(later))
        asked = after(asked, near[0], inner[0])
    found = pick(pool[0], asked)
    if owner_count == 4:
        near[1], inner[1] = after(near[1], found), after(inner[1], found)
        found = after(found, near[1], inner[1])
    pages = lax.all_to_all(found, "seq", split_axis=0, concat_axis=0, tiled=True)
    pages = pages.reshape((owner_count * bucket,) + found.shape[2:])
    slots = slot_count * pool.shape[3]
    fresh = new_kv[0].reshape(row_count, -1)
    tables = attend_tables(
        row_count, slot_count, pool.shape[3], tok_conv[0], page_conv[0], page_fill[0]
    )

    if owner_count != 4 or tp_count != 2:
        mine = lax.all_gather(quarter, "seq", axis=1, tiled=True)
        across = swap_group(mine)
        pieces = [mine, across, swap_role(mine), swap_role(across)]
        keys, values = place(position, pages, fresh)
        partial = [
            project(control, attend(side, control, tables, queries[0], keys, values, slots), pieces)
            for side in (0, 1)
        ]
        return lax.psum_scatter(
            jnp.concatenate(partial, axis=0), "tp", scatter_dimension=0, tiled=True
        )[None]

    swap_tp = functools.partial(lax.ppermute, axis_name="tp", perm=SWAP)

    def four(one, two, *hold):
        return [one, two, swap_role(after(one, *hold)), swap_role(after(two, *hold))]

    near_across = [swap_group(part) for part in near]
    next_shard = [jnp.where(middle, part, forward(part)) for part in inner]
    next_across = [swap_group(part) for part in next_shard]
    near_all = four(near[0], near_across[0]) + four(near[1], near_across[1])
    next_all = four(next_shard[0], next_across[0]) + four(next_shard[1], next_across[1])
    far = [cross(after(part, *next_across)) for part in near]

    keys, values = place(position, after(pages, *near_all, *next_all), fresh)
    left = attend(1, control, tables, queries[0], keys, values, slots)
    far_on = [forward(after(far[0], left))]
    sent, kept = [project(control, left, [out_weight])], []
    came = [swap_tp(sent[0])]
    stay = attend(0, control, tables, after(queries[0], sent[0], far[0]), keys, values, slots)
    far_on.append(forward(after(far[1], stay)))
    far[0] = jnp.where(middle, far[0], after(far_on[0], stay))
    far_across = [swap_group(far[0])]
    for pieces in (near_all, next_all):
        both = project(control, after(left, far[0], came[0], *sent), pieces, stay)
        sent.append(both[0])
        kept.append(both[1])
        came.append(swap_tp(sent[-1]))
    far[1] = jnp.where(middle, far[1], after(far_on[1], sent[2]))
    far_across.append(swap_group(far[1]))
    kept.insert(0, project(control, after(stay, sent[2], came[1], far_across[0]), [out_weight]))
    for n in range(2):
        pieces = four(far[n], far_across[n], *sent[3:])
        both = project(control, after(left, kept[0], *came[2 : 2 + 2 * n]), pieces, stay)
        sent.append(both[0])
        kept.append(both[1])
        came.append(swap_tp(sent[-1]))
    return join(control, kept, came)


def solution(mesh):
    return jax.shard_map(
        shards,
        mesh=mesh,
        in_specs=(
            P("role", ("group", "seq"), "tp"),
            P("role", ("group", "seq"), None, "tp"),
            P("role", ("group", "seq"), None, None, "tp"),
            P("tp", "seq"),
            P("role", ("group", "seq")),
            P("role", ("group", "seq")),
            P("role", ("group", "seq")),
            P("role", ("group", "seq")),
            P("role", ("group", "seq")),
        ),
        out_specs=P("role", ("group", "seq", "tp"), None),
        check_vma=False,
    )
```

```python
import functools
import math

import jax
import jax.numpy as jnp
from jax import lax
from jax.experimental import pallas as pl
from jax.experimental.pallas import tpu as pltpu
from jax.sharding import PartitionSpec as P

HD = 128
TILE = 64
KEYS = 256
LANES = 128
HIDDEN = -1e30
COLUMNS = 256
MIB = 1024 * 1024


def cost(flops=3 * 10**9):
    return pl.CostEstimate(flops=flops, bytes_accessed=1000, transcendentals=0)


def rank_kernel(owner, page, position, wanted, count):
    owners, bucket = wanted.shape
    for n in range(owners):
        count[n] = 0

    def clear(k, carry):
        for n in range(owners):
            wanted[n, k] = 0
        return carry

    lax.fori_loop(0, bucket, clear, 0)

    def put(slot, carry):
        to = owner[0, slot]
        rank = count[to]
        count[to] = rank + 1
        wanted[to, rank] = page[0, slot]
        position[slot] = to * bucket + rank
        return carry

    lax.fori_loop(0, owner.shape[1], put, 0, unroll=4)


def rank(page_owner, page_index, owners, bucket):
    smem = pl.BlockSpec(memory_space=pltpu.SMEM)
    return pl.pallas_call(
        rank_kernel,
        out_shape=(
            jax.ShapeDtypeStruct((page_owner.shape[1],), jnp.int32),
            jax.ShapeDtypeStruct((owners, bucket), jnp.int32),
        ),
        in_specs=[smem, smem],
        out_specs=(smem, smem),
        scratch_shapes=[pltpu.SMEM((owners,), jnp.int32)],
        cost_estimate=cost(),
        name="rank",
    )(page_owner, page_index)


def place_kernel(position, pages, fresh, keys, values):
    kv_local, key_total = keys.shape[:2]
    slots, page_len, rows = position.shape[0], pages.shape[2], fresh.shape[0]
    channels = kv_local * HD
    hist = slots * page_len
    fresh_base = hist + KEYS
    for head in range(kv_local):
        values[head, :, HD:] = jnp.ones((key_total, HD), jnp.bfloat16)
        for first, last in ((hist, fresh_base), (fresh_base + rows, key_total)):
            keys[head, first:last] = jnp.zeros((last - first, HD), jnp.bfloat16)
            values[head, first:last, :HD] = jnp.zeros((last - first, HD), jnp.bfloat16)
        at = head * HD
        keys[head, fresh_base : fresh_base + rows] = fresh[:, at : at + HD]
        values[head, fresh_base : fresh_base + rows, :HD] = fresh[:, channels + at : channels + at + HD]

    def place(slot, carry):
        page = position[slot]
        row = pl.ds(pl.multiple_of(slot * page_len, page_len), page_len)
        for head in range(kv_local):
            at = head * HD
            keys[head, row] = pages[page, 0, :, at : at + HD]
            values[head, row, :HD] = pages[page, 1, :, at : at + HD]
        return carry

    lax.fori_loop(0, slots, place, 0, unroll=8)


def place(position, pages, fresh):
    kv_local = pages.shape[3] // HD
    rows = fresh.shape[0]
    key_total = position.shape[0] * pages.shape[2] + KEYS + pl.cdiv(rows, KEYS) * KEYS + KEYS
    vmem = pl.BlockSpec(memory_space=pltpu.VMEM)
    return pl.pallas_call(
        place_kernel,
        out_shape=(
            jax.ShapeDtypeStruct((kv_local, key_total, HD), jnp.bfloat16),
            jax.ShapeDtypeStruct((kv_local, key_total, 2 * HD), jnp.bfloat16),
        ),
        in_specs=[pl.BlockSpec(memory_space=pltpu.SMEM), vmem, vmem],
        out_specs=(vmem, vmem),
        compiler_params=pltpu.CompilerParams(vmem_limit_bytes=20 * MIB),
        cost_estimate=cost(10**9),
        name="place",
    )(position, pages, fresh)


def attend_kernel(
    fresh_base, side, control, hist_at, hist_steps, fresh_at, fresh_steps,
    query, keys, values, key_conv, key_row, tok_conv, out, scores, sums,
):
    kv_local = keys.shape[0]
    group_size = query.shape[1] // (kv_local * HD)
    half, depth = out.shape[1], out.shape[2]
    tiles = half // TILE
    to_exp2 = math.log2(math.e) / math.sqrt(HD)
    wide = group_size * TILE

    def tile(number_here, carry):
        index = control[side] * tiles + number_here
        first = pl.multiple_of(index * TILE, TILE)
        leaving = pl.ds(pl.multiple_of(number_here * TILE, TILE), TILE)
        tokens = pl.ds(first, TILE)
        conv = tok_conv[tokens]
        number = first + lax.broadcasted_iota(jnp.int32, (TILE, 1), 0)
        steps_h, steps_f = hist_steps[index], fresh_steps[index]
        at_h, at_f = hist_at[index], fresh_at[index]
        heads = [
            jnp.concatenate(
                [
                    query[tokens, (head * group_size + g) * HD : (head * group_size + g + 1) * HD]
                    for g in range(group_size)
                ],
                axis=0,
            )
            for head in range(kv_local)
        ]

        def key_range(step):
            start = jnp.where(
                step < steps_h, at_h + step * KEYS, fresh_base + at_f + (step - steps_h) * KEYS
            )
            return pl.ds(pl.multiple_of(start, LANES), KEYS)

        def score(step, tops):
            where = key_range(step)
            ok = (key_conv[:, where] == conv) & (key_row[:, where] <= number)
            held = pl.ds(pl.multiple_of(step * KEYS, KEYS), KEYS)
            new = []
            for head in range(kv_local):
                s = lax.dot_general(
                    heads[head], keys[head, where], (((1,), (1,)), ((), ())),
                    preferred_element_type=jnp.float32,
                ).reshape(group_size, TILE, KEYS)
                s = jnp.where(ok[None], s, HIDDEN).reshape(wide, KEYS)
                scores[head, :, held] = s
                top = tops[head]
                for k in range(0, KEYS, LANES):
                    top = jnp.maximum(top, s[:, k : k + LANES])
                new.append(top)
            return tuple(new)

        low = jnp.full((wide, LANES), HIDDEN, jnp.float32)
        tops = lax.fori_loop(0, steps_h + steps_f, score, (low,) * kv_local)
        tops = [jnp.max(top, axis=1, keepdims=True) * to_exp2 for top in tops]
        sums[...] = jnp.zeros_like(sums)

        def gather(step, carry):
            where = key_range(step)
            held = pl.ds(pl.multiple_of(step * KEYS, KEYS), KEYS)
            for head in range(kv_local):
                w = jnp.exp2(scores[head, :, held] * to_exp2 - tops[head]).astype(jnp.bfloat16)
                sums[head] += jnp.dot(w, values[head, where], preferred_element_type=jnp.float32)
            return carry

        lax.fori_loop(0, steps_h + steps_f, gather, 0)
        for head in range(kv_local):
            done = (sums[head, :, :HD] / sums[head, :, HD:]).astype(jnp.bfloat16)
            for g in range(group_size):
                at = (head * group_size + g) * HD
                out[control[2 + at // depth], leaving, at % depth : at % depth + HD] = done[
                    g * TILE : (g + 1) * TILE
                ]
        return carry

    lax.fori_loop(0, tiles, tile, 0)


def attend_tables(rows, slots, page_len, tok_conv, page_conv, page_fill):
    hist = slots * page_len
    fresh_base = hist + KEYS
    key_total = fresh_base + pl.cdiv(rows, KEYS) * KEYS + KEYS
    live = jnp.arange(page_len)[None, :] < page_fill[:, None]
    hist_conv = jnp.where(live, page_conv[:, None], -1).reshape(hist)
    tail = key_total - fresh_base - rows
    key_conv = jnp.concatenate(
        [hist_conv, jnp.full((KEYS,), -1, jnp.int32), tok_conv, jnp.full((tail,), -1, jnp.int32)]
    )[None]
    key_row = jnp.maximum(jnp.arange(key_total, dtype=jnp.int32) - fresh_base, -1)[None]
    lowest, highest = tok_conv[::TILE], tok_conv[TILE - 1 :: TILE]
    hist_at = jnp.sum(page_conv[None] < lowest[:, None], axis=1, dtype=jnp.int32) * page_len
    hist_at = hist_at // LANES * LANES
    hist_end = jnp.sum(page_conv[None] <= highest[:, None], axis=1, dtype=jnp.int32) * page_len
    hist_steps = (hist_end - hist_at + KEYS - 1) // KEYS
    fresh_at = jnp.sum(tok_conv[None] < lowest[:, None], axis=1, dtype=jnp.int32) // LANES * LANES
    fresh_end = (jnp.arange(rows // TILE, dtype=jnp.int32) + 1) * TILE
    fresh_steps = (fresh_end - fresh_at + KEYS - 1) // KEYS
    return key_conv, key_row, tok_conv[:, None], hist_at, hist_steps, fresh_at, fresh_steps


def attend(side, control, tables, queries, keys, values, slots):
    rows, width = queries.shape
    kv_local, key_total = keys.shape[:2]
    group_size = width // (kv_local * HD)
    key_conv, key_row, tok_conv, *steps = tables
    fresh_base = slots + KEYS
    most = slots // KEYS + pl.cdiv(rows, KEYS)
    smem = pl.BlockSpec(memory_space=pltpu.SMEM)
    vmem = pl.BlockSpec(memory_space=pltpu.VMEM)
    return pl.pallas_call(
        functools.partial(attend_kernel, fresh_base, side),
        out_shape=jax.ShapeDtypeStruct((4, rows // 2, width // 4), jnp.bfloat16),
        in_specs=[smem] * 5 + [vmem] * 6,
        out_specs=vmem,
        scratch_shapes=[
            pltpu.VMEM((kv_local, group_size * TILE, most * KEYS), jnp.float32),
            pltpu.VMEM((kv_local, group_size * TILE, 2 * HD), jnp.float32),
        ],
        compiler_params=pltpu.CompilerParams(vmem_limit_bytes=28 * MIB),
        cost_estimate=cost((16 - 15 * side) * 10**9),
        name="attend",
    )(control, *steps, queries, keys, values, key_conv, key_row, tok_conv)


def multiply(left, pieces, at):
    total = None
    for n, piece in enumerate(pieces):
        term = jnp.dot(left[n], piece[:, at], preferred_element_type=jnp.float32)
        total = term if total is None else total + term
    return total.astype(jnp.bfloat16)


def blocks(columns):
    cut = min(COLUMNS, columns)
    return [slice(k, k + cut) for k in range(0, columns, cut)]


def parts_of(control, refs):
    if len(refs) == 1:
        depth = refs[0].shape[0] // 4
        return [
            (0, [refs[0].at[pl.ds(pl.multiple_of(control[6 + n] * depth, depth), depth)] for n in range(4)])
        ]
    columns = refs[0].shape[1]
    return [(k // 4 * columns, refs[k : k + 4]) for k in range(0, len(refs), 4)]


def project_kernel(control, left, *refs):
    for first, pieces in parts_of(control, refs[:-1]):
        for at in blocks(pieces[0].shape[1]):
            refs[-1][:, first + at.start : first + at.stop] = multiply(left, pieces, at)


def project_both_kernel(control, left, stay, *refs):
    sent, kept = refs[-2:]
    half = left.shape[1]
    for first, pieces in parts_of(control, refs[:-2]):
        for at in blocks(pieces[0].shape[1]):
            total = multiply([jnp.concatenate([left[n], stay[n]], axis=0) for n in range(4)], pieces, at)
            to = slice(first + at.start, first + at.stop)
            sent[:, to] = total[:half]
            kept[:, to] = total[half:]


def project(control, left, pieces, stay=None):
    half = left.shape[1]
    columns = pieces[0].shape[1] * max(1, len(pieces) // 4)
    smem = pl.BlockSpec(memory_space=pltpu.SMEM)
    vmem = pl.BlockSpec(memory_space=pltpu.VMEM)
    shape = jax.ShapeDtypeStruct((half, columns), jnp.bfloat16)
    rows = [left] if stay is None else [left, stay]
    return pl.pallas_call(
        project_kernel if stay is None else project_both_kernel,
        out_shape=shape if stay is None else (shape, shape),
        in_specs=[smem] + [vmem] * (len(rows) + len(pieces)),
        out_specs=vmem if stay is None else (vmem, vmem),
        compiler_params=pltpu.CompilerParams(vmem_limit_bytes=16 * MIB),
        cost_estimate=cost((3 if stay is None else 6) * 10**9),
        name="project",
    )(control, *rows, *pieces)


def join_kernel(count, control, *refs):
    out = refs[-1]
    for n in range(count):
        kept, came = refs[n], refs[count + n]
        columns = kept.shape[1]
        to = pl.ds(pl.multiple_of(control[10 + n] * LANES, LANES), columns)
        total = kept[...].astype(jnp.float32) + came[...].astype(jnp.float32)
        out[0, :, to] = total.astype(jnp.bfloat16)


def join(control, kept, came):
    smem = pl.BlockSpec(memory_space=pltpu.SMEM)
    vmem = pl.BlockSpec(memory_space=pltpu.VMEM)
    total = sum(part.shape[1] for part in kept)
    return pl.pallas_call(
        functools.partial(join_kernel, len(kept)),
        out_shape=jax.ShapeDtypeStruct((1, kept[0].shape[0], total), jnp.bfloat16),
        in_specs=[smem] + [vmem] * (2 * len(kept)),
        out_specs=vmem,
        compiler_params=pltpu.CompilerParams(vmem_limit_bytes=16 * MIB),
        cost_estimate=cost(3 * 10**8),
        name="join",
    )(control, *kept, *came)


def pick_kernel(asked, pool, out, held, rows, sem):
    owners, bucket = asked.shape
    whole = pltpu.make_async_copy(pool, held, sem.at[owners])
    whole.start()
    whole.wait()
    for owner in range(owners):

        def copy(n, carry):
            rows[owner, n] = held[asked[owner, n]]
            return carry

        lax.fori_loop(0, bucket, copy, 0, unroll=8)
        pltpu.make_async_copy(rows.at[owner], out.at[owner], sem.at[owner]).start()
    for owner in range(owners):
        pltpu.make_async_copy(rows.at[owner], out.at[owner], sem.at[owner]).wait()


def pick(pool, asked):
    hbm = pl.BlockSpec(memory_space=pltpu.HBM)
    out = asked.shape + pool.shape[1:]
    return pl.pallas_call(
        pick_kernel,
        out_shape=jax.ShapeDtypeStruct(out, jnp.bfloat16),
        in_specs=[pl.BlockSpec(memory_space=pltpu.SMEM), hbm],
        out_specs=hbm,
        scratch_shapes=[
            pltpu.VMEM(pool.shape, jnp.bfloat16),
            pltpu.VMEM(out, jnp.bfloat16),
            pltpu.SemaphoreType.DMA((asked.shape[0] + 1,)),
        ],
        compiler_params=pltpu.CompilerParams(vmem_limit_bytes=56 * MIB),
        cost_estimate=cost(),
        name="pick",
    )(asked, pool)


SWAP = [(0, 1), (1, 0)]


def after(value, *others):
    return lax.optimization_barrier((value,) + others)[0]


def shards(
    queries, new_kv, pool, out_weight, tok_conv, page_conv, page_fill, page_owner, page_index
):
    row_count = queries.shape[1]
    slot_count = page_owner.shape[1]
    owner_count = lax.axis_size("seq")
    tp_count = lax.axis_size("tp")
    bucket = 2 * slot_count // owner_count
    group, role, tp = lax.axis_index("group"), lax.axis_index("role"), lax.axis_index("tp")
    seq = lax.axis_index("seq")


    own = 2 * group + role
    depth = out_weight.shape[0] // 4
    columns = out_weight.shape[1]
    quarter = lax.dynamic_slice_in_dim(out_weight, own * depth, depth, 0)
    order = [q ^ own for q in range(4)]
    order = [(v % 2) * 2 + v // 2 for v in order]
    flip = tp if tp_count == 2 else 0
    second = jnp.where(seq < 2, 2, 1)
    third = jnp.where(seq < 2, 3, 0)
    local = [own, own ^ 2, own ^ 1, own ^ 3]
    begins = [v * columns // LANES for v in (seq, seq ^ 1, second, third)]
    begins.append(begins[-1] + columns // 2 // LANES)
    control = jnp.stack(
        [jnp.asarray(v, jnp.int32) for v in (flip, 1 - flip, *order, *local, *begins)]
    )
    swap_group = functools.partial(lax.ppermute, axis_name="group", perm=SWAP)
    swap_role = functools.partial(lax.ppermute, axis_name="role", perm=SWAP)

    if owner_count == 4:
        middle = (seq == 1) | (seq == 2)
        cut = columns // 2
        parts = [quarter[:, :cut], quarter[:, cut:]]
        pair = functools.partial(lax.ppermute, axis_name="seq", perm=[(0, 1), (1, 0), (2, 3), (3, 2)])
        cross = functools.partial(lax.ppermute, axis_name="seq", perm=[(1, 2), (2, 1)])
        forward = functools.partial(lax.ppermute, axis_name="seq", perm=[(1, 0), (2, 3)])
        near, inner = [pair(parts[0])], [cross(parts[0])]

    position, wanted = rank(page_owner, page_index, owner_count, bucket)
    asked = lax.all_to_all(wanted, "seq", split_axis=0, concat_axis=0, tiled=True)
    if owner_count == 4:
        near, inner = [after(near[0], asked)], [after(inner[0], asked)]
        later = after(parts[1], near[0], inner[0])
        near.append(pair(later))
        inner.append(cross(later))
        asked = after(asked, near[0], inner[0])
    found = pick(pool[0], asked)
    if owner_count == 4:
        near[1], inner[1] = after(near[1], found), after(inner[1], found)
        found = after(found, near[1], inner[1])
    pages = lax.all_to_all(found, "seq", split_axis=0, concat_axis=0, tiled=True)
    pages = pages.reshape((owner_count * bucket,) + found.shape[2:])
    slots = slot_count * pool.shape[3]
    fresh = new_kv[0].reshape(row_count, -1)
    tables = attend_tables(
        row_count, slot_count, pool.shape[3], tok_conv[0], page_conv[0], page_fill[0]
    )

    if owner_count != 4 or tp_count != 2:
        mine = lax.all_gather(quarter, "seq", axis=1, tiled=True)
        across = swap_group(mine)
        pieces = [mine, across, swap_role(mine), swap_role(across)]
        keys, values = place(position, pages, fresh)
        partial = [
            project(control, attend(side, control, tables, queries[0], keys, values, slots), pieces)
            for side in (0, 1)
        ]
        return lax.psum_scatter(
            jnp.concatenate(partial, axis=0), "tp", scatter_dimension=0, tiled=True
        )[None]

    swap_tp = functools.partial(lax.ppermute, axis_name="tp", perm=SWAP)

    def four(one, two, *hold):
        return [one, two, swap_role(after(one, *hold)), swap_role(after(two, *hold))]

    near_across = [swap_group(part) for part in near]
    next_shard = [jnp.where(middle, part, forward(part)) for part in inner]
    next_across = [swap_group(part) for part in next_shard]
    near_all = four(near[0], near_across[0]) + four(near[1], near_across[1])
    next_all = four(next_shard[0], next_across[0]) + four(next_shard[1], next_across[1])
    far = [cross(after(part, *next_across)) for part in near]

    keys, values = place(position, after(pages, *near_all, *next_all), fresh)
    left = attend(1, control, tables, queries[0], keys, values, slots)
    far_on = [forward(after(far[0], left))]
    sent, kept = [project(control, left, [out_weight])], []
    came = [swap_tp(sent[0])]
    stay = attend(0, control, tables, after(queries[0], sent[0], far[0]), keys, values, slots)
    far_on.append(forward(after(far[1], stay)))
    far[0] = jnp.where(middle, far[0], after(far_on[0], stay))
    far_across = [swap_group(far[0])]
    for pieces in (near_all, next_all):
        both = project(control, after(left, far[0], far[-1], came[0], *sent), pieces, stay)
        sent.append(both[0])
        kept.append(both[1])
        came.append(swap_tp(sent[-1]))
        if len(far_across) == 1:
            far[1] = jnp.where(middle, far[1], after(far_on[1], sent[1]))
            far_across.append(swap_group(far[1]))
    kept.insert(0, project(control, after(stay, sent[2], came[1], far_across[0]), [out_weight]))
    for n in range(2):
        pieces = four(far[n], far_across[n], sent[-1])
        both = project(control, after(left, kept[0], *came[2 : 3 + n]), pieces, stay)
        sent.append(both[0])
        kept.append(both[1])
        came.append(swap_tp(sent[-1]))
    return join(control, kept, came)


def solution(mesh):
    return jax.shard_map(
        shards,
        mesh=mesh,
        in_specs=(
            P("role", ("group", "seq"), "tp"),
            P("role", ("group", "seq"), None, "tp"),
            P("role", ("group", "seq"), None, None, "tp"),
            P("tp", "seq"),
            P("role", ("group", "seq")),
            P("role", ("group", "seq")),
            P("role", ("group", "seq")),
            P("role", ("group", "seq")),
            P("role", ("group", "seq")),
        ),
        out_specs=P("role", ("group", "seq", "tp"), None),
        check_vma=False,
    )
```

```python
import functools
import math

import jax
import jax.numpy as jnp
from jax import lax
from jax.experimental import pallas as pl
from jax.experimental.pallas import tpu as pltpu
from jax.sharding import PartitionSpec as P

HD = 128
TILE = 64
KEYS = 256
LANES = 128
HIDDEN = -1e30
COLUMNS = 256
MIB = 1024 * 1024


def cost(flops=3 * 10**9):
    return pl.CostEstimate(flops=flops, bytes_accessed=1000, transcendentals=0)


def rank_kernel(owner, page, position, wanted, count):
    owners, bucket = wanted.shape
    for n in range(owners):
        count[n] = 0

    def clear(k, carry):
        for n in range(owners):
            wanted[n, k] = 0
        return carry

    lax.fori_loop(0, bucket, clear, 0)

    def put(slot, carry):
        to = owner[0, slot]
        rank = count[to]
        count[to] = rank + 1
        wanted[to, rank] = page[0, slot]
        position[slot] = to * bucket + rank
        return carry

    lax.fori_loop(0, owner.shape[1], put, 0, unroll=4)


def rank(page_owner, page_index, owners, bucket):
    smem = pl.BlockSpec(memory_space=pltpu.SMEM)
    return pl.pallas_call(
        rank_kernel,
        out_shape=(
            jax.ShapeDtypeStruct((page_owner.shape[1],), jnp.int32),
            jax.ShapeDtypeStruct((owners, bucket), jnp.int32),
        ),
        in_specs=[smem, smem],
        out_specs=(smem, smem),
        scratch_shapes=[pltpu.SMEM((owners,), jnp.int32)],
        cost_estimate=cost(),
        name="rank",
    )(page_owner, page_index)


def place_kernel(position, pages, fresh, keys, values):
    kv_local, key_total = keys.shape[:2]
    slots, page_len, rows = position.shape[0], pages.shape[2], fresh.shape[0]
    channels = kv_local * HD
    hist = slots * page_len
    fresh_base = hist + KEYS
    for head in range(kv_local):
        values[head, :, HD:] = jnp.ones((key_total, HD), jnp.bfloat16)
        for first, last in ((hist, fresh_base), (fresh_base + rows, key_total)):
            keys[head, first:last] = jnp.zeros((last - first, HD), jnp.bfloat16)
            values[head, first:last, :HD] = jnp.zeros((last - first, HD), jnp.bfloat16)
        at = head * HD
        keys[head, fresh_base : fresh_base + rows] = fresh[:, at : at + HD]
        values[head, fresh_base : fresh_base + rows, :HD] = fresh[:, channels + at : channels + at + HD]

    def place(slot, carry):
        page = position[slot]
        row = pl.ds(pl.multiple_of(slot * page_len, page_len), page_len)
        for head in range(kv_local):
            at = head * HD
            keys[head, row] = pages[page, 0, :, at : at + HD]
            values[head, row, :HD] = pages[page, 1, :, at : at + HD]
        return carry

    lax.fori_loop(0, slots, place, 0, unroll=8)


def place(position, pages, fresh):
    kv_local = pages.shape[3] // HD
    rows = fresh.shape[0]
    key_total = position.shape[0] * pages.shape[2] + KEYS + pl.cdiv(rows, KEYS) * KEYS + KEYS
    vmem = pl.BlockSpec(memory_space=pltpu.VMEM)
    return pl.pallas_call(
        place_kernel,
        out_shape=(
            jax.ShapeDtypeStruct((kv_local, key_total, HD), jnp.bfloat16),
            jax.ShapeDtypeStruct((kv_local, key_total, 2 * HD), jnp.bfloat16),
        ),
        in_specs=[pl.BlockSpec(memory_space=pltpu.SMEM), vmem, vmem],
        out_specs=(vmem, vmem),
        compiler_params=pltpu.CompilerParams(vmem_limit_bytes=20 * MIB),
        cost_estimate=cost(10**9),
        name="place",
    )(position, pages, fresh)


def attend_kernel(
    fresh_base, side, control, hist_at, hist_steps, fresh_at, fresh_steps,
    query, keys, values, key_conv, key_row, tok_conv, out, scores, sums,
):
    kv_local = keys.shape[0]
    group_size = query.shape[1] // (kv_local * HD)
    half, depth = out.shape[1], out.shape[2]
    tiles = half // TILE
    to_exp2 = math.log2(math.e) / math.sqrt(HD)
    wide = group_size * TILE

    def tile(number_here, carry):
        index = control[side] * tiles + number_here
        first = pl.multiple_of(index * TILE, TILE)
        leaving = pl.ds(pl.multiple_of(number_here * TILE, TILE), TILE)
        tokens = pl.ds(first, TILE)
        conv = tok_conv[tokens]
        number = first + lax.broadcasted_iota(jnp.int32, (TILE, 1), 0)
        steps_h, steps_f = hist_steps[index], fresh_steps[index]
        at_h, at_f = hist_at[index], fresh_at[index]
        heads = [
            jnp.concatenate(
                [
                    query[tokens, (head * group_size + g) * HD : (head * group_size + g + 1) * HD]
                    for g in range(group_size)
                ],
                axis=0,
            )
            for head in range(kv_local)
        ]

        def key_range(step):
            start = jnp.where(
                step < steps_h, at_h + step * KEYS, fresh_base + at_f + (step - steps_h) * KEYS
            )
            return pl.ds(pl.multiple_of(start, LANES), KEYS)

        def score(step, tops):
            where = key_range(step)
            ok = (key_conv[:, where] == conv) & (key_row[:, where] <= number)
            held = pl.ds(pl.multiple_of(step * KEYS, KEYS), KEYS)
            new = []
            for head in range(kv_local):
                s = lax.dot_general(
                    heads[head], keys[head, where], (((1,), (1,)), ((), ())),
                    preferred_element_type=jnp.float32,
                ).reshape(group_size, TILE, KEYS)
                s = jnp.where(ok[None], s, HIDDEN).reshape(wide, KEYS)
                scores[head, :, held] = s
                top = tops[head]
                for k in range(0, KEYS, LANES):
                    top = jnp.maximum(top, s[:, k : k + LANES])
                new.append(top)
            return tuple(new)

        low = jnp.full((wide, LANES), HIDDEN, jnp.float32)
        tops = lax.fori_loop(0, steps_h + steps_f, score, (low,) * kv_local)
        tops = [jnp.max(top, axis=1, keepdims=True) * to_exp2 for top in tops]
        sums[...] = jnp.zeros_like(sums)

        def gather(step, carry):
            where = key_range(step)
            held = pl.ds(pl.multiple_of(step * KEYS, KEYS), KEYS)
            for head in range(kv_local):
                w = jnp.exp2(scores[head, :, held] * to_exp2 - tops[head]).astype(jnp.bfloat16)
                sums[head] += jnp.dot(w, values[head, where], preferred_element_type=jnp.float32)
            return carry

        lax.fori_loop(0, steps_h + steps_f, gather, 0)
        for head in range(kv_local):
            done = (sums[head, :, :HD] / sums[head, :, HD:]).astype(jnp.bfloat16)
            for g in range(group_size):
                at = (head * group_size + g) * HD
                out[control[2 + at // depth], leaving, at % depth : at % depth + HD] = done[
                    g * TILE : (g + 1) * TILE
                ]
        return carry

    lax.fori_loop(0, tiles, tile, 0)


def attend_tables(rows, slots, page_len, tok_conv, page_conv, page_fill):
    hist = slots * page_len
    fresh_base = hist + KEYS
    key_total = fresh_base + pl.cdiv(rows, KEYS) * KEYS + KEYS
    live = jnp.arange(page_len)[None, :] < page_fill[:, None]
    hist_conv = jnp.where(live, page_conv[:, None], -1).reshape(hist)
    tail = key_total - fresh_base - rows
    key_conv = jnp.concatenate(
        [hist_conv, jnp.full((KEYS,), -1, jnp.int32), tok_conv, jnp.full((tail,), -1, jnp.int32)]
    )[None]
    key_row = jnp.maximum(jnp.arange(key_total, dtype=jnp.int32) - fresh_base, -1)[None]
    lowest, highest = tok_conv[::TILE], tok_conv[TILE - 1 :: TILE]
    hist_at = jnp.sum(page_conv[None] < lowest[:, None], axis=1, dtype=jnp.int32) * page_len
    hist_at = hist_at // LANES * LANES
    hist_end = jnp.sum(page_conv[None] <= highest[:, None], axis=1, dtype=jnp.int32) * page_len
    hist_steps = (hist_end - hist_at + KEYS - 1) // KEYS
    fresh_at = jnp.sum(tok_conv[None] < lowest[:, None], axis=1, dtype=jnp.int32) // LANES * LANES
    fresh_end = (jnp.arange(rows // TILE, dtype=jnp.int32) + 1) * TILE
    fresh_steps = (fresh_end - fresh_at + KEYS - 1) // KEYS
    return key_conv, key_row, tok_conv[:, None], hist_at, hist_steps, fresh_at, fresh_steps


def attend(side, control, tables, queries, keys, values, slots):
    rows, width = queries.shape
    kv_local, key_total = keys.shape[:2]
    group_size = width // (kv_local * HD)
    key_conv, key_row, tok_conv, *steps = tables
    fresh_base = slots + KEYS
    most = slots // KEYS + pl.cdiv(rows, KEYS)
    smem = pl.BlockSpec(memory_space=pltpu.SMEM)
    vmem = pl.BlockSpec(memory_space=pltpu.VMEM)
    return pl.pallas_call(
        functools.partial(attend_kernel, fresh_base, side),
        out_shape=jax.ShapeDtypeStruct((4, rows // 2, width // 4), jnp.bfloat16),
        in_specs=[smem] * 5 + [vmem] * 6,
        out_specs=vmem,
        scratch_shapes=[
            pltpu.VMEM((kv_local, group_size * TILE, most * KEYS), jnp.float32),
            pltpu.VMEM((kv_local, group_size * TILE, 2 * HD), jnp.float32),
        ],
        compiler_params=pltpu.CompilerParams(vmem_limit_bytes=28 * MIB),
        cost_estimate=cost((16 - 15 * side) * 10**9),
        name="attend",
    )(control, *steps, queries, keys, values, key_conv, key_row, tok_conv)


def multiply(left, pieces, at):
    total = None
    for n, piece in enumerate(pieces):
        term = jnp.dot(left[n], piece[:, at], preferred_element_type=jnp.float32)
        total = term if total is None else total + term
    return total.astype(jnp.bfloat16)


def blocks(columns):
    cut = min(COLUMNS, columns)
    return [slice(k, k + cut) for k in range(0, columns, cut)]


def parts_of(control, refs):
    if len(refs) == 1:
        depth = refs[0].shape[0] // 4
        return [
            (0, [refs[0].at[pl.ds(pl.multiple_of(control[6 + n] * depth, depth), depth)] for n in range(4)])
        ]
    columns = refs[0].shape[1]
    return [(k // 4 * columns, refs[k : k + 4]) for k in range(0, len(refs), 4)]


def project_kernel(control, left, *refs):
    for first, pieces in parts_of(control, refs[:-1]):
        for at in blocks(pieces[0].shape[1]):
            refs[-1][:, first + at.start : first + at.stop] = multiply(left, pieces, at)


def project_both_kernel(control, left, stay, *refs):
    sent, kept = refs[-2:]
    half = left.shape[1]
    for first, pieces in parts_of(control, refs[:-2]):
        for at in blocks(pieces[0].shape[1]):
            total = multiply([jnp.concatenate([left[n], stay[n]], axis=0) for n in range(4)], pieces, at)
            to = slice(first + at.start, first + at.stop)
            sent[:, to] = total[:half]
            kept[:, to] = total[half:]


def project(control, left, pieces, stay=None):
    half = left.shape[1]
    columns = pieces[0].shape[1] * max(1, len(pieces) // 4)
    smem = pl.BlockSpec(memory_space=pltpu.SMEM)
    vmem = pl.BlockSpec(memory_space=pltpu.VMEM)
    shape = jax.ShapeDtypeStruct((half, columns), jnp.bfloat16)
    rows = [left] if stay is None else [left, stay]
    return pl.pallas_call(
        project_kernel if stay is None else project_both_kernel,
        out_shape=shape if stay is None else (shape, shape),
        in_specs=[smem] + [vmem] * (len(rows) + len(pieces)),
        out_specs=vmem if stay is None else (vmem, vmem),
        compiler_params=pltpu.CompilerParams(vmem_limit_bytes=16 * MIB),
        cost_estimate=cost((3 if stay is None else 6) * 10**9),
        name="project",
    )(control, *rows, *pieces)


def join_kernel(count, control, *refs):
    out = refs[-1]
    for n in range(count):
        kept, came = refs[n], refs[count + n]
        columns = kept.shape[1]
        to = pl.ds(pl.multiple_of(control[10 + n] * LANES, LANES), columns)
        total = kept[...].astype(jnp.float32) + came[...].astype(jnp.float32)
        out[0, :, to] = total.astype(jnp.bfloat16)


def join(control, kept, came):
    smem = pl.BlockSpec(memory_space=pltpu.SMEM)
    vmem = pl.BlockSpec(memory_space=pltpu.VMEM)
    total = sum(part.shape[1] for part in kept)
    return pl.pallas_call(
        functools.partial(join_kernel, len(kept)),
        out_shape=jax.ShapeDtypeStruct((1, kept[0].shape[0], total), jnp.bfloat16),
        in_specs=[smem] + [vmem] * (2 * len(kept)),
        out_specs=vmem,
        compiler_params=pltpu.CompilerParams(vmem_limit_bytes=16 * MIB),
        cost_estimate=cost(3 * 10**8),
        name="join",
    )(control, *kept, *came)


def pick_kernel(asked, pool, out, held, rows, sem):
    owners, bucket = asked.shape
    whole = pltpu.make_async_copy(pool, held, sem.at[owners])
    whole.start()
    whole.wait()
    for owner in range(owners):

        def copy(n, carry):
            rows[owner, n] = held[asked[owner, n]]
            return carry

        lax.fori_loop(0, bucket, copy, 0, unroll=8)
        pltpu.make_async_copy(rows.at[owner], out.at[owner], sem.at[owner]).start()
    for owner in range(owners):
        pltpu.make_async_copy(rows.at[owner], out.at[owner], sem.at[owner]).wait()


def pick(pool, asked):
    hbm = pl.BlockSpec(memory_space=pltpu.HBM)
    out = asked.shape + pool.shape[1:]
    return pl.pallas_call(
        pick_kernel,
        out_shape=jax.ShapeDtypeStruct(out, jnp.bfloat16),
        in_specs=[pl.BlockSpec(memory_space=pltpu.SMEM), hbm],
        out_specs=hbm,
        scratch_shapes=[
            pltpu.VMEM(pool.shape, jnp.bfloat16),
            pltpu.VMEM(out, jnp.bfloat16),
            pltpu.SemaphoreType.DMA((asked.shape[0] + 1,)),
        ],
        compiler_params=pltpu.CompilerParams(vmem_limit_bytes=56 * MIB),
        cost_estimate=cost(),
        name="pick",
    )(asked, pool)


SWAP = [(0, 1), (1, 0)]


def after(value, *others):
    return lax.optimization_barrier((value,) + others)[0]


def shards(
    queries, new_kv, pool, out_weight, tok_conv, page_conv, page_fill, page_owner, page_index
):
    row_count = queries.shape[1]
    slot_count = page_owner.shape[1]
    owner_count = lax.axis_size("seq")
    tp_count = lax.axis_size("tp")
    bucket = 2 * slot_count // owner_count
    group, role, tp = lax.axis_index("group"), lax.axis_index("role"), lax.axis_index("tp")
    seq = lax.axis_index("seq")


    own = 2 * group + role
    depth = out_weight.shape[0] // 4
    columns = out_weight.shape[1]
    quarter = lax.dynamic_slice_in_dim(out_weight, own * depth, depth, 0)
    order = [q ^ own for q in range(4)]
    order = [(v % 2) * 2 + v // 2 for v in order]
    flip = tp if tp_count == 2 else 0
    second = jnp.where(seq < 2, 2, 1)
    third = jnp.where(seq < 2, 3, 0)
    local = [own, own ^ 2, own ^ 1, own ^ 3]
    begins = [v * columns // LANES for v in (seq, seq ^ 1, second, third)]
    begins.append(begins[-1] + columns // 2 // LANES)
    control = jnp.stack(
        [jnp.asarray(v, jnp.int32) for v in (flip, 1 - flip, *order, *local, *begins)]
    )
    swap_group = functools.partial(lax.ppermute, axis_name="group", perm=SWAP)
    swap_role = functools.partial(lax.ppermute, axis_name="role", perm=SWAP)

    if owner_count == 4:
        middle = (seq == 1) | (seq == 2)
        cut = columns // 2
        parts = [quarter[:, :cut], quarter[:, cut:]]
        pair = functools.partial(lax.ppermute, axis_name="seq", perm=[(0, 1), (1, 0), (2, 3), (3, 2)])
        cross = functools.partial(lax.ppermute, axis_name="seq", perm=[(1, 2), (2, 1)])
        forward = functools.partial(lax.ppermute, axis_name="seq", perm=[(1, 0), (2, 3)])
        near, inner = [pair(parts[0])], [cross(parts[0])]

    position, wanted = rank(page_owner, page_index, owner_count, bucket)
    asked = lax.all_to_all(wanted, "seq", split_axis=0, concat_axis=0, tiled=True)
    if owner_count == 4:
        near, inner = [after(near[0], asked)], [after(inner[0], asked)]
        later = after(parts[1], near[0], inner[0])
        near.append(pair(later))
        inner.append(cross(later))
        asked = after(asked, near[0], inner[0])
    found = pick(pool[0], asked)
    if owner_count == 4:
        near[1], inner[1] = after(near[1], found), after(inner[1], found)
        found = after(found, near[1], inner[1])
    pages = lax.all_to_all(found, "seq", split_axis=0, concat_axis=0, tiled=True)
    pages = pages.reshape((owner_count * bucket,) + found.shape[2:])
    slots = slot_count * pool.shape[3]
    fresh = new_kv[0].reshape(row_count, -1)
    tables = attend_tables(
        row_count, slot_count, pool.shape[3], tok_conv[0], page_conv[0], page_fill[0]
    )

    if owner_count != 4 or tp_count != 2:
        mine = lax.all_gather(quarter, "seq", axis=1, tiled=True)
        across = swap_group(mine)
        pieces = [mine, across, swap_role(mine), swap_role(across)]
        keys, values = place(position, pages, fresh)
        partial = [
            project(control, attend(side, control, tables, queries[0], keys, values, slots), pieces)
            for side in (0, 1)
        ]
        return lax.psum_scatter(
            jnp.concatenate(partial, axis=0), "tp", scatter_dimension=0, tiled=True
        )[None]

    swap_tp = functools.partial(lax.ppermute, axis_name="tp", perm=SWAP)

    def four(one, two, *hold):
        return [one, two, swap_role(after(one, *hold)), swap_role(after(two, *hold))]

    near_across = [swap_group(part) for part in near]
    next_shard = [jnp.where(middle, part, forward(part)) for part in inner]
    next_across = [swap_group(part) for part in next_shard]
    near_all = four(near[0], near_across[0]) + four(near[1], near_across[1])
    next_all = four(next_shard[0], next_across[0]) + four(next_shard[1], next_across[1])
    far = [cross(after(near[0], *next_across))]

    keys, values = place(position, after(pages, *near_all, *next_all), fresh)
    far.append(cross(after(near[1], keys)))
    left = attend(1, control, tables, queries[0], keys, values, slots)
    far_on = [forward(after(far[0], left))]
    sent, kept = [project(control, left, [out_weight])], []
    came = [swap_tp(sent[0])]
    stay = attend(0, control, tables, after(queries[0], sent[0], far[0]), keys, values, slots)
    far_on.append(forward(after(far[1], stay)))
    far[0] = jnp.where(middle, far[0], after(far_on[0], stay))
    far_across = [swap_group(far[0])]
    for pieces in (near_all, next_all):
        both = project(control, after(left, far[0], far[-1], came[0], *sent), pieces, stay)
        sent.append(both[0])
        kept.append(both[1])
        came.append(swap_tp(sent[-1]))
        if len(far_across) == 1:
            far[1] = jnp.where(middle, far[1], after(far_on[1], sent[1]))
            far_across.append(swap_group(far[1]))
    for n in range(2):
        pieces = four(far[n], far_across[n], sent[-1], came[1])
        both = project(control, after(left, *kept), pieces, stay)
        sent.append(both[0])
        kept.append(both[1])
        came.append(swap_tp(sent[-1]))
        if n == 0:
            kept.insert(0, project(control, after(stay, sent[3], came[2]), [out_weight]))
    return join(control, kept, came)


def solution(mesh):
    return jax.shard_map(
        shards,
        mesh=mesh,
        in_specs=(
            P("role", ("group", "seq"), "tp"),
            P("role", ("group", "seq"), None, "tp"),
            P("role", ("group", "seq"), None, None, "tp"),
            P("tp", "seq"),
            P("role", ("group", "seq")),
            P("role", ("group", "seq")),
            P("role", ("group", "seq")),
            P("role", ("group", "seq")),
            P("role", ("group", "seq")),
        ),
        out_specs=P("role", ("group", "seq", "tp"), None),
        check_vma=False,
    )
```

```python
import functools
import math

import jax
import jax.numpy as jnp
from jax import lax
from jax.experimental import pallas as pl
from jax.experimental.pallas import tpu as pltpu
from jax.sharding import PartitionSpec as P

HD = 128
TILE = 64
KEYS = 256
LANES = 128
HIDDEN = -1e30
COLUMNS = 256
MIB = 1024 * 1024


def cost(flops=3 * 10**9):
    return pl.CostEstimate(flops=flops, bytes_accessed=1000, transcendentals=0)


def rank_kernel(owner, page, position, wanted, count):
    owners, bucket = wanted.shape
    for n in range(owners):
        count[n] = 0

    def clear(k, carry):
        for n in range(owners):
            wanted[n, k] = 0
        return carry

    lax.fori_loop(0, bucket, clear, 0)

    def put(slot, carry):
        to = owner[0, slot]
        rank = count[to]
        count[to] = rank + 1
        wanted[to, rank] = page[0, slot]
        position[slot] = to * bucket + rank
        return carry

    lax.fori_loop(0, owner.shape[1], put, 0, unroll=4)


def rank(page_owner, page_index, owners, bucket):
    smem = pl.BlockSpec(memory_space=pltpu.SMEM)
    return pl.pallas_call(
        rank_kernel,
        out_shape=(
            jax.ShapeDtypeStruct((page_owner.shape[1],), jnp.int32),
            jax.ShapeDtypeStruct((owners, bucket), jnp.int32),
        ),
        in_specs=[smem, smem],
        out_specs=(smem, smem),
        scratch_shapes=[pltpu.SMEM((owners,), jnp.int32)],
        cost_estimate=cost(),
        name="rank",
    )(page_owner, page_index)


def place_kernel(position, pages, fresh, keys, values):
    kv_local, key_total = keys.shape[:2]
    slots, page_len, rows = position.shape[0], pages.shape[2], fresh.shape[0]
    channels = kv_local * HD
    hist = slots * page_len
    fresh_base = hist + KEYS
    for head in range(kv_local):
        values[head, :, HD:] = jnp.ones((key_total, HD), jnp.bfloat16)
        for first, last in ((hist, fresh_base), (fresh_base + rows, key_total)):
            keys[head, first:last] = jnp.zeros((last - first, HD), jnp.bfloat16)
            values[head, first:last, :HD] = jnp.zeros((last - first, HD), jnp.bfloat16)
        at = head * HD
        keys[head, fresh_base : fresh_base + rows] = fresh[:, at : at + HD]
        values[head, fresh_base : fresh_base + rows, :HD] = fresh[:, channels + at : channels + at + HD]

    def place(slot, carry):
        page = position[slot]
        row = pl.ds(pl.multiple_of(slot * page_len, page_len), page_len)
        for head in range(kv_local):
            at = head * HD
            keys[head, row] = pages[page, 0, :, at : at + HD]
            values[head, row, :HD] = pages[page, 1, :, at : at + HD]
        return carry

    lax.fori_loop(0, slots, place, 0, unroll=8)


def place(position, pages, fresh):
    kv_local = pages.shape[3] // HD
    rows = fresh.shape[0]
    key_total = position.shape[0] * pages.shape[2] + KEYS + pl.cdiv(rows, KEYS) * KEYS + KEYS
    vmem = pl.BlockSpec(memory_space=pltpu.VMEM)
    return pl.pallas_call(
        place_kernel,
        out_shape=(
            jax.ShapeDtypeStruct((kv_local, key_total, HD), jnp.bfloat16),
            jax.ShapeDtypeStruct((kv_local, key_total, 2 * HD), jnp.bfloat16),
        ),
        in_specs=[pl.BlockSpec(memory_space=pltpu.SMEM), vmem, vmem],
        out_specs=(vmem, vmem),
        compiler_params=pltpu.CompilerParams(vmem_limit_bytes=20 * MIB),
        cost_estimate=cost(10**9),
        name="place",
    )(position, pages, fresh)


def attend_kernel(
    fresh_base, side, control, hist_at, hist_steps, fresh_at, fresh_steps,
    query, keys, values, key_conv, key_row, tok_conv, out, scores, sums,
):
    kv_local = keys.shape[0]
    group_size = query.shape[1] // (kv_local * HD)
    half, depth = out.shape[1], out.shape[2]
    tiles = half // TILE
    to_exp2 = math.log2(math.e) / math.sqrt(HD)
    wide = group_size * TILE

    def tile(number_here, carry):
        index = control[side] * tiles + number_here
        first = pl.multiple_of(index * TILE, TILE)
        leaving = pl.ds(pl.multiple_of(number_here * TILE, TILE), TILE)
        tokens = pl.ds(first, TILE)
        conv = tok_conv[tokens]
        number = first + lax.broadcasted_iota(jnp.int32, (TILE, 1), 0)
        steps_h, steps_f = hist_steps[index], fresh_steps[index]
        at_h, at_f = hist_at[index], fresh_at[index]
        heads = [
            jnp.concatenate(
                [
                    query[tokens, (head * group_size + g) * HD : (head * group_size + g + 1) * HD]
                    for g in range(group_size)
                ],
                axis=0,
            )
            for head in range(kv_local)
        ]

        def key_range(step):
            start = jnp.where(
                step < steps_h, at_h + step * KEYS, fresh_base + at_f + (step - steps_h) * KEYS
            )
            return pl.ds(pl.multiple_of(start, LANES), KEYS)

        def score(step, tops):
            where = key_range(step)
            ok = (key_conv[:, where] == conv) & (key_row[:, where] <= number)
            held = pl.ds(pl.multiple_of(step * KEYS, KEYS), KEYS)
            new = []
            for head in range(kv_local):
                s = lax.dot_general(
                    heads[head], keys[head, where], (((1,), (1,)), ((), ())),
                    preferred_element_type=jnp.float32,
                ).reshape(group_size, TILE, KEYS)
                s = jnp.where(ok[None], s, HIDDEN).reshape(wide, KEYS)
                scores[head, :, held] = s
                top = tops[head]
                for k in range(0, KEYS, LANES):
                    top = jnp.maximum(top, s[:, k : k + LANES])
                new.append(top)
            return tuple(new)

        low = jnp.full((wide, LANES), HIDDEN, jnp.float32)
        tops = lax.fori_loop(0, steps_h + steps_f, score, (low,) * kv_local)
        tops = [jnp.max(top, axis=1, keepdims=True) * to_exp2 for top in tops]
        sums[...] = jnp.zeros_like(sums)

        def gather(step, carry):
            where = key_range(step)
            held = pl.ds(pl.multiple_of(step * KEYS, KEYS), KEYS)
            for head in range(kv_local):
                w = jnp.exp2(scores[head, :, held] * to_exp2 - tops[head]).astype(jnp.bfloat16)
                sums[head] += jnp.dot(w, values[head, where], preferred_element_type=jnp.float32)
            return carry

        lax.fori_loop(0, steps_h + steps_f, gather, 0)
        for head in range(kv_local):
            done = (sums[head, :, :HD] / sums[head, :, HD:]).astype(jnp.bfloat16)
            for g in range(group_size):
                at = (head * group_size + g) * HD
                out[control[2 + at // depth], leaving, at % depth : at % depth + HD] = done[
                    g * TILE : (g + 1) * TILE
                ]
        return carry

    lax.fori_loop(0, tiles, tile, 0)


def attend_tables(rows, slots, page_len, tok_conv, page_conv, page_fill):
    hist = slots * page_len
    fresh_base = hist + KEYS
    key_total = fresh_base + pl.cdiv(rows, KEYS) * KEYS + KEYS
    live = jnp.arange(page_len)[None, :] < page_fill[:, None]
    hist_conv = jnp.where(live, page_conv[:, None], -1).reshape(hist)
    tail = key_total - fresh_base - rows
    key_conv = jnp.concatenate(
        [hist_conv, jnp.full((KEYS,), -1, jnp.int32), tok_conv, jnp.full((tail,), -1, jnp.int32)]
    )[None]
    key_row = jnp.maximum(jnp.arange(key_total, dtype=jnp.int32) - fresh_base, -1)[None]
    lowest, highest = tok_conv[::TILE], tok_conv[TILE - 1 :: TILE]
    hist_at = jnp.sum(page_conv[None] < lowest[:, None], axis=1, dtype=jnp.int32) * page_len
    hist_at = hist_at // LANES * LANES
    hist_end = jnp.sum(page_conv[None] <= highest[:, None], axis=1, dtype=jnp.int32) * page_len
    hist_steps = (hist_end - hist_at + KEYS - 1) // KEYS
    fresh_at = jnp.sum(tok_conv[None] < lowest[:, None], axis=1, dtype=jnp.int32) // LANES * LANES
    fresh_end = (jnp.arange(rows // TILE, dtype=jnp.int32) + 1) * TILE
    fresh_steps = (fresh_end - fresh_at + KEYS - 1) // KEYS
    return key_conv, key_row, tok_conv[:, None], hist_at, hist_steps, fresh_at, fresh_steps


def attend(side, control, tables, queries, keys, values, slots):
    rows, width = queries.shape
    kv_local, key_total = keys.shape[:2]
    group_size = width // (kv_local * HD)
    key_conv, key_row, tok_conv, *steps = tables
    fresh_base = slots + KEYS
    most = slots // KEYS + pl.cdiv(rows, KEYS)
    smem = pl.BlockSpec(memory_space=pltpu.SMEM)
    vmem = pl.BlockSpec(memory_space=pltpu.VMEM)
    return pl.pallas_call(
        functools.partial(attend_kernel, fresh_base, side),
        out_shape=jax.ShapeDtypeStruct((4, rows // 2, width // 4), jnp.bfloat16),
        in_specs=[smem] * 5 + [vmem] * 6,
        out_specs=vmem,
        scratch_shapes=[
            pltpu.VMEM((kv_local, group_size * TILE, most * KEYS), jnp.float32),
            pltpu.VMEM((kv_local, group_size * TILE, 2 * HD), jnp.float32),
        ],
        compiler_params=pltpu.CompilerParams(vmem_limit_bytes=28 * MIB),
        cost_estimate=cost((16 - 15 * side) * 10**9),
        name="attend",
    )(control, *steps, queries, keys, values, key_conv, key_row, tok_conv)


def multiply(left, pieces, at):
    total = None
    for n, piece in enumerate(pieces):
        term = jnp.dot(left[n], piece[:, at], preferred_element_type=jnp.float32)
        total = term if total is None else total + term
    return total.astype(jnp.bfloat16)


def blocks(columns):
    cut = min(COLUMNS, columns)
    return [slice(k, min(k + cut, columns)) for k in range(0, columns, cut)]


def parts_of(control, refs):
    if len(refs) == 1:
        depth = refs[0].shape[0] // 4
        return [
            (0, [refs[0].at[pl.ds(pl.multiple_of(control[6 + n] * depth, depth), depth)] for n in range(4)])
        ]
    parts, first = [], 0
    for k in range(0, len(refs), 4):
        parts.append((first, refs[k : k + 4]))
        first += refs[k].shape[1]
    return parts


def project_kernel(control, left, *refs):
    for first, pieces in parts_of(control, refs[:-1]):
        for at in blocks(pieces[0].shape[1]):
            refs[-1][:, first + at.start : first + at.stop] = multiply(left, pieces, at)


def finish_kernel(has_out, control, left, came, *refs):
    for first, pieces in parts_of(control, refs[: len(refs) - 1 - has_out]):
        for at in blocks(pieces[0].shape[1]):
            to = slice(first + at.start, first + at.stop)
            total = multiply(left, pieces, at).astype(jnp.float32) + came[:, to].astype(jnp.float32)
            refs[-1][0, :, to] = total.astype(jnp.bfloat16)


def project(control, left, pieces, came=None, base=None, out=None, width=None):
    half = left.shape[1]
    columns = sum(piece.shape[1] for piece in pieces[::4])
    vmem = pl.BlockSpec(memory_space=pltpu.VMEM)
    in_specs = [vmem]
    operands = [left]
    aliases = {}
    if came is None:
        kernel = project_kernel
        out_shape = jax.ShapeDtypeStruct((half, columns), jnp.bfloat16)
        out_specs = vmem
    else:
        kernel = functools.partial(finish_kernel, int(out is not None))
        in_specs.append(vmem)
        operands.append(came)
        out_shape = jax.ShapeDtypeStruct((1, half, width), jnp.bfloat16)
        out_specs = pl.BlockSpec((1, half, columns), lambda j, control: (0, 0, control[base]))
    in_specs += [vmem] * len(pieces)
    operands += pieces
    if out is not None:
        in_specs.append(pl.BlockSpec(memory_space=pl.ANY))
        operands.append(out)
        aliases = {len(operands): 0}
    return pl.pallas_call(
        kernel,
        out_shape=out_shape,
        grid_spec=pltpu.PrefetchScalarGridSpec(
            num_scalar_prefetch=1, grid=(1,), in_specs=in_specs, out_specs=out_specs
        ),
        input_output_aliases=aliases,
        compiler_params=pltpu.CompilerParams(vmem_limit_bytes=16 * MIB),
        cost_estimate=cost(),
        name="project" if came is None else "finish",
    )(control, *operands)


def pick_kernel(asked, pool, out, held, rows, sem):
    owners, bucket = asked.shape
    whole = pltpu.make_async_copy(pool, held, sem.at[owners])
    whole.start()
    whole.wait()
    for owner in range(owners):

        def copy(n, carry):
            rows[owner, n] = held[asked[owner, n]]
            return carry

        lax.fori_loop(0, bucket, copy, 0, unroll=8)
        pltpu.make_async_copy(rows.at[owner], out.at[owner], sem.at[owner]).start()
    for owner in range(owners):
        pltpu.make_async_copy(rows.at[owner], out.at[owner], sem.at[owner]).wait()


def pick(pool, asked):
    hbm = pl.BlockSpec(memory_space=pltpu.HBM)
    out = asked.shape + pool.shape[1:]
    return pl.pallas_call(
        pick_kernel,
        out_shape=jax.ShapeDtypeStruct(out, jnp.bfloat16),
        in_specs=[pl.BlockSpec(memory_space=pltpu.SMEM), hbm],
        out_specs=hbm,
        scratch_shapes=[
            pltpu.VMEM(pool.shape, jnp.bfloat16),
            pltpu.VMEM(out, jnp.bfloat16),
            pltpu.SemaphoreType.DMA((asked.shape[0] + 1,)),
        ],
        compiler_params=pltpu.CompilerParams(vmem_limit_bytes=56 * MIB),
        cost_estimate=cost(),
        name="pick",
    )(asked, pool)


SWAP = [(0, 1), (1, 0)]


def after(value, *others):
    return lax.optimization_barrier((value,) + others)[0]


def shards(
    queries, new_kv, pool, out_weight, tok_conv, page_conv, page_fill, page_owner, page_index
):
    row_count = queries.shape[1]
    slot_count = page_owner.shape[1]
    owner_count = lax.axis_size("seq")
    tp_count = lax.axis_size("tp")
    bucket = 2 * slot_count // owner_count
    group, role, tp = lax.axis_index("group"), lax.axis_index("role"), lax.axis_index("tp")
    seq = lax.axis_index("seq")


    own = 2 * group + role
    depth = out_weight.shape[0] // 4
    columns = out_weight.shape[1]
    quarter = lax.dynamic_slice_in_dim(out_weight, own * depth, depth, 0)
    order = [q ^ own for q in range(4)]
    order = [(v % 2) * 2 + v // 2 for v in order]
    flip = tp if tp_count == 2 else 0
    second = jnp.where(seq < 2, 2, 1)
    third = jnp.where(seq < 2, 3, 0)
    local = [own, own ^ 2, own ^ 1, own ^ 3]
    control = jnp.stack(
        [jnp.asarray(v, jnp.int32) for v in (flip, 1 - flip, *order, *local, seq, seq ^ 1, second, 2 * third, 2 * third + 1)]
    )
    swap_group = functools.partial(lax.ppermute, axis_name="group", perm=SWAP)
    swap_role = functools.partial(lax.ppermute, axis_name="role", perm=SWAP)

    if owner_count == 4:
        middle = (seq == 1) | (seq == 2)
        cut = columns // 2
        parts = [quarter[:, :cut], quarter[:, cut:]]
        pair = functools.partial(lax.ppermute, axis_name="seq", perm=[(0, 1), (1, 0), (2, 3), (3, 2)])
        cross = functools.partial(lax.ppermute, axis_name="seq", perm=[(1, 2), (2, 1)])
        forward = functools.partial(lax.ppermute, axis_name="seq", perm=[(1, 0), (2, 3)])
        near, inner = [pair(parts[0])], [cross(parts[0])]

    position, wanted = rank(page_owner, page_index, owner_count, bucket)
    asked = lax.all_to_all(wanted, "seq", split_axis=0, concat_axis=0, tiled=True)
    if owner_count == 4:
        near, inner = [after(near[0], asked)], [after(inner[0], asked)]
        later = after(parts[1], near[0], inner[0])
        near.append(pair(later))
        inner.append(cross(later))
        asked = after(asked, near[0], inner[0])
    found = pick(pool[0], asked)
    if owner_count == 4:
        near[1], inner[1] = after(near[1], found), after(inner[1], found)
        found = after(found, near[1], inner[1])
    pages = lax.all_to_all(found, "seq", split_axis=0, concat_axis=0, tiled=True)
    pages = pages.reshape((owner_count * bucket,) + found.shape[2:])
    slots = slot_count * pool.shape[3]
    fresh = new_kv[0].reshape(row_count, -1)
    tables = attend_tables(
        row_count, slot_count, pool.shape[3], tok_conv[0], page_conv[0], page_fill[0]
    )

    if owner_count != 4 or tp_count != 2:
        mine = lax.all_gather(quarter, "seq", axis=1, tiled=True)
        across = swap_group(mine)
        pieces = [mine, across, swap_role(mine), swap_role(across)]
        keys, values = place(position, pages, fresh)
        partial = [
            project(control, attend(side, control, tables, queries[0], keys, values, slots), pieces)
            for side in (0, 1)
        ]
        return lax.psum_scatter(
            jnp.concatenate(partial, axis=0), "tp", scatter_dimension=0, tiled=True
        )[None]

    swap_tp = functools.partial(lax.ppermute, axis_name="tp", perm=SWAP)

    def four(one, two, *hold):
        return [one, two, swap_role(after(one, *hold)), swap_role(after(two, *hold))]

    near_across = [swap_group(part) for part in near]
    next_shard = [jnp.where(middle, part, forward(part)) for part in inner]
    next_across = [swap_group(part) for part in next_shard]
    near_all = four(near[0], near_across[0]) + four(near[1], near_across[1])
    next_all = four(next_shard[0], next_across[0]) + four(next_shard[1], next_across[1])
    far = [cross(after(part, *next_across)) for part in near]

    keys, values = place(position, after(pages, *near_all, *next_all), fresh)
    left = attend(1, control, tables, queries[0], keys, values, slots)
    far_on = [forward(after(far[0], left))]
    sent = [project(control, left, [out_weight])]
    far_on.append(forward(after(far[1], sent[0])))
    sent.append(project(control, after(left, sent[-1]), near_all))
    far[0] = jnp.where(middle, far[0], after(far_on[0], sent[1]))
    far_across = [swap_group(far[0])]
    sent.append(project(control, after(left, sent[-1]), next_all))
    came = [swap_tp(each) for each in sent]
    stay = attend(0, control, tables, after(queries[0], sent[2], far[0]), keys, values, slots)
    far[1] = jnp.where(middle, far[1], after(far_on[1], stay))
    far_across.append(swap_group(far[1]))
    far_all = [four(far[0], far_across[0], stay)]
    total = columns * owner_count
    out = project(control, after(stay, *came[:2]), [out_weight], came[0], 10, None, total)
    out = project(control, stay, near_all, came[1], 11, out, total)
    out = project(control, stay, next_all, came[2], 12, out, total)
    sent.append(project(control, after(left, out), far_all[0]))
    came.append(swap_tp(sent[3]))
    far_all.append(four(far[1], far_across[1], sent[3]))
    sent.append(project(control, left, far_all[1]))
    came.append(swap_tp(sent[4]))
    out = project(control, after(stay, sent[4]), far_all[0], came[3], 13, out, total)
    return project(control, stay, far_all[1], came[4], 14, out, total)


def solution(mesh):
    return jax.shard_map(
        shards,
        mesh=mesh,
        in_specs=(
            P("role", ("group", "seq"), "tp"),
            P("role", ("group", "seq"), None, "tp"),
            P("role", ("group", "seq"), None, None, "tp"),
            P("tp", "seq"),
            P("role", ("group", "seq")),
            P("role", ("group", "seq")),
            P("role", ("group", "seq")),
            P("role", ("group", "seq")),
            P("role", ("group", "seq")),
        ),
        out_specs=P("role", ("group", "seq", "tp"), None),
        check_vma=False,
    )
```

```python
import functools
import math

import jax
import jax.numpy as jnp
from jax import lax
from jax.experimental import pallas as pl
from jax.experimental.pallas import tpu as pltpu
from jax.sharding import PartitionSpec as P

HD = 128
TILE = 64
KEYS = 256
LANES = 128
HIDDEN = -1e30
COLUMNS = 256
MIB = 1024 * 1024


def cost(flops=3 * 10**9):
    return pl.CostEstimate(flops=flops, bytes_accessed=1000, transcendentals=0)


def rank_kernel(owner, page, position, wanted, count):
    owners, bucket = wanted.shape
    for n in range(owners):
        count[n] = 0

    def clear(k, carry):
        for n in range(owners):
            wanted[n, k] = 0
        return carry

    lax.fori_loop(0, bucket, clear, 0)

    def put(slot, carry):
        to = owner[0, slot]
        rank = count[to]
        count[to] = rank + 1
        wanted[to, rank] = page[0, slot]
        position[slot] = to * bucket + rank
        return carry

    lax.fori_loop(0, owner.shape[1], put, 0, unroll=4)


def rank(page_owner, page_index, owners, bucket):
    smem = pl.BlockSpec(memory_space=pltpu.SMEM)
    return pl.pallas_call(
        rank_kernel,
        out_shape=(
            jax.ShapeDtypeStruct((page_owner.shape[1],), jnp.int32),
            jax.ShapeDtypeStruct((owners, bucket), jnp.int32),
        ),
        in_specs=[smem, smem],
        out_specs=(smem, smem),
        scratch_shapes=[pltpu.SMEM((owners,), jnp.int32)],
        cost_estimate=cost(),
        name="rank",
    )(page_owner, page_index)


def place_kernel(position, pages, fresh, keys, values):
    kv_local, key_total = keys.shape[:2]
    slots, page_len, rows = position.shape[0], pages.shape[2], fresh.shape[0]
    channels = kv_local * HD
    hist = slots * page_len
    fresh_base = hist + KEYS
    for head in range(kv_local):
        values[head, :, HD:] = jnp.ones((key_total, HD), jnp.bfloat16)
        for first, last in ((hist, fresh_base), (fresh_base + rows, key_total)):
            keys[head, first:last] = jnp.zeros((last - first, HD), jnp.bfloat16)
            values[head, first:last, :HD] = jnp.zeros((last - first, HD), jnp.bfloat16)
        at = head * HD
        keys[head, fresh_base : fresh_base + rows] = fresh[:, at : at + HD]
        values[head, fresh_base : fresh_base + rows, :HD] = fresh[:, channels + at : channels + at + HD]

    def place(slot, carry):
        page = position[slot]
        row = pl.ds(pl.multiple_of(slot * page_len, page_len), page_len)
        for head in range(kv_local):
            at = head * HD
            keys[head, row] = pages[page, 0, :, at : at + HD]
            values[head, row, :HD] = pages[page, 1, :, at : at + HD]
        return carry

    lax.fori_loop(0, slots, place, 0, unroll=8)


def place(position, pages, fresh):
    kv_local = pages.shape[3] // HD
    rows = fresh.shape[0]
    key_total = position.shape[0] * pages.shape[2] + KEYS + pl.cdiv(rows, KEYS) * KEYS + KEYS
    vmem = pl.BlockSpec(memory_space=pltpu.VMEM)
    return pl.pallas_call(
        place_kernel,
        out_shape=(
            jax.ShapeDtypeStruct((kv_local, key_total, HD), jnp.bfloat16),
            jax.ShapeDtypeStruct((kv_local, key_total, 2 * HD), jnp.bfloat16),
        ),
        in_specs=[pl.BlockSpec(memory_space=pltpu.SMEM), vmem, vmem],
        out_specs=(vmem, vmem),
        compiler_params=pltpu.CompilerParams(vmem_limit_bytes=20 * MIB),
        cost_estimate=cost(10**9),
        name="place",
    )(position, pages, fresh)


def attend_kernel(
    fresh_base, side, control, hist_at, hist_steps, fresh_at, fresh_steps,
    query, keys, values, key_conv, key_row, tok_conv, out, scores, sums,
):
    kv_local = keys.shape[0]
    group_size = query.shape[1] // (kv_local * HD)
    half, depth = out.shape[1], out.shape[2]
    tiles = half // TILE
    to_exp2 = math.log2(math.e) / math.sqrt(HD)
    wide = group_size * TILE

    def tile(number_here, carry):
        index = control[side] * tiles + number_here
        first = pl.multiple_of(index * TILE, TILE)
        leaving = pl.ds(pl.multiple_of(number_here * TILE, TILE), TILE)
        tokens = pl.ds(first, TILE)
        conv = tok_conv[tokens]
        number = first + lax.broadcasted_iota(jnp.int32, (TILE, 1), 0)
        steps_h, steps_f = hist_steps[index], fresh_steps[index]
        at_h, at_f = hist_at[index], fresh_at[index]
        heads = [
            jnp.concatenate(
                [
                    query[tokens, (head * group_size + g) * HD : (head * group_size + g + 1) * HD]
                    for g in range(group_size)
                ],
                axis=0,
            )
            for head in range(kv_local)
        ]

        def key_range(step):
            start = jnp.where(
                step < steps_h, at_h + step * KEYS, fresh_base + at_f + (step - steps_h) * KEYS
            )
            return pl.ds(pl.multiple_of(start, LANES), KEYS)

        def score(step, tops):
            where = key_range(step)
            ok = (key_conv[:, where] == conv) & (key_row[:, where] <= number)
            held = pl.ds(pl.multiple_of(step * KEYS, KEYS), KEYS)
            new = []
            for head in range(kv_local):
                s = lax.dot_general(
                    heads[head], keys[head, where], (((1,), (1,)), ((), ())),
                    preferred_element_type=jnp.float32,
                ).reshape(group_size, TILE, KEYS)
                s = jnp.where(ok[None], s, HIDDEN).reshape(wide, KEYS)
                scores[head, :, held] = s
                top = tops[head]
                for k in range(0, KEYS, LANES):
                    top = jnp.maximum(top, s[:, k : k + LANES])
                new.append(top)
            return tuple(new)

        low = jnp.full((wide, LANES), HIDDEN, jnp.float32)
        tops = lax.fori_loop(0, steps_h + steps_f, score, (low,) * kv_local)
        tops = [jnp.max(top, axis=1, keepdims=True) * to_exp2 for top in tops]
        sums[...] = jnp.zeros_like(sums)

        def gather(step, carry):
            where = key_range(step)
            held = pl.ds(pl.multiple_of(step * KEYS, KEYS), KEYS)
            for head in range(kv_local):
                w = jnp.exp2(scores[head, :, held] * to_exp2 - tops[head]).astype(jnp.bfloat16)
                sums[head] += jnp.dot(w, values[head, where], preferred_element_type=jnp.float32)
            return carry

        lax.fori_loop(0, steps_h + steps_f, gather, 0)
        for head in range(kv_local):
            done = (sums[head, :, :HD] / sums[head, :, HD:]).astype(jnp.bfloat16)
            for g in range(group_size):
                at = (head * group_size + g) * HD
                out[control[2 + at // depth], leaving, at % depth : at % depth + HD] = done[
                    g * TILE : (g + 1) * TILE
                ]
        return carry

    lax.fori_loop(0, tiles, tile, 0)


def attend_tables(rows, slots, page_len, tok_conv, page_conv, page_fill):
    hist = slots * page_len
    fresh_base = hist + KEYS
    key_total = fresh_base + pl.cdiv(rows, KEYS) * KEYS + KEYS
    live = jnp.arange(page_len)[None, :] < page_fill[:, None]
    hist_conv = jnp.where(live, page_conv[:, None], -1).reshape(hist)
    tail = key_total - fresh_base - rows
    key_conv = jnp.concatenate(
        [hist_conv, jnp.full((KEYS,), -1, jnp.int32), tok_conv, jnp.full((tail,), -1, jnp.int32)]
    )[None]
    key_row = jnp.maximum(jnp.arange(key_total, dtype=jnp.int32) - fresh_base, -1)[None]
    lowest, highest = tok_conv[::TILE], tok_conv[TILE - 1 :: TILE]
    hist_at = jnp.sum(page_conv[None] < lowest[:, None], axis=1, dtype=jnp.int32) * page_len
    hist_at = hist_at // LANES * LANES
    hist_end = jnp.sum(page_conv[None] <= highest[:, None], axis=1, dtype=jnp.int32) * page_len
    hist_steps = (hist_end - hist_at + KEYS - 1) // KEYS
    fresh_at = jnp.sum(tok_conv[None] < lowest[:, None], axis=1, dtype=jnp.int32) // LANES * LANES
    fresh_end = (jnp.arange(rows // TILE, dtype=jnp.int32) + 1) * TILE
    fresh_steps = (fresh_end - fresh_at + KEYS - 1) // KEYS
    return key_conv, key_row, tok_conv[:, None], hist_at, hist_steps, fresh_at, fresh_steps


def attend(side, control, tables, queries, keys, values, slots):
    rows, width = queries.shape
    kv_local, key_total = keys.shape[:2]
    group_size = width // (kv_local * HD)
    key_conv, key_row, tok_conv, *steps = tables
    fresh_base = slots + KEYS
    most = slots // KEYS + pl.cdiv(rows, KEYS)
    smem = pl.BlockSpec(memory_space=pltpu.SMEM)
    vmem = pl.BlockSpec(memory_space=pltpu.VMEM)
    return pl.pallas_call(
        functools.partial(attend_kernel, fresh_base, side),
        out_shape=jax.ShapeDtypeStruct((4, rows // 2, width // 4), jnp.bfloat16),
        in_specs=[smem] * 5 + [vmem] * 6,
        out_specs=vmem,
        scratch_shapes=[
            pltpu.VMEM((kv_local, group_size * TILE, most * KEYS), jnp.float32),
            pltpu.VMEM((kv_local, group_size * TILE, 2 * HD), jnp.float32),
        ],
        compiler_params=pltpu.CompilerParams(vmem_limit_bytes=28 * MIB),
        cost_estimate=cost((16 - 15 * side) * 10**9),
        name="attend",
    )(control, *steps, queries, keys, values, key_conv, key_row, tok_conv)


def multiply(left, pieces, at):
    total = None
    for n, piece in enumerate(pieces):
        term = jnp.dot(left[n], piece[:, at], preferred_element_type=jnp.float32)
        total = term if total is None else total + term
    return total.astype(jnp.bfloat16)


def blocks(columns):
    cut = min(COLUMNS, columns)
    return [slice(k, min(k + cut, columns)) for k in range(0, columns, cut)]


def parts_of(control, refs):
    if len(refs) == 1:
        depth = refs[0].shape[0] // 4
        return [
            (0, [refs[0].at[pl.ds(pl.multiple_of(control[6 + n] * depth, depth), depth)] for n in range(4)])
        ]
    parts, first = [], 0
    for k in range(0, len(refs), 4):
        parts.append((first, refs[k : k + 4]))
        first += refs[k].shape[1]
    return parts


def project_kernel(control, left, *refs):
    for first, pieces in parts_of(control, refs[:-1]):
        for at in blocks(pieces[0].shape[1]):
            refs[-1][:, first + at.start : first + at.stop] = multiply(left, pieces, at)


def finish_kernel(has_out, control, left, came, *refs):
    for first, pieces in parts_of(control, refs[: len(refs) - 1 - has_out]):
        for at in blocks(pieces[0].shape[1]):
            to = slice(first + at.start, first + at.stop)
            total = multiply(left, pieces, at).astype(jnp.float32) + came[:, to].astype(jnp.float32)
            refs[-1][0, :, to] = total.astype(jnp.bfloat16)


def project(control, left, pieces, came=None, base=None, out=None, width=None):
    half = left.shape[1]
    columns = sum(piece.shape[1] for piece in pieces[::4])
    vmem = pl.BlockSpec(memory_space=pltpu.VMEM)
    in_specs = [vmem]
    operands = [left]
    aliases = {}
    if came is None:
        kernel = project_kernel
        out_shape = jax.ShapeDtypeStruct((half, columns), jnp.bfloat16)
        out_specs = vmem
    else:
        kernel = functools.partial(finish_kernel, int(out is not None))
        in_specs.append(vmem)
        operands.append(came)
        out_shape = jax.ShapeDtypeStruct((1, half, width), jnp.bfloat16)
        out_specs = pl.BlockSpec((1, half, columns), lambda j, control: (0, 0, control[base]))
    in_specs += [vmem] * len(pieces)
    operands += pieces
    if out is not None:
        in_specs.append(pl.BlockSpec(memory_space=pl.ANY))
        operands.append(out)
        aliases = {len(operands): 0}
    return pl.pallas_call(
        kernel,
        out_shape=out_shape,
        grid_spec=pltpu.PrefetchScalarGridSpec(
            num_scalar_prefetch=1, grid=(1,), in_specs=in_specs, out_specs=out_specs
        ),
        input_output_aliases=aliases,
        compiler_params=pltpu.CompilerParams(vmem_limit_bytes=16 * MIB),
        cost_estimate=cost(10**8 if base == 12 else 3 * 10**9),
        name="project" if came is None else "finish",
    )(control, *operands)


def pick_kernel(asked, pool, out, held, rows, sem):
    owners, bucket = asked.shape
    whole = pltpu.make_async_copy(pool, held, sem.at[owners])
    whole.start()
    whole.wait()
    for owner in range(owners):

        def copy(n, carry):
            rows[owner, n] = held[asked[owner, n]]
            return carry

        lax.fori_loop(0, bucket, copy, 0, unroll=8)
        pltpu.make_async_copy(rows.at[owner], out.at[owner], sem.at[owner]).start()
    for owner in range(owners):
        pltpu.make_async_copy(rows.at[owner], out.at[owner], sem.at[owner]).wait()


def pick(pool, asked):
    hbm = pl.BlockSpec(memory_space=pltpu.HBM)
    out = asked.shape + pool.shape[1:]
    return pl.pallas_call(
        pick_kernel,
        out_shape=jax.ShapeDtypeStruct(out, jnp.bfloat16),
        in_specs=[pl.BlockSpec(memory_space=pltpu.SMEM), hbm],
        out_specs=hbm,
        scratch_shapes=[
            pltpu.VMEM(pool.shape, jnp.bfloat16),
            pltpu.VMEM(out, jnp.bfloat16),
            pltpu.SemaphoreType.DMA((asked.shape[0] + 1,)),
        ],
        compiler_params=pltpu.CompilerParams(vmem_limit_bytes=56 * MIB),
        cost_estimate=cost(),
        name="pick",
    )(asked, pool)


SWAP = [(0, 1), (1, 0)]


def after(value, *others):
    return lax.optimization_barrier((value,) + others)[0]


def shards(
    queries, new_kv, pool, out_weight, tok_conv, page_conv, page_fill, page_owner, page_index
):
    row_count = queries.shape[1]
    slot_count = page_owner.shape[1]
    owner_count = lax.axis_size("seq")
    tp_count = lax.axis_size("tp")
    bucket = 2 * slot_count // owner_count
    group, role, tp = lax.axis_index("group"), lax.axis_index("role"), lax.axis_index("tp")
    seq = lax.axis_index("seq")


    own = 2 * group + role
    depth = out_weight.shape[0] // 4
    columns = out_weight.shape[1]
    quarter = lax.dynamic_slice_in_dim(out_weight, own * depth, depth, 0)
    order = [q ^ own for q in range(4)]
    order = [(v % 2) * 2 + v // 2 for v in order]
    flip = tp if tp_count == 2 else 0
    second = jnp.where(seq < 2, 2, 1)
    third = jnp.where(seq < 2, 3, 0)
    local = [own, own ^ 2, own ^ 1, own ^ 3]
    control = jnp.stack(
        [jnp.asarray(v, jnp.int32) for v in (flip, 1 - flip, *order, *local, seq, seq ^ 1, second, 2 * third, 2 * third + 1)]
    )
    swap_group = functools.partial(lax.ppermute, axis_name="group", perm=SWAP)
    swap_role = functools.partial(lax.ppermute, axis_name="role", perm=SWAP)

    if owner_count == 4:
        middle = (seq == 1) | (seq == 2)
        cut = columns // 2
        parts = [quarter[:, :cut], quarter[:, cut:]]
        pair = functools.partial(lax.ppermute, axis_name="seq", perm=[(0, 1), (1, 0), (2, 3), (3, 2)])
        cross = functools.partial(lax.ppermute, axis_name="seq", perm=[(1, 2), (2, 1)])
        forward = functools.partial(lax.ppermute, axis_name="seq", perm=[(1, 0), (2, 3)])
        near, inner = [pair(parts[0])], [cross(parts[0])]

    position, wanted = rank(page_owner, page_index, owner_count, bucket)
    asked = lax.all_to_all(wanted, "seq", split_axis=0, concat_axis=0, tiled=True)
    if owner_count == 4:
        near, inner = [after(near[0], asked)], [after(inner[0], asked)]
        later = after(parts[1], near[0], inner[0])
        near.append(pair(later))
        inner.append(cross(later))
        asked = after(asked, near[0], inner[0])
    found = pick(pool[0], asked)
    if owner_count == 4:
        near[1], inner[1] = after(near[1], found), after(inner[1], found)
        found = after(found, near[1], inner[1])
    pages = lax.all_to_all(found, "seq", split_axis=0, concat_axis=0, tiled=True)
    pages = pages.reshape((owner_count * bucket,) + found.shape[2:])
    slots = slot_count * pool.shape[3]
    fresh = new_kv[0].reshape(row_count, -1)
    tables = attend_tables(
        row_count, slot_count, pool.shape[3], tok_conv[0], page_conv[0], page_fill[0]
    )

    if owner_count != 4 or tp_count != 2:
        mine = lax.all_gather(quarter, "seq", axis=1, tiled=True)
        across = swap_group(mine)
        pieces = [mine, across, swap_role(mine), swap_role(across)]
        keys, values = place(position, pages, fresh)
        partial = [
            project(control, attend(side, control, tables, queries[0], keys, values, slots), pieces)
            for side in (0, 1)
        ]
        return lax.psum_scatter(
            jnp.concatenate(partial, axis=0), "tp", scatter_dimension=0, tiled=True
        )[None]

    swap_tp = functools.partial(lax.ppermute, axis_name="tp", perm=SWAP)

    def four(one, two, *hold):
        return [one, two, swap_role(after(one, *hold)), swap_role(after(two, *hold))]

    near_across = [swap_group(part) for part in near]
    next_shard = [jnp.where(middle, part, forward(part)) for part in inner]
    next_across = [swap_group(part) for part in next_shard]
    near_all = four(near[0], near_across[0]) + four(near[1], near_across[1])
    next_all = four(next_shard[0], next_across[0]) + four(next_shard[1], next_across[1])
    far = [cross(after(part, *next_across)) for part in near]

    keys, values = place(position, after(pages, *near_all, *next_all), fresh)
    left = attend(1, control, tables, queries[0], keys, values, slots)
    far_on = [forward(after(far[0], left))]
    sent = [project(control, left, [out_weight])]
    far_on.append(forward(after(far[1], sent[0])))
    sent.append(project(control, after(left, sent[-1]), near_all))
    far[0] = jnp.where(middle, far[0], after(far_on[0], sent[1]))
    far_across = [swap_group(far[0])]
    sent.append(project(control, after(left, sent[-1]), next_all))
    came = [swap_tp(each) for each in sent]
    stay = attend(0, control, tables, after(queries[0], sent[2], far[0]), keys, values, slots)
    far[1] = jnp.where(middle, far[1], after(far_on[1], stay))
    far_across.append(swap_group(far[1]))
    far_all = [four(far[0], far_across[0], stay)]
    total = columns * owner_count
    out = project(control, after(stay, *came[:2]), [out_weight], came[0], 10, None, total)
    out = project(control, stay, near_all, came[1], 11, out, total)
    sent.append(project(control, after(left, out), far_all[0]))
    came.append(swap_tp(sent[3]))
    out = project(control, after(stay, sent[3]), next_all, came[2], 12, out, total)
    far_all.append(four(far[1], far_across[1], out, came[3]))
    sent.append(project(control, after(left, out), far_all[1]))
    came.append(swap_tp(sent[4]))
    out = project(control, after(stay, sent[4]), far_all[0], came[3], 13, out, total)
    return project(control, stay, far_all[1], came[4], 14, out, total)


def solution(mesh):
    return jax.shard_map(
        shards,
        mesh=mesh,
        in_specs=(
            P("role", ("group", "seq"), "tp"),
            P("role", ("group", "seq"), None, "tp"),
            P("role", ("group", "seq"), None, None, "tp"),
            P("tp", "seq"),
            P("role", ("group", "seq")),
            P("role", ("group", "seq")),
            P("role", ("group", "seq")),
            P("role", ("group", "seq")),
            P("role", ("group", "seq")),
        ),
        out_specs=P("role", ("group", "seq", "tp"), None),
        check_vma=False,
    )
```

```python
import functools
import math

import jax
import jax.numpy as jnp
from jax import lax
from jax.experimental import pallas as pl
from jax.experimental.pallas import tpu as pltpu
from jax.sharding import PartitionSpec as P

HD = 128
TILE = 96
KEYS = 256
LANES = 128
HIDDEN = -1e30
COLUMNS = 256
MIB = 1024 * 1024


def cost(flops=3 * 10**9):
    return pl.CostEstimate(flops=flops, bytes_accessed=1000, transcendentals=0)


def rank_kernel(owner, page, position, wanted, count):
    owners, bucket = wanted.shape
    for n in range(owners):
        count[n] = 0

    def clear(k, carry):
        for n in range(owners):
            wanted[n, k] = 0
        return carry

    lax.fori_loop(0, bucket, clear, 0)

    def put(slot, carry):
        to = owner[0, slot]
        rank = count[to]
        count[to] = rank + 1
        wanted[to, rank] = page[0, slot]
        position[slot] = to * bucket + rank
        return carry

    lax.fori_loop(0, owner.shape[1], put, 0, unroll=4)


def rank(page_owner, page_index, owners, bucket):
    smem = pl.BlockSpec(memory_space=pltpu.SMEM)
    return pl.pallas_call(
        rank_kernel,
        out_shape=(
            jax.ShapeDtypeStruct((page_owner.shape[1],), jnp.int32),
            jax.ShapeDtypeStruct((owners, bucket), jnp.int32),
        ),
        in_specs=[smem, smem],
        out_specs=(smem, smem),
        scratch_shapes=[pltpu.SMEM((owners,), jnp.int32)],
        cost_estimate=cost(),
        name="rank",
    )(page_owner, page_index)


def place_kernel(position, pages, fresh, keys, values):
    kv_local, key_total = keys.shape[:2]
    slots, page_len, rows = position.shape[0], pages.shape[2], fresh.shape[0]
    channels = kv_local * HD
    hist = slots * page_len
    fresh_base = hist + KEYS
    for head in range(kv_local):
        values[head, :, HD:] = jnp.ones((key_total, HD), jnp.bfloat16)
        for first, last in ((hist, fresh_base), (fresh_base + rows, key_total)):
            keys[head, first:last] = jnp.zeros((last - first, HD), jnp.bfloat16)
            values[head, first:last, :HD] = jnp.zeros((last - first, HD), jnp.bfloat16)
        at = head * HD
        keys[head, fresh_base : fresh_base + rows] = fresh[:, at : at + HD]
        values[head, fresh_base : fresh_base + rows, :HD] = fresh[:, channels + at : channels + at + HD]

    def place(slot, carry):
        page = position[slot]
        row = pl.ds(pl.multiple_of(slot * page_len, page_len), page_len)
        for head in range(kv_local):
            at = head * HD
            keys[head, row] = pages[page, 0, :, at : at + HD]
            values[head, row, :HD] = pages[page, 1, :, at : at + HD]
        return carry

    lax.fori_loop(0, slots, place, 0, unroll=8)


def place(position, pages, fresh):
    kv_local = pages.shape[3] // HD
    rows = fresh.shape[0]
    key_total = position.shape[0] * pages.shape[2] + KEYS + pl.cdiv(rows, KEYS) * KEYS + KEYS
    vmem = pl.BlockSpec(memory_space=pltpu.VMEM)
    return pl.pallas_call(
        place_kernel,
        out_shape=(
            jax.ShapeDtypeStruct((kv_local, key_total, HD), jnp.bfloat16),
            jax.ShapeDtypeStruct((kv_local, key_total, 2 * HD), jnp.bfloat16),
        ),
        in_specs=[pl.BlockSpec(memory_space=pltpu.SMEM), vmem, vmem],
        out_specs=(vmem, vmem),
        compiler_params=pltpu.CompilerParams(vmem_limit_bytes=20 * MIB),
        cost_estimate=cost(10**9),
        name="place",
    )(position, pages, fresh)


def attend_kernel(
    fresh_base, side, control, hist_at, hist_steps, fresh_at, fresh_steps,
    query, keys, values, key_conv, key_row, tok_conv, out, scores, sums,
):
    kv_local = keys.shape[0]
    group_size = query.shape[1] // (kv_local * HD)
    half, depth = out.shape[1], out.shape[2]
    tiles = half // TILE
    to_exp2 = math.log2(math.e) / math.sqrt(HD)
    wide = group_size * TILE

    def tile(number_here, carry):
        index = control[side] * tiles + number_here
        first = pl.multiple_of(index * TILE, TILE)
        leaving = pl.ds(pl.multiple_of(number_here * TILE, TILE), TILE)
        tokens = pl.ds(first, TILE)
        conv = tok_conv[tokens]
        number = first + lax.broadcasted_iota(jnp.int32, (TILE, 1), 0)
        steps_h, steps_f = hist_steps[index], fresh_steps[index]
        at_h, at_f = hist_at[index], fresh_at[index]
        heads = [
            jnp.concatenate(
                [
                    query[tokens, (head * group_size + g) * HD : (head * group_size + g + 1) * HD]
                    for g in range(group_size)
                ],
                axis=0,
            )
            for head in range(kv_local)
        ]

        def key_range(step):
            start = jnp.where(
                step < steps_h, at_h + step * KEYS, fresh_base + at_f + (step - steps_h) * KEYS
            )
            return pl.ds(pl.multiple_of(start, LANES), KEYS)

        def score(step, tops):
            where = key_range(step)
            ok = (key_conv[:, where] == conv) & (key_row[:, where] <= number)
            held = pl.ds(pl.multiple_of(step * KEYS, KEYS), KEYS)
            new = []
            for head in range(kv_local):
                s = lax.dot_general(
                    heads[head], keys[head, where], (((1,), (1,)), ((), ())),
                    preferred_element_type=jnp.float32,
                ).reshape(group_size, TILE, KEYS)
                s = jnp.where(ok[None], s, HIDDEN).reshape(wide, KEYS)
                scores[head, :, held] = s
                top = tops[head]
                for k in range(0, KEYS, LANES):
                    top = jnp.maximum(top, s[:, k : k + LANES])
                new.append(top)
            return tuple(new)

        low = jnp.full((wide, LANES), HIDDEN, jnp.float32)
        tops = lax.fori_loop(0, steps_h + steps_f, score, (low,) * kv_local)
        tops = [jnp.max(top, axis=1, keepdims=True) * to_exp2 for top in tops]
        sums[...] = jnp.zeros_like(sums)

        def gather(step, carry):
            where = key_range(step)
            held = pl.ds(pl.multiple_of(step * KEYS, KEYS), KEYS)
            for head in range(kv_local):
                w = jnp.exp2(scores[head, :, held] * to_exp2 - tops[head]).astype(jnp.bfloat16)
                sums[head] += jnp.dot(w, values[head, where], preferred_element_type=jnp.float32)
            return carry

        lax.fori_loop(0, steps_h + steps_f, gather, 0)
        for head in range(kv_local):
            done = (sums[head, :, :HD] / sums[head, :, HD:]).astype(jnp.bfloat16)
            for g in range(group_size):
                at = (head * group_size + g) * HD
                out[control[2 + at // depth], leaving, at % depth : at % depth + HD] = done[
                    g * TILE : (g + 1) * TILE
                ]
        return carry

    lax.fori_loop(0, tiles, tile, 0)


def attend_tables(rows, slots, page_len, tok_conv, page_conv, page_fill):
    hist = slots * page_len
    fresh_base = hist + KEYS
    key_total = fresh_base + pl.cdiv(rows, KEYS) * KEYS + KEYS
    live = jnp.arange(page_len)[None, :] < page_fill[:, None]
    hist_conv = jnp.where(live, page_conv[:, None], -1).reshape(hist)
    tail = key_total - fresh_base - rows
    key_conv = jnp.concatenate(
        [hist_conv, jnp.full((KEYS,), -1, jnp.int32), tok_conv, jnp.full((tail,), -1, jnp.int32)]
    )[None]
    key_row = jnp.maximum(jnp.arange(key_total, dtype=jnp.int32) - fresh_base, -1)[None]
    lowest, highest = tok_conv[::TILE], tok_conv[TILE - 1 :: TILE]
    hist_at = jnp.sum(page_conv[None] < lowest[:, None], axis=1, dtype=jnp.int32) * page_len
    hist_at = hist_at // LANES * LANES
    hist_end = jnp.sum(page_conv[None] <= highest[:, None], axis=1, dtype=jnp.int32) * page_len
    hist_steps = (hist_end - hist_at + KEYS - 1) // KEYS
    fresh_at = jnp.sum(tok_conv[None] < lowest[:, None], axis=1, dtype=jnp.int32) // LANES * LANES
    fresh_end = (jnp.arange(rows // TILE, dtype=jnp.int32) + 1) * TILE
    fresh_steps = (fresh_end - fresh_at + KEYS - 1) // KEYS
    return key_conv, key_row, tok_conv[:, None], hist_at, hist_steps, fresh_at, fresh_steps


def attend(side, control, tables, queries, keys, values, slots):
    rows, width = queries.shape
    kv_local, key_total = keys.shape[:2]
    group_size = width // (kv_local * HD)
    key_conv, key_row, tok_conv, *steps = tables
    fresh_base = slots + KEYS
    most = slots // KEYS + pl.cdiv(rows, KEYS)
    smem = pl.BlockSpec(memory_space=pltpu.SMEM)
    vmem = pl.BlockSpec(memory_space=pltpu.VMEM)
    return pl.pallas_call(
        functools.partial(attend_kernel, fresh_base, side),
        out_shape=jax.ShapeDtypeStruct((4, rows // 2, width // 4), jnp.bfloat16),
        in_specs=[smem] * 5 + [vmem] * 6,
        out_specs=vmem,
        scratch_shapes=[
            pltpu.VMEM((kv_local, group_size * TILE, most * KEYS), jnp.float32),
            pltpu.VMEM((kv_local, group_size * TILE, 2 * HD), jnp.float32),
        ],
        compiler_params=pltpu.CompilerParams(vmem_limit_bytes=28 * MIB),
        cost_estimate=cost((16 - 15 * side) * 10**9),
        name="attend",
    )(control, *steps, queries, keys, values, key_conv, key_row, tok_conv)


def multiply(left, pieces, at):
    total = None
    for n, piece in enumerate(pieces):
        term = jnp.dot(left[n], piece[:, at], preferred_element_type=jnp.float32)
        total = term if total is None else total + term
    return total.astype(jnp.bfloat16)


def blocks(columns):
    cut = min(COLUMNS, columns)
    return [slice(k, min(k + cut, columns)) for k in range(0, columns, cut)]


def parts_of(control, refs):
    if len(refs) == 1:
        depth = refs[0].shape[0] // 4
        return [
            (0, [refs[0].at[pl.ds(pl.multiple_of(control[6 + n] * depth, depth), depth)] for n in range(4)])
        ]
    parts, first = [], 0
    for k in range(0, len(refs), 4):
        parts.append((first, refs[k : k + 4]))
        first += refs[k].shape[1]
    return parts


def project_kernel(control, left, *refs):
    for first, pieces in parts_of(control, refs[:-1]):
        for at in blocks(pieces[0].shape[1]):
            refs[-1][:, first + at.start : first + at.stop] = multiply(left, pieces, at)


def finish_kernel(has_out, control, left, came, *refs):
    for first, pieces in parts_of(control, refs[: len(refs) - 1 - has_out]):
        for at in blocks(pieces[0].shape[1]):
            to = slice(first + at.start, first + at.stop)
            total = multiply(left, pieces, at).astype(jnp.float32) + came[:, to].astype(jnp.float32)
            refs[-1][0, :, to] = total.astype(jnp.bfloat16)


def project(control, left, pieces, came=None, base=None, out=None, width=None):
    half = left.shape[1]
    columns = sum(piece.shape[1] for piece in pieces[::4])
    vmem = pl.BlockSpec(memory_space=pltpu.VMEM)
    in_specs = [vmem]
    operands = [left]
    aliases = {}
    if came is None:
        kernel = project_kernel
        out_shape = jax.ShapeDtypeStruct((half, columns), jnp.bfloat16)
        out_specs = vmem
    else:
        kernel = functools.partial(finish_kernel, int(out is not None))
        in_specs.append(vmem)
        operands.append(came)
        out_shape = jax.ShapeDtypeStruct((1, half, width), jnp.bfloat16)
        out_specs = pl.BlockSpec((1, half, columns), lambda j, control: (0, 0, control[base]))
    in_specs += [vmem] * len(pieces)
    operands += pieces
    if out is not None:
        in_specs.append(pl.BlockSpec(memory_space=pl.ANY))
        operands.append(out)
        aliases = {len(operands): 0}
    return pl.pallas_call(
        kernel,
        out_shape=out_shape,
        grid_spec=pltpu.PrefetchScalarGridSpec(
            num_scalar_prefetch=1, grid=(1,), in_specs=in_specs, out_specs=out_specs
        ),
        input_output_aliases=aliases,
        compiler_params=pltpu.CompilerParams(vmem_limit_bytes=16 * MIB),
        cost_estimate=cost(),
        name="project" if came is None else "finish",
    )(control, *operands)


def pick_kernel(asked, pool, out, held, rows, sem):
    owners, bucket = asked.shape
    whole = pltpu.make_async_copy(pool, held, sem.at[owners])
    whole.start()
    whole.wait()
    for owner in range(owners):

        def copy(n, carry):
            rows[owner, n] = held[asked[owner, n]]
            return carry

        lax.fori_loop(0, bucket, copy, 0, unroll=8)
        pltpu.make_async_copy(rows.at[owner], out.at[owner], sem.at[owner]).start()
    for owner in range(owners):
        pltpu.make_async_copy(rows.at[owner], out.at[owner], sem.at[owner]).wait()


def pick(pool, asked):
    hbm = pl.BlockSpec(memory_space=pltpu.HBM)
    out = asked.shape + pool.shape[1:]
    return pl.pallas_call(
        pick_kernel,
        out_shape=jax.ShapeDtypeStruct(out, jnp.bfloat16),
        in_specs=[pl.BlockSpec(memory_space=pltpu.SMEM), hbm],
        out_specs=hbm,
        scratch_shapes=[
            pltpu.VMEM(pool.shape, jnp.bfloat16),
            pltpu.VMEM(out, jnp.bfloat16),
            pltpu.SemaphoreType.DMA((asked.shape[0] + 1,)),
        ],
        compiler_params=pltpu.CompilerParams(vmem_limit_bytes=56 * MIB),
        cost_estimate=cost(),
        name="pick",
    )(asked, pool)


SWAP = [(0, 1), (1, 0)]


def after(value, *others):
    return lax.optimization_barrier((value,) + others)[0]


def shards(
    queries, new_kv, pool, out_weight, tok_conv, page_conv, page_fill, page_owner, page_index
):
    row_count = queries.shape[1]
    slot_count = page_owner.shape[1]
    owner_count = lax.axis_size("seq")
    tp_count = lax.axis_size("tp")
    bucket = 2 * slot_count // owner_count
    group, role, tp = lax.axis_index("group"), lax.axis_index("role"), lax.axis_index("tp")
    seq = lax.axis_index("seq")


    own = 2 * group + role
    depth = out_weight.shape[0] // 4
    columns = out_weight.shape[1]
    quarter = lax.dynamic_slice_in_dim(out_weight, own * depth, depth, 0)
    order = [q ^ own for q in range(4)]
    order = [(v % 2) * 2 + v // 2 for v in order]
    flip = tp if tp_count == 2 else 0
    second = jnp.where(seq < 2, 2, 1)
    third = jnp.where(seq < 2, 3, 0)
    local = [own, own ^ 2, own ^ 1, own ^ 3]
    control = jnp.stack(
        [jnp.asarray(v, jnp.int32) for v in (flip, 1 - flip, *order, *local, seq, seq ^ 1, second, 2 * third, 2 * third + 1)]
    )
    swap_group = functools.partial(lax.ppermute, axis_name="group", perm=SWAP)
    swap_role = functools.partial(lax.ppermute, axis_name="role", perm=SWAP)

    if owner_count == 4:
        middle = (seq == 1) | (seq == 2)
        cut = columns // 2
        parts = [quarter[:, :cut], quarter[:, cut:]]
        pair = functools.partial(lax.ppermute, axis_name="seq", perm=[(0, 1), (1, 0), (2, 3), (3, 2)])
        cross = functools.partial(lax.ppermute, axis_name="seq", perm=[(1, 2), (2, 1)])
        forward = functools.partial(lax.ppermute, axis_name="seq", perm=[(1, 0), (2, 3)])
        near, inner = [pair(parts[0])], [cross(parts[0])]

    position, wanted = rank(page_owner, page_index, owner_count, bucket)
    asked = lax.all_to_all(wanted, "seq", split_axis=0, concat_axis=0, tiled=True)
    if owner_count == 4:
        near, inner = [after(near[0], asked)], [after(inner[0], asked)]
        later = after(parts[1], near[0], inner[0])
        near.append(pair(later))
        inner.append(cross(later))
        asked = after(asked, near[0], inner[0])
    found = pick(pool[0], asked)
    if owner_count == 4:
        near[1], inner[1] = after(near[1], found), after(inner[1], found)
        found = after(found, near[1], inner[1])
    pages = lax.all_to_all(found, "seq", split_axis=0, concat_axis=0, tiled=True)
    pages = pages.reshape((owner_count * bucket,) + found.shape[2:])
    slots = slot_count * pool.shape[3]
    fresh = new_kv[0].reshape(row_count, -1)
    tables = attend_tables(
        row_count, slot_count, pool.shape[3], tok_conv[0], page_conv[0], page_fill[0]
    )

    if owner_count != 4 or tp_count != 2:
        mine = lax.all_gather(quarter, "seq", axis=1, tiled=True)
        across = swap_group(mine)
        pieces = [mine, across, swap_role(mine), swap_role(across)]
        keys, values = place(position, pages, fresh)
        partial = [
            project(control, attend(side, control, tables, queries[0], keys, values, slots), pieces)
            for side in (0, 1)
        ]
        return lax.psum_scatter(
            jnp.concatenate(partial, axis=0), "tp", scatter_dimension=0, tiled=True
        )[None]

    swap_tp = functools.partial(lax.ppermute, axis_name="tp", perm=SWAP)

    def four(one, two, *hold):
        return [one, two, swap_role(after(one, *hold)), swap_role(after(two, *hold))]

    near_across = [swap_group(part) for part in near]
    next_shard = [jnp.where(middle, part, forward(part)) for part in inner]
    next_across = [swap_group(part) for part in next_shard]
    near_all = four(near[0], near_across[0]) + four(near[1], near_across[1])
    next_all = four(next_shard[0], next_across[0]) + four(next_shard[1], next_across[1])
    far = [cross(after(part, *next_across)) for part in near]

    keys, values = place(position, after(pages, *near_all, *next_all), fresh)
    left = attend(1, control, tables, queries[0], keys, values, slots)
    far_on = [forward(after(far[0], left))]
    sent = [project(control, left, [out_weight])]
    far_on.append(forward(after(far[1], sent[0])))
    sent.append(project(control, after(left, sent[-1]), near_all))
    far[0] = jnp.where(middle, far[0], after(far_on[0], sent[1]))
    far_across = [swap_group(far[0])]
    sent.append(project(control, after(left, sent[-1]), next_all))
    came = [swap_tp(each) for each in sent]
    stay = attend(0, control, tables, after(queries[0], sent[2], far[0]), keys, values, slots)
    far[1] = jnp.where(middle, far[1], after(far_on[1], stay))
    far_across.append(swap_group(far[1]))
    far_all = [four(far[0], far_across[0], stay)]
    total = columns * owner_count
    out = project(control, after(stay, *came[:2]), [out_weight], came[0], 10, None, total)
    out = project(control, stay, near_all, came[1], 11, out, total)
    out = project(control, stay, next_all, came[2], 12, out, total)
    sent.append(project(control, after(left, out), far_all[0]))
    came.append(swap_tp(sent[3]))
    far_all.append(four(far[1], far_across[1], sent[3]))
    sent.append(project(control, left, far_all[1]))
    came.append(swap_tp(sent[4]))
    out = project(control, after(stay, sent[4]), far_all[0], came[3], 13, out, total)
    return project(control, stay, far_all[1], came[4], 14, out, total)


def solution(mesh):
    return jax.shard_map(
        shards,
        mesh=mesh,
        in_specs=(
            P("role", ("group", "seq"), "tp"),
            P("role", ("group", "seq"), None, "tp"),
            P("role", ("group", "seq"), None, None, "tp"),
            P("tp", "seq"),
            P("role", ("group", "seq")),
            P("role", ("group", "seq")),
            P("role", ("group", "seq")),
            P("role", ("group", "seq")),
            P("role", ("group", "seq")),
        ),
        out_specs=P("role", ("group", "seq", "tp"), None),
        check_vma=False,
    )
```
